32 devices in a mesh: dp: 16 (over z, x, core), mp: 2 (over y).
Axes of the slice: x: 2, y: 2, z: 4, core: 2. Of those that a mesh axis runs over, the one named last changes fastest.
Arguments:
- layer_input: bfloat16 [32, 512, 768], P('dp', 'mp'), may hold values from -6 to 6
- cotangent: bfloat16 [32, 512, 768], P('dp', 'mp'), may hold values from -6 to 6
- lengths: int32 [32, 2], P('dp'), may hold values from 1 to 256, as said below
- bucket: int32 [32], P('dp'), may hold values from 0 to 1
- w_qkv: bfloat16 [2, 3, 768, 768], P(None, None, 'dp', 'mp'), may hold values from -0.21875 to 0.21875
- bias_qv: bfloat16 [2, 2, 768], P(None, None, 'mp'), may hold values from -1.5 to 1.5
- w_out: bfloat16 [2, 768, 768], P(None, 'mp', 'dp'), may hold values from -1.75 to 1.75
- bias_out: bfloat16 [2, 2, 768], replicated, may hold values from -1.5 to 1.5
- ln_gain: bfloat16 [2, 2, 768], replicated, may hold values from 0.099609375 to 1.8984375
- ln_bias: bfloat16 [2, 2, 768], replicated, may hold values from -1.5 to 1.5
- w_up: bfloat16 [2, 768, 3072], P(None, 'dp', 'mp'), may hold values from -0.21875 to 0.21875
- bias_up: bfloat16 [2, 3072], P(None, 'mp'), may hold values from -1.5 to 1.5
- w_down: bfloat16 [2, 3072, 768], P(None, 'mp', 'dp'), may hold values from -0.109375 to 0.109375
Outputs:
- output: bfloat16 [32, 512, 768], P('dp', 'mp')
- input_grad: bfloat16 [32, 512, 768], P('dp', 'mp')
- grad_w_qkv: float32 [2, 3, 768, 768], P(None, None, 'dp', 'mp')
- grad_bias_qv: float32 [2, 2, 768], P(None, None, 'mp')
- grad_w_out: float32 [2, 768, 768], P(None, 'mp', 'dp')
- grad_bias_out: float32 [2, 2, 768], replicated
- grad_ln_gain: float32 [2, 2, 768], replicated
- grad_ln_bias: float32 [2, 2, 768], replicated
- grad_w_up: float32 [2, 768, 3072], P(None, 'dp', 'mp')
- grad_bias_up: float32 [2, 3072], P(None, 'mp')
- grad_w_down: float32 [2, 3072, 768], P(None, 'mp', 'dp')
The draws below stay inside these ranges and needn't reach their ends.
Inputs may be any that keep to these rules, and one draw needn't show every extreme that they name: `lengths`: each entry is at most 256; in every draw some entry equals 256 and some equals 1. `bucket`: 1 marks a slot holding one item, 0 a slot holding two items.
All inputs are finite; a program needn't handle non-finite values.
Results may differ from the reference program's by a relative error of at most 0.025.
Values may be sent and summed in bfloat16 or wider, within the bound.
A program may use at most 256 MiB of HBM per device.

```python
import math
import jax
import jax.numpy as jnp
from jax import lax

D = 768
FF = 3072
HEAD_DIM = 64
SEQ = 512
LAYERS = 2
SLOTS = 32


def draw_lengths(key, part):
    key = jax.random.fold_in(key, 7)
    key_values, key_order = jax.random.split(key)
    values = jax.random.randint(key_values, (SLOTS * 2,), 1, SEQ // 2 + 1, dtype=jnp.int32)
    order = jax.random.permutation(key_order, SLOTS * 2)
    values = values.at[order[0]].set(SEQ // 2).at[order[1]].set(1)
    return values.reshape(SLOTS, 2).astype(jnp.int32)


def touch_ends(entries, key, least, largest):
    longest = entries.shape.index(max(entries.shape))
    spots = []
    for shift in (0, 1):
        where = [jax.random.randint(jax.random.fold_in(key, axis), (), 0, length) for axis, length in enumerate(entries.shape)]
        where[longest] = (where[longest] + shift) % entries.shape[longest]
        spots.append(tuple(where))
    return entries.at[spots[0]].set(least).at[spots[1]].set(largest)


def level_of(stream_key, dims, pieces, smallest, top_value):
    loudness = 1.0
    for dim, blocks in pieces:
        steps = jax.random.uniform(jax.random.fold_in(jax.random.fold_in(stream_key, 6), dim), (blocks,), jnp.float32, smallest / len(pieces), top_value / len(pieces))
        loudness = loudness * jnp.repeat(jnp.exp(steps), dims[dim] // blocks).reshape((-1,) + (1,) * (len(dims) - 1 - dim))
    return loudness


def centred(own_key, dims, width, most, cuts=(), kind=jnp.bfloat16):
    values = jax.random.normal(own_key, dims, jnp.float32) * width
    if len(cuts) > 0:
        values = level_of(own_key, dims, cuts, -0.22, 0.18) * values
    return jnp.clip(values, min=-most, max=most).astype(kind)


def setup_inputs(seed: int = 0) -> dict:
    seeds = jax.random.split(jax.random.key(seed), 14)
    layer_input = centred(seeds[0], (SLOTS, SEQ, D), 1.0, 6.0, ((0, 16), (1, 2)))
    cotangent = centred(seeds[1], (SLOTS, SEQ, D), 1.0, 6.0, ((0, 16), (1, 2)))
    lengths = draw_lengths(jax.random.fold_in(seeds[13], 71), 0)
    bucket = touch_ends(jax.random.randint(seeds[3], (SLOTS,), 0, 2), jax.random.fold_in(seeds[3], 1), 0, 1).astype(jnp.int32)
    w_qkv = centred(seeds[4], (LAYERS, 3, D, D), D ** -0.5, 0.21875, ((2, 16), (3, 2)))
    bias_qv = centred(seeds[5], (LAYERS, 2, D), 0.3, 1.5, ((2, 2),))
    w_out = centred(seeds[6], (LAYERS, D, D), (D // 64) ** -0.5, 1.75, ((1, 2), (2, 16)))
    bias_out = centred(seeds[7], (LAYERS, 2, D), 0.3, 1.5)
    ln_gain = jnp.clip(1.0 + 0.18 * jax.random.normal(seeds[8], (LAYERS, 2, D), jnp.float32), 0.099609375, 1.8984375).astype(jnp.bfloat16)
    ln_bias = centred(seeds[9], (LAYERS, 2, D), 0.3, 1.5)
    w_up = centred(seeds[10], (LAYERS, D, FF), D ** -0.5, 0.21875, ((1, 16), (2, 2)))
    bias_up = centred(seeds[11], (LAYERS, FF), 0.3, 1.5, ((1, 2),))
    w_down = centred(seeds[12], (LAYERS, FF, D), FF ** -0.5, 0.109375, ((1, 2), (2, 16)))
    return {"layer_input": layer_input, "cotangent": cotangent, "lengths": lengths, "bucket": bucket, "w_qkv": w_qkv, "bias_qv": bias_qv, "w_out": w_out, "bias_out": bias_out, "ln_gain": ln_gain, "ln_bias": ln_bias, "w_up": w_up, "bias_up": bias_up, "w_down": w_down}


@jax.custom_vjp
def low(v):
    return lax.optimization_barrier(v.astype(jnp.bfloat16)).astype(jnp.float32)

@jax.custom_vjp
def low_back(v):
    return v

def low_keep(v):
    return (low(v), None)

def low_pass(kept, grad):
    return (grad,)

def back_keep(v):
    return (v, None)

def back_low(kept, grad):
    return (low(grad),)
low.defvjp(low_keep, low_pass)
low_back.defvjp(back_keep, back_low)
highest = lax.Precision.HIGHEST
epsilon = 1e-12
masked_score = -1000000000.0

def build_mask(lengths, bucket, full_length):
    position = jnp.arange(full_length, dtype=jnp.int32)
    half_len = full_length // 2
    first_len = lengths[:, 0][:, None]
    second_len = lengths[:, 1][:, None]
    packed = (bucket == 0)[:, None]
    upper_half = (position >= half_len)[None, :]
    start_key = jnp.where(packed & upper_half, half_len, 0)
    end_key = jnp.where(packed, jnp.where(upper_half, half_len + second_len, first_len), first_len + second_len)
    key_pos = position[None, None, :]
    return (key_pos >= start_key[:, :, None]) & (key_pos < end_key[:, :, None])

def normalize(values, gain_vec, shift_vec):
    center = values - lax.optimization_barrier(jnp.mean(values, axis=-1, keepdims=True))
    variance = lax.optimization_barrier(jnp.mean(center * center, axis=-1, keepdims=True))
    return center * lax.rsqrt(variance + epsilon) * gain_vec + shift_vec

def one_layer(state_in, params, layer_index, key_valid):
    w_qkv, bias_qv, w_out, bias_out, ln_gain, ln_bias, w_up, bias_up, w_down = params
    batch_size = state_in.shape[0]
    head_count = D // HEAD_DIM
    projected = low_back(jnp.einsum('bsd,tdc->bstc', low(state_in), w_qkv[layer_index], precision=highest))
    queries = low(projected[:, :, 0] + bias_qv[layer_index, 0]).reshape(batch_size, SEQ, head_count, HEAD_DIM)
    keys_low = low(projected[:, :, 1]).reshape(batch_size, SEQ, head_count, HEAD_DIM)
    values_low = low(projected[:, :, 2] + bias_qv[layer_index, 1]).reshape(batch_size, SEQ, head_count, HEAD_DIM)
    scores = jnp.einsum('bqhe,bkhe->bhqk', queries, keys_low, precision=highest) * 0.125
    scores = low_back(jnp.where(key_valid[:, None], scores, masked_score))
    attn_probs = jax.nn.softmax(scores, axis=-1)
    context = jnp.einsum('bhqk,bkhe->bqhe', low(attn_probs), values_low, precision=highest)
    context = low(low_back(context)).reshape(batch_size, SEQ, D)
    attn_out = low_back(jnp.einsum('bsc,cd->bsd', context, w_out[layer_index], precision=highest)) + bias_out[layer_index, 0]
    hidden = normalize(state_in + attn_out, ln_gain[layer_index, 0], ln_bias[layer_index, 0])
    pre_active = low_back(jnp.einsum('bsd,df->bsf', low(hidden), w_up[layer_index], precision=highest)) + bias_up[layer_index]
    active = low(jax.nn.gelu(pre_active, approximate=False))
    ffn_out = low_back(jnp.einsum('bsf,fd->bsd', active, w_down[layer_index], precision=highest)) + bias_out[layer_index, 1]
    return normalize(hidden + ffn_out, ln_gain[layer_index, 1], ln_bias[layer_index, 1])

def reference(layer_input, cotangent, lengths, bucket, w_qkv, bias_qv, w_out, bias_out, ln_gain, ln_bias, w_up, bias_up, w_down):
    params = tuple((weight_arg.astype(jnp.float32) for weight_arg in (w_qkv, bias_qv, w_out, bias_out, ln_gain, ln_bias, w_up, bias_up, w_down)))
    group_size = math.gcd(8, SLOTS)
    group_count = SLOTS // group_size

    def forward(state_all, weights):

        def per_group(inputs):
            states, group_lengths, group_bucket = inputs
            key_valid = build_mask(group_lengths, group_bucket, SEQ)
            for layer_index in range(LAYERS):
                states = one_layer(states, weights, layer_index, key_valid)
            return states
        grouped = (state_all.reshape(group_count, group_size, SEQ, D), lengths.reshape(group_count, group_size, 2), bucket.reshape(group_count, group_size))
        return lax.map(jax.checkpoint(per_group), grouped).reshape(SLOTS, SEQ, D)
    result, pullback = jax.vjp(forward, layer_input.astype(jnp.float32), params)
    grad_input, grad_params = pullback(cotangent.astype(jnp.float32))
    return (result.astype(jnp.bfloat16), grad_input.astype(jnp.bfloat16), grad_params[0], grad_params[1], grad_params[2], grad_params[3], grad_params[4], grad_params[5], grad_params[6], grad_params[7], grad_params[8])
```

```python
import functools
import jax
import jax.numpy as jnp
from jax import lax
from jax.experimental import pallas as pl
from jax.experimental.pallas import tpu as pltpu
from jax.sharding import PartitionSpec as P

HEAD_DIM = 64
GROUPS = 16
MESH = pl.DeviceIdType.MESH


class Place:
    def __init__(self, fold):
        d = lax.axis_index("dp")
        self.fold = fold
        self.member = lax.rem(d, fold) if fold > 1 else 0
        g = d // fold if fold > 1 else d
        self.z = g // 4
        self.xc = lax.rem(g, 4)
        self.x = self.xc // 2
        self.c = lax.rem(self.xc, 2)
        self.y = lax.axis_index("mp")
    def dev(self, z, xc, y):
        return {"dp": (z * 4 + xc) * self.fold + self.member, "mp": y}

def gather_kernel(fold, nk, packed, w, lsem, zs, zr, xs, xr, ys, yr, fs, fr, cs, cr):
    p = Place(fold)
    z, xc, y = p.z, p.xc, p.y
    xo = (1 - p.x) * 2 + p.c
    co = p.x * 2 + (1 - p.c)
    yo = 1 - y
    barrier = pltpu.get_barrier_semaphore()
    peers = [p.dev(lax.rem(z + dz, 4), xc, y) for dz in (1, 2, 3)] + [p.dev(z, xo, y), p.dev(z, xc, yo), p.dev(z, co, y)]
    for d in peers:
        pl.semaphore_signal(barrier, inc=1, device_id=d, device_id_type=MESH)
    pl.semaphore_wait(barrier, 6)
    zj = [lax.rem(z + 4 - j, 4) for j in range(4)]
    def rc(src, dst, s, r, dev):
        return pltpu.make_async_remote_copy(src_ref=src, dst_ref=dst, send_sem=s, recv_sem=r, device_id=dev, device_id_type=MESH)
    sends = []
    def go(c):
        c.start(); sends.append(c)
    def own(k): return pltpu.make_async_copy(packed.at[k], w.at[k, y, z, xc], lsem.at[k])
    def zcopy(k, j): return rc(packed.at[k], w.at[k, y, z, xc], zs.at[k, j - 1], zr.at[k, j - 1], p.dev(lax.rem(z + j, 4), xc, y))
    def src(k, j): return packed.at[k] if j == 0 else w.at[k, y, zj[j], xc]
    def xcopy(k, j): return rc(src(k, j), w.at[k, y, zj[j], xc], xs.at[k, j], xr.at[k, j], p.dev(z, xo, y))
    def ycopy(k, j): return rc(src(k, j), w.at[k, y, zj[j], xc], ys.at[k, j], yr.at[k, j], p.dev(z, xc, yo))
    def fcopy(k, j):
        if j % 2 == 0:
            b = w.at[k, y, zj[j], xo]
            return rc(b, b, fs.at[k, j], fr.at[k, j], p.dev(z, xc, yo))
        b = w.at[k, yo, zj[j], xc]
        return rc(b, b, fs.at[k, j], fr.at[k, j], p.dev(z, xo, y))
    cols = [(y, xc), (y, xo), (yo, xc), (yo, xo)]
    def ccopy(k, i):
        cy, cx = cols[i]
        b = w.at[k, cy, :, cx]
        return rc(b, b, cs.at[k, i], cr.at[k, i], p.dev(z, co, y))
    def a(k):
        own(k).start()
        for j in (1, 2, 3): go(zcopy(k, j))
        go(xcopy(k, 0)); go(ycopy(k, 0))
    def b(k):
        for j in (1, 2, 3):
            zcopy(k, j).wait_recv()
            go(xcopy(k, j)); go(ycopy(k, j))
        own(k).wait()
        go(ccopy(k, 0))
    def c(k):
        for j in range(4):
            xcopy(k, j).wait_recv()
            if j % 2 == 0: go(fcopy(k, j))
            ycopy(k, j).wait_recv()
            if j % 2 == 1: go(fcopy(k, j))
        go(ccopy(k, 1)); go(ccopy(k, 2))
    def d(k):
        for j in range(4): fcopy(k, j).wait_recv()
        go(ccopy(k, 3))
    def e(k):
        for i in range(4): ccopy(k, i).wait_recv()
    a(0); a(1); b(0)
    for k in range(nk + 2):
        if k + 2 < nk: a(k + 2)
        if k + 1 < nk: b(k + 1)
        if k < nk: c(k)
        if 0 <= k - 1 < nk: d(k - 1)
        if 0 <= k - 2 < nk: e(k - 2)
    for s in sends: s.wait_send()

def gather(packed, fold=1, collective_id=1):
    nk, rows, cols = packed.shape
    D = pltpu.SemaphoreType.DMA
    return pl.pallas_call(
        functools.partial(gather_kernel, fold, nk),
        out_shape=jax.ShapeDtypeStruct((nk, 2, 4, 4, rows, cols), jnp.bfloat16),
        in_specs=[pl.BlockSpec(memory_space=pl.ANY)],
        out_specs=pl.BlockSpec(memory_space=pl.ANY),
        scratch_shapes=[D((nk,)), D((nk, 3)), D((nk, 3)), D((nk, 4)), D((nk, 4)), D((nk, 4)), D((nk, 4)), D((nk, 4)), D((nk, 4)), D((nk, 4)), D((nk, 4))],
        compiler_params=pltpu.CompilerParams(collective_id=collective_id, has_side_effects=True),
    )(packed)

def scatter_kernel(fold, nk, grads, out, own, rcb, rx, ry, rx2, ry2, rz, lsem, cs, cr, xs, xr, ys, yr, zs, zr):
    p = Place(fold)
    z, xc, y, x, c0 = p.z, p.xc, p.y, p.x, p.c
    xo = (1 - p.x) * 2 + p.c
    co = p.x * 2 + (1 - p.c)
    yo = 1 - y
    barrier = pltpu.get_barrier_semaphore()
    peers = [p.dev(lax.rem(z + dz, 4), xc, y) for dz in (1, 2, 3)] + [p.dev(z, xo, y), p.dev(z, xc, yo), p.dev(z, co, y)]
    for d in peers:
        pl.semaphore_signal(barrier, inc=1, device_id=d, device_id_type=MESH)
    pl.semaphore_wait(barrier, 6)
    def rc(src, dst, s, r, dev):
        return pltpu.make_async_remote_copy(src_ref=src, dst_ref=dst, send_sem=s, recv_sem=r, device_id=dev, device_id_type=MESH)
    sends = []
    def go(c):
        c.start(); sends.append(c)
    F = jnp.float32
    def load(k): return pltpu.make_async_copy(grads.at[k, :, :, :, c0], own.at[k], lsem.at[k])
    def ccopy(k): return rc(grads.at[k, :, :, :, 1 - c0], rcb.at[k], cs.at[k], cr.at[k], p.dev(z, co, y))
    def x1(k): return rc(own.at[k, :, 0:2, 1 - x], rx.at[k], xs.at[k, 0], xr.at[k, 0], p.dev(z, xo, y))
    def y1(k): return rc(own.at[k, 1 - y, 2:4], ry.at[k], ys.at[k, 0], yr.at[k, 0], p.dev(z, xc, yo))
    def y2(k): return rc(own.at[k, 1 - y, 0:2, x], ry2.at[k], ys.at[k, 1], yr.at[k, 1], p.dev(z, xc, yo))
    def x2(k): return rc(own.at[k, y, 2:4, 1 - x], rx2.at[k], xs.at[k, 1], xr.at[k, 1], p.dev(z, xo, y))
    def zc(k, j):
        zt = lax.rem(z + j, 4)
        return rc(own.at[k, y, zt, x], rz.at[k, j - 1], zs.at[k, j - 1], zr.at[k, j - 1], p.dev(zt, xc, y))
    def a(k):
        load(k).start(); go(ccopy(k))
    def b(k):
        load(k).wait(); ccopy(k).wait_recv()
        @pl.loop(0, 16)
        def _(i):
            yy, zz, xx = i // 8, lax.rem(i // 2, 4), lax.rem(i, 2)
            own[k, yy, zz, xx] = (own[k, yy, zz, xx].astype(F) + rcb[k, yy, zz, xx].astype(F)).astype(jnp.bfloat16)
        go(x1(k)); go(y1(k))
    def c(k):
        x1(k).wait_recv(); y1(k).wait_recv()
        @pl.loop(0, 4)
        def _(i):
            u, v = i // 2, lax.rem(i, 2)
            own[k, u, v, x] = (own[k, u, v, x].astype(F) + rx[k, u, v].astype(F)).astype(jnp.bfloat16)
            own[k, y, 2 + u, v] = (own[k, y, 2 + u, v].astype(F) + ry[k, u, v].astype(F)).astype(jnp.bfloat16)
        go(y2(k)); go(x2(k))
    def d(k):
        x2(k).wait_recv(); y2(k).wait_recv()
        @pl.loop(0, 2)
        def _(i):
            own[k, y, i, x] = (own[k, y, i, x].astype(F) + ry2[k, i].astype(F)).astype(jnp.bfloat16)
            own[k, y, 2 + i, x] = (own[k, y, 2 + i, x].astype(F) + rx2[k, i].astype(F)).astype(jnp.bfloat16)
        for j in (1, 2, 3): go(zc(k, j))
    def e(k):
        for j in (1, 2, 3): zc(k, j).wait_recv()
        out[k] = own[k, y, z, x].astype(F) + rz[k, 0].astype(F) + rz[k, 1].astype(F) + rz[k, 2].astype(F)
    a(0); a(1); b(0)
    for k in range(nk + 2):
        if k + 2 < nk: a(k + 2)
        if k + 1 < nk: b(k + 1)
        if k < nk: c(k)
        if 0 <= k - 1 < nk: d(k - 1)
        if 0 <= k - 2 < nk: e(k - 2)
    for s in sends: s.wait_send()

def scatter(grads, fold=1, collective_id=2):
    nk, _, _, _, _, rows, cols = grads.shape
    D = pltpu.SemaphoreType.DMA
    V = lambda *s: pltpu.VMEM(s + (rows, cols), jnp.bfloat16)
    return pl.pallas_call(
        functools.partial(scatter_kernel, fold, nk),
        out_shape=jax.ShapeDtypeStruct((nk, rows, cols), jnp.float32),
        in_specs=[pl.BlockSpec(memory_space=pl.ANY)],
        out_specs=pl.BlockSpec(memory_space=pltpu.VMEM),
        scratch_shapes=[V(nk, 2, 4, 2), V(nk, 2, 4, 2), V(nk, 2, 2), V(nk, 2, 2), V(nk, 2), V(nk, 2), V(nk, 3),
            D((nk,)), D((nk,)), D((nk,)), D((nk, 2)), D((nk, 2)), D((nk, 2)), D((nk, 2)), D((nk, 3)), D((nk, 3))],
        compiler_params=pltpu.CompilerParams(collective_id=collective_id, has_side_effects=True, vmem_limit_bytes=60 * 2**20),
    )(grads)


epsilon = 1e-12
masked_score = -1000000000.0


def gelu_exact(values):
    return jax.nn.gelu(values, approximate=False)


def build_mask(lengths, bucket, full_length):
    position = jnp.arange(full_length, dtype=jnp.int32)
    half_len = full_length // 2
    first_len = lengths[:, 0][:, None]
    second_len = lengths[:, 1][:, None]
    packed = (bucket == 0)[:, None]
    upper_half = (position >= half_len)[None, :]
    start_key = jnp.where(packed & upper_half, half_len, 0)
    end_key = jnp.where(
        packed, jnp.where(upper_half, half_len + second_len, first_len), first_len + second_len
    )
    key_pos = position[None, None, :]
    return (key_pos >= start_key[:, :, None]) & (key_pos < end_key[:, :, None])


def normalize(values):
    center = values - jnp.mean(values, axis=-1, keepdims=True)
    variance = jnp.mean(center * center, axis=-1, keepdims=True)
    inverse = lax.rsqrt(variance + epsilon)
    return (center * inverse, inverse)


def norm_back(grad_in, normed, inverse, gain_vec):
    scaled = grad_in * gain_vec
    return inverse * (
        scaled
        - jnp.mean(scaled, axis=-1, keepdims=True)
        - normed * jnp.mean(scaled * normed, axis=-1, keepdims=True)
    )


def attention_scores(queries, keys_low, key_valid):
    scores = (
        jnp.einsum("bqhe,bkhe->bhqk", queries, keys_low, preferred_element_type=jnp.float32) * 0.125
    )
    return jnp.where(key_valid[:, None], scores, masked_score)


def forward_layer(state_in, weights, vectors, key_valid):
    w_qkv, w_out, w_up, w_down = weights
    qv_bias, out_bias, gain_vec, shift_vec, up_bias = vectors
    batch_size = state_in.shape[0]
    full_x = state_in.astype(jnp.bfloat16)
    full_length = full_x.shape[1]
    local_width = w_qkv.shape[2]
    head_count = local_width // HEAD_DIM
    head_shape = (batch_size, full_length, head_count, HEAD_DIM)
    projected = jnp.einsum("bsd,tdc->tbsc", full_x, w_qkv, preferred_element_type=jnp.float32)
    queries = (projected[0] + qv_bias[0]).astype(jnp.bfloat16).reshape(head_shape)
    keys_low = projected[1].astype(jnp.bfloat16).reshape(head_shape)
    values_low = (projected[2] + qv_bias[1]).astype(jnp.bfloat16).reshape(head_shape)
    scores = attention_scores(queries, keys_low, key_valid)
    row_max = jnp.max(scores, axis=-1, keepdims=True)
    log_total = row_max + jnp.log(jnp.sum(jnp.exp(scores - row_max), axis=-1, keepdims=True))
    probs_low = jnp.exp(scores - log_total).astype(jnp.bfloat16)
    context = jnp.einsum(
        "bhqk,bkhe->bqhe", probs_low, values_low, preferred_element_type=jnp.float32
    )
    context = context.astype(jnp.bfloat16).reshape(batch_size, full_length, local_width)
    attn_out = (
        jnp.einsum("bsc,cd->bsd", context, w_out, preferred_element_type=jnp.float32)
    )
    normed_one, inverse_one = normalize(state_in + attn_out + out_bias[0])
    hidden = normed_one * gain_vec[0] + shift_vec[0]
    full_hidden = hidden.astype(jnp.bfloat16)
    pre_active = (
        jnp.einsum("bsd,df->bsf", full_hidden, w_up, preferred_element_type=jnp.float32) + up_bias
    )
    active = gelu_exact(pre_active).astype(jnp.bfloat16)
    ffn_out = (
        jnp.einsum("bsf,fd->bsd", active, w_down, preferred_element_type=jnp.float32)
    )
    normed_two, inverse_two = normalize(hidden + ffn_out + out_bias[1])
    result = normed_two * gain_vec[1] + shift_vec[1]
    saved_one = (
        full_x,
        queries,
        keys_low,
        values_low,
        log_total,
        context,
        normed_one,
        inverse_one,
        full_hidden,
        pre_active,
        active,
        normed_two,
        inverse_two,
    )
    return (result, saved_one)


def backward_layer(grad_in, saved_one, weights, vectors, key_valid):
    w_qkv, w_out, w_up, w_down = weights
    qv_bias, out_bias, gain_vec, shift_vec, up_bias = vectors
    (
        full_x,
        queries,
        keys_low,
        values_low,
        log_total,
        context,
        normed_one,
        inverse_one,
        full_hidden,
        pre_active,
        active,
        normed_two,
        inverse_two,
    ) = saved_one
    batch_size, full_length, head_count, _ = queries.shape
    local_width = head_count * HEAD_DIM
    flat_shape = (batch_size, full_length, local_width)
    gain_two = jnp.sum(grad_in * normed_two, axis=(0, 1))
    shift_two = jnp.sum(grad_in, axis=(0, 1))
    grad_second = norm_back(grad_in, normed_two, inverse_two, gain_vec[1])
    out_two = jnp.sum(grad_second, axis=(0, 1))
    full_second = grad_second.astype(jnp.bfloat16)
    grad_down = jnp.einsum("bsf,bsd->fd", active, full_second, preferred_element_type=jnp.float32)
    grad_active = jnp.einsum("bsd,fd->bsf", full_second, w_down, preferred_element_type=jnp.float32)
    grad_pre = jax.vjp(gelu_exact, pre_active)[1](grad_active)[0]
    up_grad = jnp.sum(grad_pre, axis=(0, 1))
    pre_low = grad_pre.astype(jnp.bfloat16)
    grad_up = jnp.einsum("bsd,bsf->df", full_hidden, pre_low, preferred_element_type=jnp.float32)
    grad_hidden = (
        (jnp.einsum("bsf,df->bsd", pre_low, w_up, preferred_element_type=jnp.float32))
        + grad_second
    )
    gain_one = jnp.sum(grad_hidden * normed_one, axis=(0, 1))
    shift_one = jnp.sum(grad_hidden, axis=(0, 1))
    grad_first = norm_back(grad_hidden, normed_one, inverse_one, gain_vec[0])
    out_one = jnp.sum(grad_first, axis=(0, 1))
    full_first = grad_first.astype(jnp.bfloat16)
    grad_out = jnp.einsum("bsc,bsd->cd", context, full_first, preferred_element_type=jnp.float32)
    grad_context = jnp.einsum("bsd,cd->bsc", full_first, w_out, preferred_element_type=jnp.float32)
    grad_context = grad_context.astype(jnp.bfloat16).reshape(queries.shape)
    scores = attention_scores(queries, keys_low, key_valid)
    attn_probs = jnp.exp(scores - log_total)
    probs_low = attn_probs.astype(jnp.bfloat16)
    grad_probs = jnp.einsum(
        "bqhe,bkhe->bhqk", grad_context, values_low, preferred_element_type=jnp.float32
    )
    grad_value = jnp.einsum(
        "bhqk,bqhe->bkhe", probs_low, grad_context, preferred_element_type=jnp.float32
    )
    grad_scores = attn_probs * (
        grad_probs - jnp.sum(attn_probs * grad_probs, axis=-1, keepdims=True)
    )
    scores_low = jnp.where(key_valid[:, None], grad_scores, 0.0).astype(jnp.bfloat16)
    grad_query = (
        jnp.einsum("bhqk,bkhe->bqhe", scores_low, keys_low, preferred_element_type=jnp.float32)
        * 0.125
    )
    grad_key = (
        jnp.einsum("bhqk,bqhe->bkhe", scores_low, queries, preferred_element_type=jnp.float32)
        * 0.125
    )
    grad_query = grad_query.reshape(flat_shape)
    grad_key = grad_key.reshape(flat_shape)
    grad_value = grad_value.reshape(flat_shape)
    qv_grad = jnp.stack([jnp.sum(grad_query, axis=(0, 1)), jnp.sum(grad_value, axis=(0, 1))])
    grad_proj = jnp.stack([grad_query, grad_key, grad_value], axis=0).astype(jnp.bfloat16)
    grad_qkv = jnp.einsum("bsd,tbsc->tdc", full_x, grad_proj, preferred_element_type=jnp.float32)
    grad_prev = (
        (jnp.einsum("tbsc,tdc->bsd", grad_proj, w_qkv, preferred_element_type=jnp.float32))
        + grad_first
    )
    matrices = (grad_qkv, grad_out, grad_up, grad_down)
    vector_set = (
        qv_grad,
        jnp.stack([out_one, out_two]),
        jnp.stack([gain_one, gain_two]),
        jnp.stack([shift_one, shift_two]),
        up_grad,
    )
    return (grad_prev, matrices, vector_set)


def full_weights(chunks, layer):
    a, b, c = (chunks[3 * layer + i].reshape(2, 768, 1536) for i in range(3))
    w_qkv = a[:, :, :1152].reshape(2, 768, 3, 384).transpose(2, 1, 0, 3).reshape(3, 768, 768)
    w_out = a[:, :, 1152:].transpose(0, 2, 1).reshape(768, 768)
    w_up = b.transpose(1, 0, 2).reshape(768, 3072)
    w_down = c.transpose(0, 2, 1).reshape(3072, 768)
    return w_qkv, w_out, w_up, w_down


def chunk_grads(matrices):
    g_qkv, g_out, g_up, g_down = (m.astype(jnp.bfloat16) for m in matrices)
    a = jnp.concatenate([
        g_qkv.reshape(3, 768, 2, 384).transpose(2, 1, 0, 3).reshape(2, 768, 1152),
        g_out.reshape(2, 384, 768).transpose(0, 2, 1)], axis=2)
    b = g_up.reshape(768, 2, 1536).transpose(1, 0, 2)
    c = g_down.reshape(2, 1536, 768).transpose(0, 2, 1)
    return [a, b, c]


def swap_rows(values):
    m = lax.axis_index("mp")
    keep = lax.dynamic_index_in_dim(values, m, 0, keepdims=False)
    send = lax.dynamic_index_in_dim(values, 1 - m, 0, keepdims=False)
    got = lax.ppermute(send, "mp", [(0, 1), (1, 0)])
    first = jnp.where(m == 0, keep, got)
    return jnp.concatenate([first, jnp.where(m == 0, got, keep)], 0)[None]


def swap_slots(values):
    m = lax.axis_index("mp")
    halves = values.reshape(2, values.shape[1] // 2, values.shape[2])
    keep = lax.dynamic_index_in_dim(halves, m, 0, keepdims=False)
    send = lax.dynamic_index_in_dim(halves, 1 - m, 0, keepdims=False)
    got = lax.ppermute(send, "mp", [(0, 1), (1, 0)])
    first = jnp.where(m == 0, keep, got)
    return jnp.stack([first, jnp.where(m == 0, got, keep)], 0)


def per_device(layer_input, cotangent, lengths, bucket, w_qkv, bias_qv, w_out, bias_out,
               ln_gain, ln_bias, w_up, bias_up, w_down):
    layers = w_qkv.shape[0]
    dp = lax.axis_size("dp")
    fold = dp // GROUPS
    part = lax.axis_index("mp")
    width = layer_input.shape[2]
    members = [[g * fold + i for i in range(fold)] for g in range(GROUPS)]
    packed = []
    for l in range(layers):
        packed.append(jnp.concatenate([w_qkv[l, 0], w_qkv[l, 1], w_qkv[l, 2], w_out[l].T], 1))
        packed.append(w_up[l])
        packed.append(w_down[l].T)
    packed = jnp.stack(packed)
    if fold > 1:
        packed = lax.all_gather(packed, "dp", axis=1, tiled=True, axis_index_groups=members)
    chunks = gather(packed, fold)
    weights = [full_weights(chunks, l) for l in range(layers)]
    full_qv = lax.all_gather(bias_qv, "mp", axis=2, tiled=True).astype(jnp.float32)
    full_up = lax.all_gather(bias_up, "mp", axis=1, tiled=True).astype(jnp.float32)
    vectors = [(full_qv[l], bias_out[l].astype(jnp.float32), ln_gain[l].astype(jnp.float32),
                ln_bias[l].astype(jnp.float32), full_up[l]) for l in range(layers)]
    current = swap_rows(layer_input).astype(jnp.float32)
    full_length = current.shape[1]
    mine = lambda v: lax.dynamic_slice_in_dim(v, part, 1, 0)
    key_valid = build_mask(mine(lengths), mine(bucket), full_length)
    kept = []
    for l in range(layers):
        current, saved = forward_layer(current, weights[l], vectors[l], key_valid)
        kept.append(saved)
    output = swap_slots(current.astype(jnp.bfloat16))
    grad_now = swap_rows(cotangent).astype(jnp.float32)
    sums = [None] * layers
    vecs = [None] * layers
    for l in reversed(range(layers)):
        grad_now, matrices, vecs[l] = backward_layer(grad_now, kept[l], weights[l], vectors[l], key_valid)
        sums[l] = chunk_grads(matrices)
    input_grad = swap_slots(grad_now.astype(jnp.bfloat16))
    grads = jnp.stack([g for l in range(layers) for g in sums[l]])
    grads = grads.reshape(3 * layers, 2, 4, 2, 2, 48, 1536)
    shards = scatter(grads, fold)
    if fold > 1:
        shards = lax.psum_scatter(shards, "dp", scatter_dimension=1, tiled=True, axis_index_groups=members)
    rows = shards.shape[1]
    shards = shards.reshape(layers, 3, rows, 1536)
    a, b, c = shards[:, 0], shards[:, 1], shards[:, 2]
    grad_qkv = a[:, :, :1152].reshape(layers, rows, 3, 384).transpose(0, 2, 1, 3)
    grad_out = a[:, :, 1152:].transpose(0, 2, 1)
    grad_down = c.transpose(0, 2, 1)
    stacked = [jnp.stack([vecs[l][i] for l in range(layers)]) for i in range(5)]
    qv, bias, gain, shift, up = lax.psum(tuple(stacked), ("dp", "mp"))
    half = width // 2
    qv = lax.dynamic_slice_in_dim(qv, part * half, half, 2)
    up = lax.dynamic_slice_in_dim(up, part * w_up.shape[2], w_up.shape[2], 1)
    return output, input_grad, grad_qkv, qv, grad_out, bias, gain, shift, b, up, grad_down


def solution(mesh):
    in_specs = (
        P("dp", "mp", None),
        P("dp", "mp", None),
        P("dp", None),
        P("dp"),
        P(None, None, "dp", "mp"),
        P(None, None, "mp"),
        P(None, "mp", "dp"),
        P(),
        P(),
        P(),
        P(None, "dp", "mp"),
        P(None, "mp"),
        P(None, "mp", "dp"),
    )
    out_specs = (
        P("dp", "mp", None),
        P("dp", "mp", None),
        P(None, None, "dp", "mp"),
        P(None, None, "mp"),
        P(None, "mp", "dp"),
        P(),
        P(),
        P(),
        P(None, "dp", "mp"),
        P(None, "mp"),
        P(None, "mp", "dp"),
    )
    return jax.shard_map(
        per_device, mesh=mesh, in_specs=in_specs, out_specs=out_specs, check_vma=False
    )
```

```python
import functools

import jax
import jax.numpy as jnp
from jax import lax
from jax.experimental import pallas as pl
from jax.experimental.pallas import tpu as pltpu
from jax.sharding import PartitionSpec as P

F32 = jnp.float32
BF16 = jnp.bfloat16
S = 512
D = 768
HALF = 384
UNITS = 1536
GROUPS = 16
EPS = 1e-12
MESH = pl.DeviceIdType.MESH
NN = (((1,), (0,)), ((), ()))
NT = (((1,), (1,)), ((), ()))
TN = (((0,), (0,)), ((), ()))
ANY = pl.BlockSpec(memory_space=pl.ANY)
VMEM = pl.BlockSpec(memory_space=pltpu.VMEM)
SMEM = pl.BlockSpec(memory_space=pltpu.SMEM)


def dot(a, b, dims=NN):
    return lax.dot_general(a, b, dims, preferred_element_type=F32)


def at(start, size):
    return pl.ds(pl.multiple_of(start, size), size)


def remote(src, dst, send_sem, recv_sem, device):
    return pltpu.make_async_remote_copy(
        src_ref=src, dst_ref=dst, send_sem=send_sem, recv_sem=recv_sem,
        device_id=device, device_id_type=MESH)


class Place:
    def __init__(self, fold):
        d = lax.axis_index("dp")
        self.fold = fold
        self.member = lax.rem(d, fold) if fold > 1 else 0
        g = d // fold if fold > 1 else d
        self.z = g // 4
        self.xc = lax.rem(g, 4)
        self.x = self.xc // 2
        self.c = lax.rem(self.xc, 2)
        self.y = lax.axis_index("mp")
        self.xo = (1 - self.x) * 2 + self.c
        self.co = self.x * 2 + (1 - self.c)
        self.yo = 1 - self.y
        self.to_z = [None] + [self.device(lax.rem(self.z + j, 4), self.xc, self.y) for j in (1, 2, 3)]
        self.to_x = self.device(self.z, self.xo, self.y)
        self.to_y = self.device(self.z, self.xc, self.yo)
        self.to_c = self.device(self.z, self.co, self.y)

    def device(self, z, xc, y):
        return {"dp": (z * 4 + xc) * self.fold + self.member, "mp": y}

    def greet(self):
        barrier = pltpu.get_barrier_semaphore()
        for device in (*self.to_z[1:], self.to_x, self.to_y, self.to_c):
            pl.semaphore_signal(barrier, inc=1, device_id=device, device_id_type=MESH)
        pl.semaphore_wait(barrier, 6)


class Gather:
    def __init__(self, place, packed, w, lsem, zs, zr, xs, xr, ys, yr, fs, fr, cs, cr):
        self.p, self.packed, self.w, self.lsem = place, packed, w, lsem
        self.sems = (zs, zr, xs, xr, ys, yr, fs, fr, cs, cr)
        self.zj = [lax.rem(place.z + 4 - j, 4) for j in range(4)]
        self.sends = []

    def go(self, copy):
        copy.start()
        self.sends.append(copy)

    def own(self, k):
        p = self.p
        return pltpu.make_async_copy(self.packed.at[k], self.w.at[k, p.y, p.z, p.xc], self.lsem.at[k])

    def src(self, k, j):
        p = self.p
        return self.packed.at[k] if j == 0 else self.w.at[k, p.y, self.zj[j], p.xc]

    def zcopy(self, k, j):
        p, (zs, zr, *_) = self.p, self.sems
        return remote(self.packed.at[k], self.w.at[k, p.y, p.z, p.xc], zs.at[k, j - 1], zr.at[k, j - 1], p.to_z[j])

    def xcopy(self, k, j):
        p, (_, _, xs, xr, *_) = self.p, self.sems
        return remote(self.src(k, j), self.w.at[k, p.y, self.zj[j], p.xc], xs.at[k, j], xr.at[k, j], p.to_x)

    def ycopy(self, k, j):
        p, (_, _, _, _, ys, yr, *_) = self.p, self.sems
        return remote(self.src(k, j), self.w.at[k, p.y, self.zj[j], p.xc], ys.at[k, j], yr.at[k, j], p.to_y)

    def fcopy(self, k, j):
        p, (*_, fs, fr, _, _) = self.p, self.sems
        if j % 2 == 0:
            block, to = self.w.at[k, p.y, self.zj[j], p.xo], p.to_y
        else:
            block, to = self.w.at[k, p.yo, self.zj[j], p.xc], p.to_x
        return remote(block, block, fs.at[k, j], fr.at[k, j], to)

    def ccopy(self, k, i):
        p, (*_, cs, cr) = self.p, self.sems
        y, xc = ((p.y, p.xc), (p.y, p.xo), (p.yo, p.xc), (p.yo, p.xo))[i]
        block = self.w.at[k, y, :, xc]
        return remote(block, block, cs.at[k, i], cr.at[k, i], p.to_c)

    def start(self, k):
        self.own(k).start()
        for j in (1, 2, 3):
            self.go(self.zcopy(k, j))
        self.go(self.xcopy(k, 0))
        self.go(self.ycopy(k, 0))

    def spread(self, k):
        for j in (1, 2, 3):
            self.zcopy(k, j).wait_recv()
            self.go(self.xcopy(k, j))
            self.go(self.ycopy(k, j))
        self.own(k).wait()
        self.go(self.ccopy(k, 0))

    def forward(self, k):
        for j in range(4):
            self.xcopy(k, j).wait_recv()
            if j % 2 == 0:
                self.go(self.fcopy(k, j))
            self.ycopy(k, j).wait_recv()
            if j % 2 == 1:
                self.go(self.fcopy(k, j))
        self.go(self.ccopy(k, 1))
        self.go(self.ccopy(k, 2))

    def share(self, k):
        for j in range(4):
            self.fcopy(k, j).wait_recv()
        self.go(self.ccopy(k, 3))

    def arrive(self, k):
        for i in range(4):
            self.ccopy(k, i).wait_recv()

    def finish(self):
        for copy in self.sends:
            copy.wait_send()

    @staticmethod
    def scratch(n):
        dma = pltpu.SemaphoreType.DMA
        return [dma((n,)), dma((n, 3)), dma((n, 3))] + [dma((n, 4))] * 8


def columns(w, y, cols):
    v = w[y, :, :, :, cols]
    return v.reshape(D, v.shape[-1])


def bounds(lengths, bucket, m):
    l0, l1, one = lengths[m, 0], lengths[m, 1], bucket[m] == 1
    half = S // 2
    return jnp.where(one, l0 + l1, l0), jnp.where(one, 0, half), jnp.where(one, l0 + l1, half + l1)


def key_bias(limits):
    first_end, second_start, second_end = limits
    k = lax.broadcasted_iota(jnp.int32, (S, 128), 0)
    lo = jnp.where(k < first_end, 0.0, -1e9)
    hi = jnp.where((k >= second_start) & (k < second_end), 0.0, -1e9)
    return lo, hi


def with_mask(q2, k2, half, bias):
    lane = lax.broadcasted_iota(jnp.int32, (S, 128), 1)
    low = lax.broadcasted_iota(jnp.int32, (S, 128), 0) < S // 2
    own = (lane // 64) == half
    o = 64 * (1 - half)
    one = lambda pick: jnp.where(pick, 1.0, 0.0)
    qa = jnp.where(lane == o, one(low), jnp.where(lane == o + 1, one(~low), 0.0))
    ka = jnp.where(lane == o, bias[0], jnp.where(lane == o + 1, bias[1], 0.0))
    qm = jnp.where(own, q2.astype(F32) * 0.125, qa).astype(BF16)
    km = jnp.where(own, k2.astype(F32), ka).astype(BF16)
    return qm, km


def head_pair(pair):
    y, r = pair // 3, lax.rem(pair, 3)
    return y, [at(o + 128 * r, 128) for o in (0, HALF, 2 * HALF)]


def attend(qkv, ctx, lse, limits, pair):
    y, (qc, kc, vc) = head_pair(pair)
    q2, k2, v2 = qkv[y, :, qc], qkv[y, :, kc], qkv[y, :, vc]
    bias = key_bias(limits)
    v2t = v2.T
    parts = []
    for half in range(2):
        qm, km = with_mask(q2, k2, half, bias)
        st = dot(km, qm, NT)
        top = jnp.max(st, axis=0, keepdims=True)
        e = jnp.exp(st - top)
        total = jnp.sum(e, axis=0, keepdims=True)
        lse[pair * 2 + half] = top + jnp.log(total)
        ct = dot(v2t[64 * half:64 * half + 64], e.astype(BF16))
        parts.append(ct * (1.0 / total))
    ctx[y, :, qc] = jnp.concatenate(parts, 0).T.astype(BF16)


def normalize(h, rows, gain, shift, n, r):
    v = h[rows, :]
    c = v - jnp.mean(v, axis=-1, keepdims=True)
    inverse = lax.rsqrt(jnp.mean(c * c, axis=-1, keepdims=True) + EPS)
    normed = c * inverse
    n[rows, :] = normed
    r[rows, :] = jnp.broadcast_to(inverse, (inverse.shape[0], 128))
    return normed * gain + shift


def gelu_parts(u):
    cdf = 0.5 * (1.0 + lax.erf(u * 0.7071067811865476))
    return u * cdf, cdf + u * (jnp.exp(-0.5 * u * u) * 0.3989422804014327)


def forward_kernel(fold, layers, packed, xin, cot, vec, glob, lengths, bucket,
                   w, cotf, out, xrt_o, qkv_o, lse_o, ctx_o, n1_o, r1_o, y1t_o, act_o, dg_o, n2_o, r2_o,
                   wv, xh, vecf, x, xr, xrt, qkv, lse, ctx, h, n1, r1, y1, y1r, y1t, act, dg, n2, r2, outv,
                   wsem, esem, ssem, *gsems):
    p = Place(fold)
    m = p.y
    g = Gather(p, packed, w, *gsems)
    parts = 3 * layers
    saves = {}
    names = ("xrt", "qkv", "lse", "ctx", "n1", "r1", "y1t", "act", "dg", "n2", "r2")

    def load(k):
        return pltpu.make_async_copy(w.at[k], wv.at[k % 3], wsem.at[k])

    def save(i, l, src, dst):
        if i in saves:
            saves.pop(i).wait()
        saves[i] = pltpu.make_async_copy(src, dst.at[l], ssem.at[names.index(i), l])
        saves[i].start()

    def before(*names):
        for i in names:
            if i in saves:
                saves.pop(i).wait()

    own_x = pltpu.make_async_copy(xin.at[m], xh.at[m], esem.at[0])
    swap_x = remote(xin.at[1 - m], xh.at[m], esem.at[1], esem.at[2], p.to_y)
    own_c = pltpu.make_async_copy(cot.at[m], cotf.at[m], esem.at[3])
    swap_c = remote(cot.at[1 - m], cotf.at[m], esem.at[4], esem.at[5], p.to_y)
    own_v = pltpu.make_async_copy(vec, vecf.at[m], esem.at[6])
    swap_v = remote(vec, vecf.at[m], esem.at[7], esem.at[8], p.to_y)
    limits = bounds(lengths, bucket, m)

    def row(i):
        return glob[i:i + 1, :]

    def stage_a(l):
        wa = wv.at[3 * l % 3]
        before("xrt", "qkv", "lse", "ctx", "n1", "r1", "y1t")
        xrt[...] = xr[...].T
        save("xrt", l, xrt, xrt_o)
        for y in range(2):
            for t in range(3):
                cols = slice(HALF * t, HALF * t + HALF)
                v = dot(xr[...], columns(wa, y, cols))
                if t != 1:
                    v = v + vecf[y, 2 + l:3 + l, HALF * (t // 2):HALF * (t // 2) + HALF]
                qkv[y, :, cols] = v.astype(BF16)
        save("qkv", l, qkv, qkv_o)

    def stage_att(l, first, last):
        pl.loop(first, last)(lambda i: attend(qkv, ctx, lse, limits, i))

    def stage_out(l):
        wa = wv.at[3 * l % 3]
        save("lse", l, lse, lse_o)
        save("ctx", l, ctx, ctx_o)
        wo = [columns(wa, y, slice(3 * HALF, 4 * HALF)) for y in range(2)]
        h[...] = x[...] + row(6 * l) + dot(ctx[0], wo[0], NT) + dot(ctx[1], wo[1], NT)

        @pl.loop(0, 4)
        def _(i):
            rows = at(128 * i, 128)
            o = normalize(h, rows, row(6 * l + 2), row(6 * l + 4), n1, r1)
            y1[rows, :] = o
            y1r[rows, :] = o.astype(BF16)
        y1t[...] = y1r[...].T
        save("n1", l, n1, n1_o)
        save("r1", l, r1, r1_o)
        save("y1t", l, y1t, y1t_o)

    def stage_b(l):
        wb = wv.at[(3 * l + 1) % 3]
        before("act", "dg", "n2", "r2")
        for y in range(2):
            @pl.loop(0, 3)
            def _(i):
                cols = at(512 * i, 512)
                u = dot(y1r[...], columns(wb, y, cols)) + vecf[y, l:l + 1, cols]
                a, d = gelu_parts(u)
                act[y, :, cols] = a.astype(BF16)
                dg[y, :, cols] = d.astype(BF16)
        save("act", l, act, act_o)
        save("dg", l, dg, dg_o)

    def stage_c(l):
        wc = wv.at[(3 * l + 2) % 3]
        full = slice(0, UNITS)
        h[...] = (y1[...] + row(6 * l + 1) + dot(act[0], columns(wc, 0, full), NT)
                  + dot(act[1], columns(wc, 1, full), NT))

        @pl.loop(0, 4)
        def _(i):
            rows = at(128 * i, 128)
            o = normalize(h, rows, row(6 * l + 3), row(6 * l + 5), n2, r2)
            x[rows, :] = o
            xr[rows, :] = o.astype(BF16)
        save("n2", l, n2, n2_o)
        save("r2", l, r2, r2_o)

    def compute(k):
        l, kind = k // 3, k % 3
        load(k).wait()
        if kind == 0:
            stage_a(l)
            stage_att(l, 0, 6)
            stage_out(l)
        elif kind == 1:
            stage_b(l)
        else:
            stage_c(l)

    own_x.start()
    own_v.start()
    own_c.start()
    p.greet()
    g.start(0)
    swap_v.start()
    swap_x.start()
    g.start(1)
    g.spread(0)
    for k in range(parts + 2):
        if k + 2 < parts:
            g.start(k + 2)
        if k + 1 < parts:
            g.spread(k + 1)
        if k == 1:
            swap_c.start()
        if k < parts:
            g.forward(k)
        if 0 <= k - 1 < parts:
            g.share(k - 1)
        if 0 <= k - 2 < parts:
            g.arrive(k - 2)
            load(k - 2).start()
            if k == 2:
                own_x.wait()
                swap_x.wait()
                own_v.wait()
                swap_v.wait()
                for i in range(2):
                    rows = slice(256 * i, 256 * i + 256)
                    xr[rows, :] = xh[i]
                    x[rows, :] = xh[i].astype(F32)
            compute(k - 2)
    own_c.wait()
    swap_c.wait()
    last = pltpu.make_async_copy(xr, out, esem.at[9])
    last.start()
    g.finish()
    for copy in saves.values():
        copy.wait()
    last.wait()


def forward(packed, xin, cot, vec, glob, lengths, bucket, layers, fold):
    n = 3 * layers
    dma = pltpu.SemaphoreType.DMA
    saved = [((D, S), BF16), ((2, S, 3 * HALF), BF16), ((12, 1, S), F32), ((2, S, HALF), BF16), ((S, D), F32), ((S, 128), F32),
             ((D, S), BF16), ((2, S, UNITS), BF16), ((2, S, UNITS), BF16), ((S, D), F32), ((S, 128), F32)]
    shape = jax.ShapeDtypeStruct
    vm = pltpu.VMEM
    return pl.pallas_call(
        functools.partial(forward_kernel, fold, layers),
        out_shape=[shape((n, 2, 4, 4, 48, UNITS), BF16), shape((2, S // 2, D), BF16), shape((S, D), BF16)]
        + [shape((layers, *s), d) for s, d in saved],
        in_specs=[ANY, ANY, ANY, ANY, VMEM, SMEM, SMEM],
        out_specs=[ANY] * (3 + len(saved)),
        scratch_shapes=[
            vm((3, 2, 4, 4, 48, UNITS), BF16), vm((2, S // 2, D), BF16), vm((2, 8, UNITS), F32), vm((S, D), F32),
            vm((S, D), BF16), vm((D, S), BF16), vm((2, S, 3 * HALF), BF16), vm((12, 1, S), F32), vm((2, S, HALF), BF16),
            vm((S, D), F32), vm((S, D), F32), vm((S, 128), F32), vm((S, D), F32), vm((S, D), BF16), vm((D, S), BF16),
            vm((2, S, UNITS), BF16), vm((2, S, UNITS), BF16), vm((S, D), F32), vm((S, 128), F32),
            vm((S, D), BF16), dma((n,)), dma((10,)), dma((11, layers)), *Gather.scratch(n)],
        compiler_params=pltpu.CompilerParams(collective_id=1, has_side_effects=True, vmem_limit_bytes=60 * 2**20),
    )(packed, xin, cot, vec, glob, lengths, bucket)


class Reduce:
    def __init__(self, place, total, slots, held, out, rc, rx, ry, rx2, ry2, rz, cs, cr, xs, xr, ys, yr, zs, zr, free):
        self.p, self.total, self.slots = place, total, slots
        self.held, self.out, self.buffers = held, out, (rc, rx, ry, rx2, ry2, rz)
        self.sems = (cs, cr, xs, xr, ys, yr, zs, zr)
        self.free = free
        self.sends = {}
        self.at = {}
        self.fresh = None

    def slot(self, u):
        for copy in self.sends.pop(u - self.slots, ()):
            copy.wait_send()
        return self.held.at[u % self.slots]

    def go(self, u, copy):
        copy.start()
        self.sends.setdefault(u, []).append(copy)

    def copies(self, u, kind, j=0):
        p, s = self.p, u % self.slots
        h = self.held.at[s]
        rc, rx, ry, rx2, ry2, rz = self.buffers
        cs, cr, xs, xr, ys, yr, zs, zr = self.sems
        if kind == "c":
            return remote(h.at[:, :, :, 1 - p.c], rc.at[s], cs.at[s], cr.at[s], p.to_c)
        if kind == "x1":
            return remote(h.at[:, 0:2, 1 - p.x, p.c], rx.at[s], xs.at[s, 0], xr.at[s, 0], p.to_x)
        if kind == "y1":
            return remote(h.at[p.yo, 2:4, :, p.c], ry.at[s], ys.at[s, 0], yr.at[s, 0], p.to_y)
        if kind == "y2":
            return remote(h.at[p.yo, 0:2, p.x, p.c], ry2.at[s], ys.at[s, 1], yr.at[s, 1], p.to_y)
        if kind == "x2":
            return remote(h.at[p.y, 2:4, 1 - p.x, p.c], rx2.at[s], xs.at[s, 1], xr.at[s, 1], p.to_x)
        to = lax.rem(p.z + j, 4)
        return remote(h.at[p.y, to, p.x, p.c], rz.at[s, j - 1], zs.at[s, j - 1], zr.at[s, j - 1], p.to_z[j])

    def peers(self):
        p = self.p
        return (p.to_c, p.to_x, p.to_y, p.to_z[1], p.to_z[2], p.to_z[3])

    def submit(self, u):
        if u >= self.slots:
            for i in range(6):
                pl.semaphore_wait(self.free.at[i], 1)
        self.go(u, self.copies(u, "c"))
        self.at[u] = 0
        self.fresh = u

    def stage(self, i, u):
        p, s = self.p, u % self.slots
        h = self.held.at[s]
        rc, rx, ry, rx2, ry2, rz = (b.at[s] for b in self.buffers)
        wait = lambda kind, j=0: self.copies(u, kind, j).wait_recv()
        if i == 1:
            wait("c")

            @pl.loop(0, 16)
            def _(n):
                y, z, x = n // 8, lax.rem(n // 2, 4), lax.rem(n, 2)
                h[y, z, x, p.c] = h[y, z, x, p.c] + rc[y, z, x]
            self.go(u, self.copies(u, "x1"))
            self.go(u, self.copies(u, "y1"))
        elif i == 2:
            wait("x1")
            wait("y1")

            @pl.loop(0, 4)
            def _(n):
                a, b = n // 2, lax.rem(n, 2)
                h[a, b, p.x, p.c] = h[a, b, p.x, p.c] + rx[a, b]
                h[p.y, 2 + a, b, p.c] = h[p.y, 2 + a, b, p.c] + ry[a, b]
            self.go(u, self.copies(u, "y2"))
            self.go(u, self.copies(u, "x2"))
        elif i == 3:
            wait("x2")
            wait("y2")

            @pl.loop(0, 2)
            def _(n):
                h[p.y, n, p.x, p.c] = h[p.y, n, p.x, p.c] + ry2[n]
                h[p.y, 2 + n, p.x, p.c] = h[p.y, 2 + n, p.x, p.c] + rx2[n]
            for j in (1, 2, 3):
                self.go(u, self.copies(u, "z", j))
        else:
            for j in (1, 2, 3):
                wait("z", j)
            f = lambda v: v.astype(F32)
            self.out[u] = f(h[p.y, p.z, p.x, p.c]) + f(rz[0]) + f(rz[1]) + f(rz[2])
            if u + self.slots < self.total:
                for i, device in zip((0, 1, 2, 5, 4, 3), self.peers()):
                    pl.semaphore_signal(self.free.at[i], inc=1, device_id=device, device_id_type=MESH)

    def pump(self):
        for u in sorted(self.at, reverse=True):
            if u == self.fresh:
                continue
            self.at[u] += 1
            self.stage(self.at[u], u)
            if self.at[u] == 4:
                del self.at[u]
        self.fresh = None

    def finish(self):
        for copies in self.sends.values():
            for copy in copies:
                copy.wait_send()

    @staticmethod
    def scratch(n, part):
        dma = pltpu.SemaphoreType.DMA
        v = lambda *s: pltpu.VMEM((n, *s, 48, part), BF16)
        return [v(2, 4, 2, 2)], [v(2, 4, 2), v(2, 2), v(2, 2), v(2), v(2), v(3), dma((n,)), dma((n,))] + [dma((n, 2))] * 4 + [
            dma((n, 3))] * 2 + [pltpu.SemaphoreType.REGULAR((6,))]


class Total:
    def __init__(self, place, v, got, zall, sems):
        self.p, self.v, self.got, self.zall = place, v, got, zall
        self.send, self.recv = sems
        self.last = []

    def copy(self, i):
        p = self.p
        if i < 3:
            return remote(self.v.at[i], self.got.at[i], self.send.at[i], self.recv.at[i], (p.to_c, p.to_x, p.to_y)[i])
        return remote(self.v.at[3], self.zall.at[p.z], self.send.at[i], self.recv.at[i], p.to_z[i - 2])

    def step(self, i, out=None):
        if 1 <= i <= 3:
            self.copy(i - 1).wait_recv()
            self.v[i] = self.v[i - 1] + self.got[i - 1]
        if i < 3:
            self.copy(i).start()
        elif i == 3:
            for j in (3, 4, 5):
                self.copy(j).start()
            self.zall[self.p.z] = self.v[3]
        else:
            for j in (3, 4, 5):
                self.copy(j).wait_recv()
            z = self.zall
            out[...] = (z[0] + z[1]) + (z[2] + z[3])
            for j in range(6):
                self.copy(j).wait_send()

    @staticmethod
    def scratch(rows):
        dma = pltpu.SemaphoreType.DMA
        v = lambda n: pltpu.VMEM((n, rows, D), F32)
        return [v(4), v(3), v(4), dma((6,)), dma((6,))]


def attend_back(qkv, lse, gc, gqkv, sums, limits, pair):
    y, (qc, kc, vc) = head_pair(pair)
    q2, k2, v2, c2 = qkv[y, :, qc], qkv[y, :, kc], qkv[y, :, vc], gc[y, :, qc]
    bias = key_bias(limits)
    lane = lax.broadcasted_iota(jnp.int32, (S, 128), 1)
    k2t = k2.T
    gq, gk, gv = [], [], []
    for half in range(2):
        qm, km = with_mask(q2, k2, half, bias)
        st = dot(km, qm, NT)
        probs = jnp.exp(st - lse[pair * 2 + half])
        vm = jnp.where((lane // 64) == half, v2, jnp.zeros_like(v2))
        gp = dot(vm, c2, NT)
        prod = probs * gp
        total = jnp.sum(prod, axis=0, keepdims=True)
        gs = (prod - probs * total).astype(BF16)
        gv.append(dot(probs.astype(BF16), c2))
        gk.append(dot(gs, q2))
        gq.append(dot(k2t[64 * half:64 * half + 64], gs))
    pick = lambda v: jnp.where(lane < 64, v[0], v[1])
    gqt = jnp.concatenate(gq, 0).T * 0.125
    gkt = pick(gk) * 0.125
    gvt = pick(gv)
    gqkv[y, :, qc] = gqt.astype(BF16)
    gqkv[y, :, kc] = gkt.astype(BF16)
    gqkv[y, :, vc] = gvt.astype(BF16)
    sums[y, 0, :, qc] = jnp.sum(gqt, axis=0, keepdims=True)
    sums[y, 1, :, qc] = jnp.sum(gvt, axis=0, keepdims=True)


def norm_back(g, rows, gain, n, r):
    v = g[rows, :]
    normed, inverse = n[rows, :], r[rows, 0:1]
    e = v * gain
    gh = inverse * (e - jnp.mean(e, axis=-1, keepdims=True) - normed * jnp.mean(e * normed, axis=-1, keepdims=True))
    add = lambda t: jnp.sum(t, axis=0, keepdims=True)
    return gh, add(v * normed), add(v), add(gh)


SLOTS = 5
PART = UNITS // 2
ROWS = 24


def backward_kernel(fold, layers, w, cotf, outx, glob, lengths, bucket,
                    xrt_o, qkv_o, lse_o, ctx_o, n1_o, r1_o, y1t_o, act_o, dg_o, n2_o, r2_o,
                    output, ingrad, shards, vout, vlate,
                    wv, g, gh, n, r, low, lowt, act, dg, y1t, ctx, qkv, lse, xrt, gc, gqkv, sums, gin,
                    wsem, lsem, esem, *rest):
    p = Place(fold)
    m = p.y
    red = Reduce(p, 6 * layers, SLOTS, rest[0], shards, *rest[1:16])
    early = Total(p, *rest[16:19], rest[19:21])
    late = Total(p, *rest[21:24], rest[24:26])
    limits = bounds(lengths, bucket, m)
    order = [3 * l + t for l in reversed(range(layers)) for t in (2, 1, 0)]
    full = slice(0, UNITS)

    def row(i):
        return glob[i:i + 1, :]

    def weights(i):
        return pltpu.make_async_copy(w.at[order[i]], wv.at[i % 2], wsem.at[i % 2])

    table = {"n2": (n2_o, n), "r2": (r2_o, r), "act": (act_o, act), "dg": (dg_o, dg), "y1t": (y1t_o, y1t),
             "n1": (n1_o, n), "r1": (r1_o, r), "ctx": (ctx_o, ctx), "qkv": (qkv_o, qkv), "lse": (lse_o, lse),
             "xrt": (xrt_o, xrt)}
    loads = {}

    def begin(l, *names):
        for i in names:
            src, dst = table[i]
            loads[i] = pltpu.make_async_copy(src.at[l], dst, lsem.at[list(table).index(i)])
            loads[i].start()

    def need(*names):
        for i in names:
            loads.pop(i).wait()

    def add(line, value):
        early.v[0, line:line + 1, :] = early.v[0, line:line + 1, :] + value

    def norm_stage(l, which):
        base = 12 * (layers - 1 - l)

        @pl.loop(0, 4)
        def _(i):
            rows = at(128 * i, 128)
            v, a, b, c = norm_back(g, rows, row(6 * l + 2 + which), n, r)
            gh[rows, :] = v
            low[rows, :] = v.astype(BF16)
            add(base + which, a)
            add(base + 2 + which, b)
            add(base + 4 + which, c)
        lowt[...] = low[...].T

    def tiles(u, left, right, start, width, to):
        s = red.slot(u)
        for y in range(2):
            @pl.loop(0, width // HALF)
            def _(i):
                v = dot(left[...], right[y, :, at(start + HALF * i, HALF)]).astype(BF16)
                s[y, :, :, :, :, at(to + HALF * i, HALF)] = v.reshape(4, 2, 2, 48, HALF)

    def submit(u):
        red.submit(u)
        red.pump()

    def layer(l, u, i):
        base = 12 * (layers - 1 - l)
        last = l == 0
        need("n2", "r2")
        norm_stage(l, 1)
        begin(l, "n1", "r1")
        need("act")
        for half in range(2):
            tiles(u + half, lowt, act, PART * half, PART, 0)
            submit(u + half)
        if not last:
            begin(l - 1, "act")
        weights(i).wait()
        wc = wv.at[i % 2]
        need("dg", "y1t")
        for half in range(2):
            for y in range(2):
                @pl.loop(0, 2)
                def _(j):
                    cols = at(PART * half + HALF * j, HALF)
                    gi = dot(low[...], columns(wc, y, cols)) * dg[y, :, cols].astype(F32)
                    dg[y, :, cols] = gi.astype(BF16)
                    line = base + 6 + 2 * y + half
                    early.v[0, line:line + 1, at(HALF * j, HALF)] = jnp.sum(gi, axis=0, keepdims=True)
            tiles(u + 2 + half, y1t, dg, PART * half, PART, 0)
            submit(u + 2 + half)
        if i + 2 < 3 * layers:
            weights(i + 2).start()
        weights(i + 1).wait()
        wb = wv.at[(i + 1) % 2]
        g[...] = gh[...] + dot(dg[0], columns(wb, 0, full), NT) + dot(dg[1], columns(wb, 1, full), NT)
        if i + 3 < 3 * layers:
            weights(i + 3).start()
        if not last:
            begin(l - 1, "dg", "y1t")
        need("n1", "r1")
        norm_stage(l, 0)
        red.pump()
        need("ctx")
        tiles(u + 4, lowt, ctx, 0, HALF, HALF)
        weights(i + 2).wait()
        wa = wv.at[(i + 2) % 2]
        for y in range(2):
            gc[y] = dot(low[...], columns(wa, y, slice(3 * HALF, 4 * HALF))).astype(BF16)
        if not last:
            begin(l - 1, "n2", "r2", "ctx")
        else:
            early.step(0)
        need("qkv", "lse", "xrt")
        pl.loop(0, 3)(lambda j: attend_back(qkv, lse, gc, gqkv, sums, limits, j))
        red.pump()
        if last:
            early.step(1)
        pl.loop(3, 6)(lambda j: attend_back(qkv, lse, gc, gqkv, sums, limits, j))
        if last:
            early.step(2)
        for y in range(2):
            for t in range(2):
                where = slice(HALF * y, HALF * y + HALF)
                if last:
                    late.v[0, t:t + 1, where] = sums[y, t]
                else:
                    early.v[0, base + 10 + t:base + 11 + t, where] = sums[y, t]
        tiles(u + 4, xrt, gqkv, 2 * HALF, HALF, 0)
        submit(u + 4)
        tiles(u + 5, xrt, gqkv, 0, 2 * HALF, 0)
        submit(u + 5)
        wqkv = [columns(wa, y, slice(0, 3 * HALF)) for y in range(2)]
        if last:
            early.step(3)
            late.step(0)
            for j in range(2):
                rows = at((S // 2) * (1 - m if j == 0 else m), S // 2)
                v = gh[rows, :] + dot(gqkv[0, rows, :], wqkv[0], NT) + dot(gqkv[1, rows, :], wqkv[1], NT)
                gin[j] = v.astype(BF16)
                if j == 0:
                    swap_g.start()
            own_g.start()
        else:
            g[...] = gh[...] + dot(gqkv[0], wqkv[0], NT) + dot(gqkv[1], wqkv[1], NT)
            begin(l - 1, "qkv", "lse", "xrt")
            if i + 4 < 3 * layers:
                weights(i + 4).start()

    own_o = pltpu.make_async_copy(outx.at[m], output.at[m], esem.at[0])
    swap_o = remote(outx.at[1 - m], output.at[m], esem.at[1], esem.at[2], p.to_y)
    own_g = pltpu.make_async_copy(gin.at[1], ingrad.at[m], esem.at[3])
    swap_g = remote(gin.at[0], ingrad.at[m], esem.at[4], esem.at[5], p.to_y)
    top = layers - 1
    cload = pltpu.make_async_copy(cotf, low, esem.at[6])
    cload.start()
    begin(top, "n2", "r2", "act")
    weights(0).start()
    begin(top, "dg", "y1t")
    weights(1).start()
    begin(top, "ctx", "qkv", "lse", "xrt")
    early.v[0] = jnp.zeros((ROWS, D), F32)
    late.v[0] = jnp.zeros((8, D), F32)
    cload.wait()
    g[...] = low[...].astype(F32)
    own_o.start()
    p.greet()
    swap_o.start()
    for j, l in enumerate(reversed(range(layers))):
        layer(l, 6 * j, 3 * j)
    early.step(4, vout)
    for step in range(1, 5):
        if red.at:
            red.pump()
        late.step(step, vlate)
    while red.at:
        red.pump()
    red.finish()
    own_o.wait()
    swap_o.wait()
    own_g.wait()
    swap_g.wait()


def backward(w, cotf, outx, glob, lengths, bucket, saved, layers, fold):
    n = 6 * layers
    dma = pltpu.SemaphoreType.DMA
    shape = jax.ShapeDtypeStruct
    vm = pltpu.VMEM
    first, rest = Reduce.scratch(SLOTS, PART)
    return pl.pallas_call(
        functools.partial(backward_kernel, fold, layers),
        out_shape=[shape((2, S // 2, D), BF16), shape((2, S // 2, D), BF16), shape((n, 48, PART), F32),
                   shape((ROWS, D), F32), shape((8, D), F32)],
        in_specs=[ANY, ANY, ANY, VMEM, SMEM, SMEM] + [ANY] * 11,
        out_specs=[ANY, ANY, VMEM, VMEM, VMEM],
        scratch_shapes=[
            vm((2, 2, 4, 4, 48, UNITS), BF16), vm((S, D), F32), vm((S, D), F32), vm((S, D), F32), vm((S, 128), F32),
            vm((S, D), BF16), vm((D, S), BF16), vm((2, S, UNITS), BF16), vm((2, S, UNITS), BF16), vm((D, S), BF16),
            vm((2, S, HALF), BF16), vm((2, S, 3 * HALF), BF16), vm((12, 1, S), F32), vm((D, S), BF16), vm((2, S, HALF), BF16),
            vm((2, S, 3 * HALF), BF16), vm((2, 2, 1, HALF), F32), vm((2, S // 2, D), BF16),
            dma((2,)), dma((11,)), dma((7,)), *first, *rest, *Total.scratch(ROWS), *Total.scratch(8)],
        compiler_params=pltpu.CompilerParams(collective_id=2, has_side_effects=True, vmem_limit_bytes=62 * 2**20),
    )(w, cotf, outx, glob, lengths, bucket, *saved)


def pack(w_qkv, w_out, w_up, w_down):
    parts = []
    for l in range(w_qkv.shape[0]):
        parts.append(jnp.concatenate([w_qkv[l, 0], w_qkv[l, 1], w_qkv[l, 2], w_out[l].T], 1))
        parts.append(w_up[l])
        parts.append(w_down[l].T)
    return jnp.stack(parts)


def per_device(layer_input, cotangent, lengths, bucket, w_qkv, bias_qv, w_out, bias_out, ln_gain, ln_bias, w_up, bias_up, w_down):
    layers = w_qkv.shape[0]
    fold = lax.axis_size("dp") // GROUPS
    members = [[g * fold + i for i in range(fold)] for g in range(GROUPS)]
    packed = pack(w_qkv, w_out, w_up, w_down)
    if fold > 1:
        packed = lax.all_gather(packed, "dp", axis=1, tiled=True, axis_index_groups=members)
    qv = jnp.pad(bias_qv.reshape(layers, 2 * HALF), ((0, 0), (0, UNITS - 2 * HALF)))
    vec = jnp.concatenate([bias_up, qv], 0).astype(F32)
    vec = jnp.pad(vec, ((0, 8 - vec.shape[0]), (0, 0)))
    glob = jnp.concatenate([bias_out, ln_gain, ln_bias], 1).astype(F32).reshape(6 * layers, D)
    glob = jnp.pad(glob, ((0, 16 - 6 * layers), (0, 0)))
    w, cotf, out, *saved = forward(packed, layer_input, cotangent, vec, glob, lengths, bucket, layers, fold)
    output, ingrad, shards, early, late = backward(
        w, cotf.reshape(S, D), out.reshape(2, S // 2, D), glob, lengths, bucket, saved, layers, fold)
    if fold > 1:
        shards = lax.psum_scatter(shards, "dp", scatter_dimension=1, tiled=True, axis_index_groups=members)
        early, late = lax.psum((early, late), "dp", axis_index_groups=members)
    rows = shards.shape[1]
    part = lax.axis_index("mp")
    shards = jnp.flip(shards.reshape(layers, 6, rows, PART), 0)
    down, up, vo, qk = shards[:, 0:2], shards[:, 2:4], shards[:, 4], shards[:, 5]
    grad_qkv = jnp.stack([qk[..., :HALF], qk[..., HALF:], vo[..., :HALF]], 1)
    grad_out = vo[..., HALF:].transpose(0, 2, 1)
    grad_up = up.transpose(0, 2, 1, 3).reshape(layers, rows, UNITS)
    grad_down = down.transpose(0, 1, 3, 2).reshape(layers, UNITS, rows)
    vecs = jnp.flip(early.reshape(layers, 12, D), 0)
    gain, shift, bias = vecs[:, 0:2], vecs[:, 2:4], vecs[:, 4:6]
    grad_bias_up = lax.dynamic_slice_in_dim(vecs[:, 6:10].reshape(layers, 2, UNITS), part, 1, 1)[:, 0]
    qv = jnp.concatenate([late[None, 0:2], vecs[1:, 10:12]], 0)
    qv = lax.dynamic_slice_in_dim(qv, part * HALF, HALF, 2)
    return output, ingrad, grad_qkv, qv, grad_out, bias, gain, shift, grad_up, grad_bias_up, grad_down


def solution(mesh):
    in_specs = (
        P("dp", "mp", None),
        P("dp", "mp", None),
        P("dp", None),
        P("dp"),
        P(None, None, "dp", "mp"),
        P(None, None, "mp"),
        P(None, "mp", "dp"),
        P(),
        P(),
        P(),
        P(None, "dp", "mp"),
        P(None, "mp"),
        P(None, "mp", "dp"),
    )
    out_specs = (
        P("dp", "mp", None),
        P("dp", "mp", None),
        P(None, None, "dp", "mp"),
        P(None, None, "mp"),
        P(None, "mp", "dp"),
        P(),
        P(),
        P(),
        P(None, "dp", "mp"),
        P(None, "mp"),
        P(None, "mp", "dp"),
    )
    return jax.shard_map(
        per_device, mesh=mesh, in_specs=in_specs, out_specs=out_specs, check_vma=False
    )
```

```python
import functools

import jax
import jax.numpy as jnp
from jax import lax
from jax.experimental import pallas as pl
from jax.experimental.pallas import tpu as pltpu
from jax.sharding import PartitionSpec as P

F32 = jnp.float32
BF16 = jnp.bfloat16
S = 512
D = 768
HALF = 384
UNITS = 1536
GROUPS = 16
EPS = 1e-12
MESH = pl.DeviceIdType.MESH
NN = (((1,), (0,)), ((), ()))
NT = (((1,), (1,)), ((), ()))
TN = (((0,), (0,)), ((), ()))
ANY = pl.BlockSpec(memory_space=pl.ANY)
VMEM = pl.BlockSpec(memory_space=pltpu.VMEM)
SMEM = pl.BlockSpec(memory_space=pltpu.SMEM)


def dot(a, b, dims=NN):
    return lax.dot_general(a, b, dims, preferred_element_type=F32)


def at(start, size):
    return pl.ds(pl.multiple_of(start, size), size)


def remote(src, dst, send_sem, recv_sem, device):
    return pltpu.make_async_remote_copy(
        src_ref=src, dst_ref=dst, send_sem=send_sem, recv_sem=recv_sem,
        device_id=device, device_id_type=MESH)


class Place:
    def __init__(self, fold):
        d = lax.axis_index("dp")
        self.fold = fold
        self.member = lax.rem(d, fold) if fold > 1 else 0
        g = d // fold if fold > 1 else d
        self.z = g // 4
        self.xc = lax.rem(g, 4)
        self.x = self.xc // 2
        self.c = lax.rem(self.xc, 2)
        self.y = lax.axis_index("mp")
        self.xo = (1 - self.x) * 2 + self.c
        self.co = self.x * 2 + (1 - self.c)
        self.yo = 1 - self.y
        self.to_z = [None] + [self.device(lax.rem(self.z + j, 4), self.xc, self.y) for j in (1, 2, 3)]
        self.to_x = self.device(self.z, self.xo, self.y)
        self.to_y = self.device(self.z, self.xc, self.yo)
        self.to_c = self.device(self.z, self.co, self.y)

    def device(self, z, xc, y):
        return {"dp": (z * 4 + xc) * self.fold + self.member, "mp": y}

    def greet(self):
        barrier = pltpu.get_barrier_semaphore()
        for device in (*self.to_z[1:], self.to_x, self.to_y, self.to_c):
            pl.semaphore_signal(barrier, inc=1, device_id=device, device_id_type=MESH)
        pl.semaphore_wait(barrier, 6)


class Gather:
    def __init__(self, place, packed, w, turned, via_x, lsem, zs, zr, xs, xr, ys, yr, fs, fr, cs, cr, qs, qr):
        self.p, self.packed, self.w, self.turned, self.via_x = place, packed, w, turned, via_x
        self.sems = dict(z=(zs, zr), x=(xs, xr), y=(ys, yr), f=(fs, fr), c=(cs, cr), q=(qs, qr))
        self.lsem = lsem
        z = place.z
        low = z < 2
        self.order = [z, jnp.where(low, 1 - z, 5 - z), jnp.where(low, 2, 1), jnp.where(low, 3, 0)]
        self.inner = (z == 1) | (z == 2)
        self.partner = place.device(z + 1 - 2 * lax.rem(z, 2), place.xc, place.y)
        self.across = place.device(3 - z, place.xc, place.y)
        self.sends, self.inner_sends, self.waited = [], [], set()

    def go(self, make):
        make().start()
        self.sends.append(make)

    def go_inner(self, make):
        pl.when(self.inner)(lambda: make().start())
        self.inner_sends.append(make)

    def copy(self, kind, k, i, j, src, dst, device):
        send, recv = self.sems[kind]
        return remote(src, dst, send.at[k, i], recv.at[k, j], device)

    def block(self, k, j=0, other_x=False, other_y=False):
        p = self.p
        return self.w.at[k, p.yo if other_y else p.y, self.order[j], 1 - p.x if other_x else p.x, p.c]

    def source(self, k, j):
        return self.packed.at[k] if j == 0 else self.block(k, j)

    def own(self, k):
        return pltpu.make_async_copy(self.packed.at[k], self.block(k), self.lsem.at[k])

    def load(self, k, j):
        return self.w.at[k, :, self.order[j], :, self.p.c] if k == self.turned else self.block(k, j)

    def line(self, k, i):
        j, slot, device = ((0, 1, self.partner), (0, 2, self.across), (1, 3, self.across), (2, 2, self.partner),
                           (3, 3, self.partner))[i]
        src = dst = self.load(k, j)
        if j == 0 and k != self.turned:
            src = self.packed.at[k]
        return self.copy("z", k, i, slot, src, dst, device)

    def line_start(self, k):
        self.go(lambda: self.line(k, 0))
        self.go_inner(lambda: self.line(k, 1))

    def line_wait(self, k, j):
        self.copy("z", k, 0, j, self.load(k, j), self.load(k, j), self.partner).wait_recv()
        self.go_inner(lambda: self.line(k, j + 1))

    def to_x(self, k, j):
        return self.copy("x", k, j, j, self.source(k, j), self.block(k, j), self.p.to_x)

    def to_y(self, k, j):
        return self.copy("y", k, j, j, self.source(k, j), self.block(k, j), self.p.to_y)

    def diagonal(self, k, j):
        x = self.via_x(k, j)
        block = self.block(k, j, other_x=not x, other_y=x)
        return self.copy("f", k, j, j, block, block, self.p.to_x if x else self.p.to_y)

    def to_core(self, k, i):
        p = self.p
        if k == self.turned:
            block = self.load(k, i)
        else:
            y, x = ((p.y, p.x), (p.y, 1 - p.x), (p.yo, p.x), (p.yo, 1 - p.x))[i]
            block = self.w.at[k, y, :, x, p.c]
        return self.copy("c", k, i, i, block, block, p.to_c)

    def start(self, k):
        self.own(k).start()
        self.line_start(k)
        self.go(lambda: self.to_x(k, 0))
        self.go(lambda: self.to_y(k, 0))

    def spread(self, k, j):
        self.go(lambda: self.to_x(k, j))
        self.go(lambda: self.to_y(k, j))
        if j == 3:
            self.own(k).wait()
            self.go(lambda: self.to_core(k, 0))

    def seen(self, kind, k, j):
        if (kind, k, j) not in self.waited:
            self.waited.add((kind, k, j))
            (self.to_x if kind == "x" else self.to_y)(k, j).wait_recv()

    def forward(self, k, j):
        self.seen("y" if self.via_x(k, j) else "x", k, j)
        self.go(lambda: self.diagonal(k, j))

    def side(self, k, kind):
        for j in range(4):
            self.seen(kind, k, j)
        self.go(lambda: self.to_core(k, 1 if kind == "x" else 2))

    def share(self, k):
        for j in range(4):
            self.diagonal(k, j).wait_recv()
        self.go(lambda: self.to_core(k, 3))

    def arrive(self, k):
        for i in range(4):
            self.to_core(k, i).wait_recv()

    def turned_copy(self, i):
        p, k = self.p, self.turned
        if i < 2:
            return self.copy("q", 0, i, i, self.packed.at[k], self.block(k), (p.to_x, p.to_y)[i])
        half = slice(UNITS // 2 * (i - 2), UNITS // 2 * (i - 1))
        block = self.block(k, other_x=i == 2, other_y=i == 3).at[:, half]
        return self.copy("q", 0, i, i, block, block, (p.to_y, p.to_x)[i - 2])

    def turned_start(self):
        self.own(self.turned).start()
        self.go(lambda: self.turned_copy(0))
        self.go(lambda: self.turned_copy(1))

    def turned_forward(self, i):
        self.turned_copy(i).wait_recv()
        self.go(lambda: self.turned_copy(2 + i))

    def turned_line(self, j):
        k = self.turned
        if j == 0:
            self.own(k).wait()
            self.turned_copy(2).wait_recv()
            self.turned_copy(3).wait_recv()
            self.line_start(k)
        else:
            self.line_wait(k, j)
        self.go(lambda: self.to_core(k, j))

    def finish(self):
        for make in self.sends:
            make().wait_send()
        for make in self.inner_sends:
            pl.when(self.inner)(lambda: make().wait_send())

    @staticmethod
    def scratch(n):
        dma = pltpu.SemaphoreType.DMA
        return [dma((n,)), dma((n, 5)), dma((n, 4))] + [dma((n, 4))] * 8 + [dma((1, 4))] * 2


def columns(w, y, cols):
    v = w[y, :, :, :, :, cols]
    return v.reshape(D, v.shape[-1])


def bounds(lengths, bucket, m):
    l0, l1, one = lengths[m, 0], lengths[m, 1], bucket[m] == 1
    half = S // 2
    return jnp.where(one, l0 + l1, l0), jnp.where(one, 0, half), jnp.where(one, l0 + l1, half + l1)


def key_bias(limits):
    first_end, second_start, second_end = limits
    k = lax.broadcasted_iota(jnp.int32, (S, 128), 0)
    lo = jnp.where(k < first_end, 0.0, -1e9)
    hi = jnp.where((k >= second_start) & (k < second_end), 0.0, -1e9)
    return lo, hi


def with_mask(q2, k2, half, bias):
    lane = lax.broadcasted_iota(jnp.int32, (S, 128), 1)
    low = lax.broadcasted_iota(jnp.int32, (S, 128), 0) < S // 2
    own = (lane // 64) == half
    o = 64 * (1 - half)
    one = lambda pick: jnp.where(pick, 1.0, 0.0)
    qa = jnp.where(lane == o, one(low), jnp.where(lane == o + 1, one(~low), 0.0))
    ka = jnp.where(lane == o, bias[0], jnp.where(lane == o + 1, bias[1], 0.0))
    qm = jnp.where(own, q2.astype(F32) * 0.125, qa).astype(BF16)
    km = jnp.where(own, k2.astype(F32), ka).astype(BF16)
    return qm, km


def head_pair(pair):
    y, r = pair // 3, lax.rem(pair, 3)
    return y, [at(o + 128 * r, 128) for o in (0, HALF, 2 * HALF)]


def attend(qkv, ctx, lse, limits, pair):
    y, (qc, kc, vc) = head_pair(pair)
    q2, k2, v2 = qkv[y, :, qc], qkv[y, :, kc], qkv[y, :, vc]
    bias = key_bias(limits)
    v2t = v2.T
    parts = []
    for half in range(2):
        qm, km = with_mask(q2, k2, half, bias)
        st = dot(km, qm, NT)
        top = jnp.max(st, axis=0, keepdims=True)
        e = jnp.exp(st - top)
        total = jnp.sum(e, axis=0, keepdims=True)
        lse[pair * 2 + half] = top + jnp.log(total)
        ct = dot(v2t[64 * half:64 * half + 64], e.astype(BF16))
        parts.append(ct * (1.0 / total))
    ctx[y, :, qc] = jnp.concatenate(parts, 0).T.astype(BF16)


def normalize(h, rows, gain, shift, n, r):
    v = h[rows, :]
    c = v - jnp.mean(v, axis=-1, keepdims=True)
    inverse = lax.rsqrt(jnp.mean(c * c, axis=-1, keepdims=True) + EPS)
    normed = c * inverse
    n[rows, :] = normed
    r[rows, :] = jnp.broadcast_to(inverse, (inverse.shape[0], 128))
    return normed * gain + shift


def gelu_parts(u):
    cdf = 0.5 * (1.0 + lax.erf(u * 0.7071067811865476))
    return u * cdf, cdf + u * (jnp.exp(-0.5 * u * u) * 0.3989422804014327)


PLAN = (
    ("TS",), ("S", 0), ("S", 4), ("TF", 0), ("L", 0, 1), ("S", 2), ("L", 4, 1), ("L", 2, 1), ("S", 1), ("L", 0, 2),
    ("XY", 0, 1), ("XY", 0, 2), ("L", 2, 2), ("L", 0, 3), ("XY", 0, 3), ("F", 0, 0), ("L", 1, 1), ("L", 1, 2), ("S", 5),
    ("L", 2, 3), ("XY", 2, 2), ("CY", 0), ("F", 0, 1), ("F", 0, 2), ("L", 1, 3), ("F", 0, 3), ("TF", 1), ("L", 4, 2),
    ("CX", 0), ("SX",), ("L", 5, 1), ("L", 5, 2), ("XY", 1, 3), ("XY", 1, 1), ("XY", 1, 2), ("SH", 0), ("F", 2, 2),
    ("TL", 0), ("F", 1, 3), ("AR", 0), ("F", 1, 0), ("XY", 2, 1), ("CX", 1), ("XY", 2, 3), ("L", 4, 3), ("F", 1, 1),
    ("CY", 1), ("F", 1, 2), ("XY", 4, 3), ("L", 5, 3), ("F", 2, 3), ("SH", 1), ("F", 2, 0), ("TL", 1), ("CX", 2),
    ("TL", 2), ("F", 2, 1), ("XY", 4, 1), ("AR", 1), ("F", 4, 0), ("CY", 2), ("XY", 4, 2), ("SH", 2), ("XY", 5, 2),
    ("XY", 5, 1), ("XY", 5, 3), ("F", 4, 1), ("TL", 3), ("CY", 4), ("F", 4, 2), ("AR", 2), ("CX", 4), ("F", 5, 2),
    ("F", 5, 1), ("AR", 3), ("CX", 5), ("F", 5, 0), ("F", 4, 3), ("CY", 5), ("F", 5, 3), ("SH", 4), ("SC",), ("SH", 5),
    ("AR", 4), ("AR", 5),
)
TURNED = 3
VIA_X = ((1, 0, 0, 1), (0, 1, 1, 0), (1, 1, 1, 0), (0, 1, 0, 1), (0, 0, 1, 0), (1, 1, 1, 0))


def forward_kernel(fold, layers, packed, xin, cot, vec, glob, lengths, bucket,
                   w, cotf, out, xr_o, qkv_o, lse_o, ctx_o, n1_o, r1_o, y1r_o, act_o, dg_o, n2_o, r2_o,
                   wv, xh, vecf, x, xr, qkv, lse, ctx, h, n1, r1, y1, y1r, act, dg, n2, r2,
                   wsem, esem, ssem, *gsems):
    p = Place(fold)
    m = p.y
    parts = 3 * layers
    assert parts == len(VIA_X)
    g = Gather(p, packed, w, TURNED, lambda k, j: VIA_X[k][j], *gsems)
    saves = {}
    names = ("xr", "qkv", "lse", "ctx", "n1", "r1", "y1r", "act", "dg", "n2", "r2")

    def load(k):
        return pltpu.make_async_copy(w.at[k], wv.at[k], wsem.at[k])

    def save(i, l, src, dst):
        if i in saves:
            saves.pop(i).wait()
        saves[i] = pltpu.make_async_copy(src, dst.at[l], ssem.at[names.index(i), l])
        saves[i].start()

    def before(*names):
        for i in names:
            if i in saves:
                saves.pop(i).wait()

    own_x = pltpu.make_async_copy(xin.at[m], xh.at[m], esem.at[0])
    swap_x = remote(xin.at[1 - m], xh.at[m], esem.at[1], esem.at[2], p.to_y)
    own_c = pltpu.make_async_copy(cot.at[m], cotf.at[m], esem.at[3])
    swap_c = remote(cot.at[1 - m], cotf.at[m], esem.at[4], esem.at[5], p.to_y)
    own_v = pltpu.make_async_copy(vec, vecf.at[m], esem.at[6])
    swap_v = remote(vec, vecf.at[m], esem.at[7], esem.at[8], p.to_y)
    limits = bounds(lengths, bucket, m)

    def row(i):
        return glob[i:i + 1, :]

    def stage_a(l, y):
        wa = wv.at[3 * l]
        if y == 0:
            before("xr", "qkv", "lse", "ctx", "n1", "r1", "y1r")
            save("xr", l, xr, xr_o)
        for t in range(3):
            cols = slice(HALF * t, HALF * t + HALF)
            v = dot(xr[...], columns(wa, y, cols))
            if t != 1:
                v = v + vecf[y, 2 + l:3 + l, HALF * (t // 2):HALF * (t // 2) + HALF]
            qkv[y, :, cols] = v.astype(BF16)
        if y == 1:
            save("qkv", l, qkv, qkv_o)

    def stage_out(l):
        wa = wv.at[3 * l]
        save("lse", l, lse, lse_o)
        save("ctx", l, ctx, ctx_o)
        wo = [columns(wa, y, slice(3 * HALF, 4 * HALF)) for y in range(2)]
        h[...] = x[...] + row(6 * l) + dot(ctx[0], wo[0], NT) + dot(ctx[1], wo[1], NT)

        @pl.loop(0, 2)
        def _(i):
            rows = at(256 * i, 256)
            o = normalize(h, rows, row(6 * l + 2), row(6 * l + 4), n1, r1)
            y1[rows, :] = o
            y1r[rows, :] = o.astype(BF16)
        save("n1", l, n1, n1_o)
        save("r1", l, r1, r1_o)
        save("y1r", l, y1r, y1r_o)

    def stage_b(l, y, i):
        wb = wv.at[3 * l + 1]
        if y == 0 and i == 0:
            before("act", "dg", "n2", "r2")
        cols = slice(768 * i, 768 * i + 768)
        u = dot(y1r[...], columns(wb, y, cols)) + vecf[y, l:l + 1, cols]
        a, d = gelu_parts(u)
        act[y, :, cols] = a.astype(BF16)
        dg[y, :, cols] = d.astype(BF16)
        if y == 1 and i == 1:
            save("act", l, act, act_o)
            save("dg", l, dg, dg_o)

    def stage_c(l):
        wc = wv.at[3 * l + 2]
        before("xr")
        full = slice(0, UNITS)
        h[...] = (y1[...] + row(6 * l + 1) + dot(act[0], columns(wc, 0, full), NT)
                  + dot(act[1], columns(wc, 1, full), NT))

        @pl.loop(0, 2)
        def _(i):
            rows = at(256 * i, 256)
            o = normalize(h, rows, row(6 * l + 3), row(6 * l + 5), n2, r2)
            x[rows, :] = o
            xr[rows, :] = o.astype(BF16)
        save("n2", l, n2, n2_o)
        save("r2", l, r2, r2_o)

    pending, here, used = [], set(), [0]

    def ready(k):
        l, kind = k // 3, k % 3
        pending.append(lambda: load(k).wait())
        if k == 0:
            pending.append(first)
        if kind == 0:
            pending.append(lambda: stage_a(l, 0))
            pending.append(lambda: stage_a(l, 1))
            pending.append((6, lambda j: attend(qkv, ctx, lse, limits, j)))
            pending.append(lambda: stage_out(l))
        elif kind == 1:
            for y in range(2):
                for i in range(2):
                    pending.append(lambda y=y, i=i: stage_b(l, y, i))
        else:
            pending.append(lambda: stage_c(l))

    def first():
        own_x.wait()
        swap_x.wait()
        own_v.wait()
        swap_v.wait()
        for i in range(2):
            rows = slice(256 * i, 256 * i + 256)
            xr[rows, :] = xh[i]
            x[rows, :] = xh[i].astype(F32)

    def run(steps):
        steps = list(steps)
        while steps or pending:
            piece = pending.pop(0) if pending else None
            if isinstance(piece, tuple):
                inside, steps = steps[:piece[0]], steps[piece[0]:]

                @pl.loop(0, piece[0])
                def _(j):
                    piece[1](j)
                    for i, step in enumerate(inside):
                        pl.when(j == i)(step)
            else:
                if piece is not None:
                    piece()
                if steps:
                    steps.pop(0)()

    def arrived(k):
        g.arrive(k)
        load(k).start()
        here.add(k)
        while used[0] in here:
            ready(used[0])
            used[0] += 1

    steps = {
        "S": g.start, "L": g.line_wait, "XY": g.spread, "F": g.forward, "CX": lambda k: g.side(k, "x"),
        "CY": lambda k: g.side(k, "y"), "SH": g.share, "AR": arrived, "TS": g.turned_start, "TF": g.turned_forward,
        "TL": g.turned_line, "SX": lambda: (swap_v.start(), swap_x.start()), "SC": lambda: swap_c.start()}
    plan = [lambda t=t: steps[t[0]](*t[1:]) for t in PLAN]

    own_x.start()
    own_v.start()
    own_c.start()
    p.greet()
    run(plan)
    own_c.wait()
    swap_c.wait()
    last = pltpu.make_async_copy(xr, out, esem.at[9])
    last.start()
    g.finish()
    for copy in saves.values():
        copy.wait()
    last.wait()


def forward(packed, xin, cot, vec, glob, lengths, bucket, layers, fold):
    n = 3 * layers
    dma = pltpu.SemaphoreType.DMA
    saved = [((S, D), BF16), ((2, S, 3 * HALF), BF16), ((12, 1, S), F32), ((2, S, HALF), BF16), ((S, D), F32), ((S, 128), F32),
             ((S, D), BF16), ((2, S, UNITS), BF16), ((2, S, UNITS), BF16), ((S, D), F32), ((S, 128), F32)]
    shape = jax.ShapeDtypeStruct
    vm = pltpu.VMEM
    return pl.pallas_call(
        functools.partial(forward_kernel, fold, layers),
        out_shape=[shape((n, 2, 4, 2, 2, 48, UNITS), BF16), shape((2, S // 2, D), BF16), shape((S, D), BF16)]
        + [shape((layers, *s), d) for s, d in saved],
        in_specs=[ANY, ANY, ANY, ANY, VMEM, SMEM, SMEM],
        out_specs=[ANY] * (3 + len(saved)),
        scratch_shapes=[
            vm((n, 2, 4, 2, 2, 48, UNITS), BF16), vm((2, S // 2, D), BF16), vm((2, 8, UNITS), F32), vm((S, D), F32),
            vm((S, D), BF16), vm((2, S, 3 * HALF), BF16), vm((12, 1, S), F32), vm((2, S, HALF), BF16),
            vm((S, D), F32), vm((S, D), F32), vm((S, 128), F32), vm((S, D), F32), vm((S, D), BF16),
            vm((2, S, UNITS), BF16), vm((2, S, UNITS), BF16), vm((S, D), F32), vm((S, 128), F32),
            dma((n,)), dma((10,)), dma((11, layers)), *Gather.scratch(n)],
        compiler_params=pltpu.CompilerParams(collective_id=1, has_side_effects=True, vmem_limit_bytes=60 * 2**20),
    )(packed, xin, cot, vec, glob, lengths, bucket)


class Reduce:
    def __init__(self, place, total, slots, split, held, out, rc, rx, ry, rx2, ry2, rz, cs, cr, xs, xr, ys, yr, zs, zr, free):
        self.p, self.total, self.slots, self.split = place, total, slots, split
        self.held, self.out, self.buffers = held, out, (rc, rx, ry, rx2, ry2, rz)
        self.sems = (cs, cr, xs, xr, ys, yr, zs, zr)
        self.free = free
        self.sends = {}

    def slot(self, u):
        for args in self.sends.pop(u - self.slots, ()):
            self.copy(u - self.slots, *args).wait_send()
        return self.held.at[u % self.slots]

    def go(self, u, *args):
        self.copy(u, *args).start()
        self.sends.setdefault(u, []).append(args)

    def got(self, u, *args):
        self.copy(u, *args).wait_recv()

    def copy(self, u, kind, j=0):
        p, s, n = self.p, u % self.slots, self.split[u]
        h = self.held.at[s]
        rc, rx, ry, rx2, ry2, rz = self.buffers
        cs, cr, xs, xr, ys, yr, zs, zr = self.sems
        if kind == "c":
            return remote(h.at[:, :, :, 1 - p.c], rc.at[s], cs.at[s], cr.at[s], p.to_c)
        if kind == "x1":
            return remote(h.at[:, 0:n, 1 - p.x, p.c], rx.at[s, :, 0:n], xs.at[s, 0], xr.at[s, 0], p.to_x)
        if kind == "y1":
            return remote(h.at[p.yo, n:4, :, p.c], ry.at[s, 0:4 - n], ys.at[s, 0], yr.at[s, 0], p.to_y)
        if kind == "y2":
            return remote(h.at[p.yo, 0:n, p.x, p.c], ry2.at[s, 0:n], ys.at[s, 1], yr.at[s, 1], p.to_y)
        if kind == "x2":
            return remote(h.at[p.y, n:4, 1 - p.x, p.c], rx2.at[s, 0:4 - n], xs.at[s, 1], xr.at[s, 1], p.to_x)
        to = lax.rem(p.z + j, 4)
        return remote(h.at[p.y, to, p.x, p.c], rz.at[s, j - 1], zs.at[s, j - 1], zr.at[s, j - 1], p.to_z[j])

    def submit(self, u):
        if u >= self.slots:
            for i in range(6):
                pl.semaphore_wait(self.free.at[i], 1)
        self.go(u, "c")

    def cores(self, u):
        p, h, rc = self.p, self.held.at[u % self.slots], self.buffers[0].at[u % self.slots]
        self.got(u, "c")

        @pl.loop(0, 4)
        def _(z):
            for y in range(2):
                for x in range(2):
                    h[y, z, x, p.c] = h[y, z, x, p.c] + rc[y, z, x]
        self.go(u, "x1")
        self.go(u, "y1")

    def after_x(self, u):
        p, h, rx, n = self.p, self.held.at[u % self.slots], self.buffers[1].at[u % self.slots], self.split[u]
        self.got(u, "x1")
        for y in range(2):
            for z in range(n):
                h[y, z, p.x, p.c] = h[y, z, p.x, p.c] + rx[y, z]
        self.go(u, "y2")

    def after_y(self, u):
        p, h, ry, n = self.p, self.held.at[u % self.slots], self.buffers[2].at[u % self.slots], self.split[u]
        self.got(u, "y1")
        for z in range(n, 4):
            for x in range(2):
                h[p.y, z, x, p.c] = h[p.y, z, x, p.c] + ry[z - n, x]
        self.go(u, "x2")

    def plane(self, u):
        p, h, n = self.p, self.held.at[u % self.slots], self.split[u]
        _, _, _, rx2, ry2, _ = (b.at[u % self.slots] for b in self.buffers)
        self.got(u, "x2")
        self.got(u, "y2")
        for z in range(4):
            h[p.y, z, p.x, p.c] = h[p.y, z, p.x, p.c] + (ry2[z] if z < n else rx2[z - n])
        for j in (1, 2, 3):
            self.go(u, "z", j)

    def line(self, u):
        p, h, rz = self.p, self.held.at[u % self.slots], self.buffers[5].at[u % self.slots]
        for j in (1, 2, 3):
            self.got(u, "z", j)
        f = lambda v: v.astype(F32)
        self.out[u] = f(h[p.y, p.z, p.x, p.c]) + f(rz[0]) + f(rz[1]) + f(rz[2])
        if u + self.slots < self.total:
            for i, device in zip((0, 1, 2, 5, 4, 3), (p.to_c, p.to_x, p.to_y, *p.to_z[1:])):
                pl.semaphore_signal(self.free.at[i], inc=1, device_id=device, device_id_type=MESH)

    def finish(self):
        for u, sent in self.sends.items():
            for args in sent:
                self.copy(u, *args).wait_send()

    @staticmethod
    def scratch(n, part):
        dma = pltpu.SemaphoreType.DMA
        v = lambda *s: pltpu.VMEM((n, *s, 48, part), BF16)
        return [v(2, 4, 2, 2)], [v(2, 4, 2), v(2, 3), v(2, 2), v(2), v(3), v(3), dma((n,)), dma((n,))] + [dma((n, 2))] * 4 + [
            dma((n, 3))] * 2 + [pltpu.SemaphoreType.REGULAR((6,))]


class Total:
    def __init__(self, place, v, got, zall, sems):
        self.p, self.v, self.got, self.zall = place, v, got, zall
        self.send, self.recv = sems
        self.last = []

    def copy(self, i):
        p = self.p
        if i < 3:
            return remote(self.v.at[i], self.got.at[i], self.send.at[i], self.recv.at[i], (p.to_c, p.to_x, p.to_y)[i])
        return remote(self.v.at[3], self.zall.at[p.z], self.send.at[i], self.recv.at[i], p.to_z[i - 2])

    def step(self, i, out=None):
        if 1 <= i <= 3:
            self.copy(i - 1).wait_recv()
            self.v[i] = self.v[i - 1] + self.got[i - 1]
        if i < 3:
            self.copy(i).start()
        elif i == 3:
            for j in (3, 4, 5):
                self.copy(j).start()
            self.zall[self.p.z] = self.v[3]
        else:
            for j in (3, 4, 5):
                self.copy(j).wait_recv()
            z = self.zall
            out[...] = (z[0] + z[1]) + (z[2] + z[3])
            for j in range(6):
                self.copy(j).wait_send()

    @staticmethod
    def scratch(rows):
        dma = pltpu.SemaphoreType.DMA
        v = lambda n: pltpu.VMEM((n, rows, D), F32)
        return [v(4), v(3), v(4), dma((6,)), dma((6,))]


def attend_back(qkv, lse, gc, gqkv, sums, limits, pair):
    y, (qc, kc, vc) = head_pair(pair)
    q2, k2, v2, c2 = qkv[y, :, qc], qkv[y, :, kc], qkv[y, :, vc], gc[y, :, qc]
    bias = key_bias(limits)
    lane = lax.broadcasted_iota(jnp.int32, (S, 128), 1)
    k2t = k2.T
    gq, gk, gv = [], [], []
    for half in range(2):
        qm, km = with_mask(q2, k2, half, bias)
        st = dot(km, qm, NT)
        probs = jnp.exp(st - lse[pair * 2 + half])
        vm = jnp.where((lane // 64) == half, v2, jnp.zeros_like(v2))
        gp = dot(vm, c2, NT)
        prod = probs * gp
        total = jnp.sum(prod, axis=0, keepdims=True)
        gs = (prod - probs * total).astype(BF16)
        gv.append(dot(probs.astype(BF16), c2))
        gk.append(dot(gs, q2))
        gq.append(dot(k2t[64 * half:64 * half + 64], gs))
    pick = lambda v: jnp.where(lane < 64, v[0], v[1])
    gqt = jnp.concatenate(gq, 0).T * 0.125
    gkt = pick(gk) * 0.125
    gvt = pick(gv)
    gqkv[y, :, qc] = gqt.astype(BF16)
    gqkv[y, :, kc] = gkt.astype(BF16)
    gqkv[y, :, vc] = gvt.astype(BF16)
    sums[y, 0, :, qc] = jnp.sum(gqt, axis=0, keepdims=True)
    sums[y, 1, :, qc] = jnp.sum(gvt, axis=0, keepdims=True)


def norm_back(g, rows, gain, n, r):
    v = g[rows, :]
    normed, inverse = n[rows, :], r[rows, 0:1]
    e = v * gain
    gh = inverse * (e - jnp.mean(e, axis=-1, keepdims=True) - normed * jnp.mean(e * normed, axis=-1, keepdims=True))
    add = lambda t: jnp.sum(t, axis=0, keepdims=True)
    return gh, add(v * normed), add(v), add(gh)


BACKWARD = (
    ("SO",), ("n2", 0), ("t", 0), ("SUB", 0), ("t", 1), ("ST1", 0), ("g", 0, 0), ("SUB", 1), ("t", 2), ("ST1", 1),
    ("g", 0, 1), ("SUB", 2), ("t", 3), ("ST1", 2), ("gy", 0), ("ST2Y", 0), ("n1", 0), ("ST2X", 0), ("to", 4),
    ("SUB", 3), ("ST2Y", 1), ("gc", 0), ("ST1", 3), ("a", 0, 0), ("a", 0, 1), ("a", 0, 2), ("ST3", 0), ("a", 0, 3),
    ("ST2X", 1), ("a", 0, 4), ("ST2X", 2), ("ST2Y", 2), ("a", 0, 5), ("ST4", 0), ("tv", 4), ("ST3", 1), ("SUB", 4),
    ("ST2X", 3), ("ST2Y", 3), ("t", 5), ("ST3", 2), ("SUB", 5), ("ST1", 4), ("ST1", 5), ("gx", 0), ("n2", 1),
    ("ST4", 1), ("ST2Y", 4), ("t", 6), ("ST3", 3), ("ST2X", 4), ("ST4", 2), ("t", 7), ("SUB", 7), ("ST2X", 5),
    ("ST2Y", 5), ("g", 1, 0), ("ST1", 7), ("ST3", 4), ("ST4", 3), ("SUB", 6), ("ST1", 6), ("t", 8), ("SUB", 8),
    ("g", 1, 1), ("ST3", 5), ("ST4", 4), ("t", 9), ("ST2Y", 7), ("ST2X", 7), ("gy", 1), ("n1", 1), ("ST2Y", 6),
    ("ST4", 5), ("ST2X", 6), ("E", 0), ("SUB", 9), ("to", 10), ("E", 1), ("gc", 1), ("ST1", 8), ("ST3", 7), ("a", 1, 0),
    ("a", 1, 1), ("ST3", 6), ("E", 2), ("ST1", 9), ("a", 1, 2), ("a", 1, 3), ("E", 3), ("ST2Y", 8), ("a", 1, 4),
    ("ST2X", 8), ("a", 1, 5), ("tv", 10), ("V", 0), ("ST2X", 9), ("V", 1), ("ST4", 6), ("SUB", 10), ("ST2Y", 9),
    ("V", 2), ("ST3", 8), ("ST1", 10), ("t", 11), ("V", 3), ("SUB", 11), ("gx", 1), ("ST1", 11), ("ST2Y", 10),
    ("ST3", 9), ("ST2X", 10), ("ST2X", 11), ("ST3", 10), ("E", 4), ("ST2Y", 11), ("ST4", 9), ("ST3", 11), ("ST4", 8),
    ("ST4", 7), ("ST4", 10), ("V", 4), ("ST4", 11),
)
SPLIT = (3, 2, 2, 2, 2, 2, 2, 2, 2, 2, 2, 2)
SLOTS = 5
PART = UNITS // 2
ROWS = 24


def backward_kernel(fold, layers, w, cotf, outx, glob, lengths, bucket,
                    xr_o, qkv_o, lse_o, ctx_o, n1_o, r1_o, y1r_o, act_o, dg_o, n2_o, r2_o,
                    output, ingrad, shards, vout, vlate,
                    wv, g, gh, n, r, low, act, dg, y1r, ctx, qkv, lse, xr, gc, gqkv, sums,
                    wsem, lsem, esem, *rest):
    p = Place(fold)
    m = p.y
    red = Reduce(p, 6 * layers, SLOTS, SPLIT, rest[0], shards, *rest[1:16])
    early = Total(p, *rest[16:19], rest[19:21])
    late = Total(p, *rest[21:24], rest[24:26])
    limits = bounds(lengths, bucket, m)
    order = [3 * l + t for l in reversed(range(layers)) for t in (2, 1, 0)]
    full = slice(0, UNITS)

    def row(i):
        return glob[i:i + 1, :]

    def weights(i):
        return pltpu.make_async_copy(w.at[order[i]], wv.at[i % 2], wsem.at[i % 2])

    table = {"n2": (n2_o, n), "r2": (r2_o, r), "act": (act_o, act), "dg": (dg_o, dg), "y1r": (y1r_o, y1r),
             "n1": (n1_o, n), "r1": (r1_o, r), "ctx": (ctx_o, ctx), "qkv": (qkv_o, qkv), "lse": (lse_o, lse),
             "xr": (xr_o, xr)}
    loads = {}

    def begin(l, *names):
        for i in names:
            src, dst = table[i]
            loads[i] = pltpu.make_async_copy(src.at[l], dst, lsem.at[list(table).index(i)])
            loads[i].start()

    def need(*names):
        for i in names:
            loads.pop(i).wait()

    def add(line, value):
        early.v[0, line:line + 1, :] = early.v[0, line:line + 1, :] + value

    def norm_stage(l, which):
        base = 12 * (layers - 1 - l)

        @pl.loop(0, 4)
        def _(i):
            rows = at(128 * i, 128)
            v, a, b, c = norm_back(g, rows, row(6 * l + 2 + which), n, r)
            gh[rows, :] = v
            low[rows, :] = v.astype(BF16)
            add(base + which, a)
            add(base + 2 + which, b)
            add(base + 4 + which, c)

    def tiles(u, left, right, start, width, to):
        s = red.slot(u)
        for y in range(2):
            v = dot(left[...], right[y, :, start:start + width], TN).astype(BF16)
            s[y, :, :, :, :, to:to + width] = v.reshape(4, 2, 2, 48, width)

    def norm_two(i):
        l = layers - 1 - i
        need("n2", "r2")
        norm_stage(l, 1)
        begin(l, "n1", "r1")

    def gradient(u):
        l, kind = layers - 1 - u // 6, u % 6
        if kind < 2:
            if kind == 0:
                need("act")
            tiles(u, low, act, PART * kind, PART, 0)
            if kind == 1 and l:
                begin(l - 1, "act")
        elif kind < 4:
            if kind == 2:
                need("y1r")
            tiles(u, y1r, dg, PART * (kind - 2), PART, 0)
        else:
            tiles(u, xr, gqkv, 0, 2 * HALF, 0)

    def gradient_out(u):
        need("ctx")
        tiles(u, low, ctx, 0, HALF, HALF)

    def gradient_value(u):
        need("xr")
        tiles(u, xr, gqkv, 2 * HALF, HALF, 0)

    def units(i, half):
        if half == 0:
            weights(3 * i).wait()
            need("dg")
        wc = wv.at[3 * i % 2]
        for y in range(2):
            cols = slice(PART * half, PART * half + PART)
            gi = dot(low[...], columns(wc, y, cols)) * dg[y, :, cols].astype(F32)
            dg[y, :, cols] = gi.astype(BF16)
            line = 12 * i + 6 + 2 * y + half
            early.v[0, line:line + 1, :] = jnp.sum(gi, axis=0, keepdims=True)
        if half == 1 and 3 * i + 2 < 3 * layers:
            weights(3 * i + 2).start()

    def hidden(i):
        weights(3 * i + 1).wait()
        wb = wv.at[(3 * i + 1) % 2]
        g[...] = gh[...] + dot(dg[0], columns(wb, 0, full), NT) + dot(dg[1], columns(wb, 1, full), NT)
        if 3 * i + 3 < 3 * layers:
            weights(3 * i + 3).start()
        l = layers - 1 - i
        if l:
            begin(l - 1, "dg", "y1r")

    def norm_one(i):
        l = layers - 1 - i
        need("n1", "r1")
        norm_stage(l, 0)
        if l:
            begin(l - 1, "n2", "r2")

    def context(i):
        l = layers - 1 - i
        weights(3 * i + 2).wait()
        wa = wv.at[(3 * i + 2) % 2]
        for y in range(2):
            gc[y] = dot(low[...], columns(wa, y, slice(3 * HALF, 4 * HALF))).astype(BF16)
        if l:
            begin(l - 1, "ctx")
        need("qkv", "lse")

    def attention(i, inside):
        @pl.loop(0, 6)
        def _(j):
            attend_back(qkv, lse, gc, gqkv, sums, limits, j)
            for turn, todo in enumerate(inside):
                if todo:
                    @pl.when(j == turn)
                    def _():
                        for t in todo:
                            steps[t[0]](*t[1:])
        for y in range(2):
            for t in range(2):
                where = slice(HALF * y, HALF * y + HALF)
                if i == layers - 1:
                    late.v[0, t:t + 1, where] = sums[y, t]
                else:
                    early.v[0, 12 * i + 10 + t:12 * i + 11 + t, where] = sums[y, t]

    def state(i):
        l = layers - 1 - i
        wa = wv.at[(3 * i + 2) % 2]
        wqkv = [columns(wa, y, slice(0, 3 * HALF)) for y in range(2)]
        if l:
            g[...] = gh[...] + dot(gqkv[0], wqkv[0], NT) + dot(gqkv[1], wqkv[1], NT)
            begin(l - 1, "qkv", "lse", "xr")
            weights(3 * i + 4).start()
        else:
            for j in range(2):
                rows = at((S // 2) * (1 - m if j == 0 else m), S // 2)
                v = gh[rows, :] + dot(gqkv[0, rows, :], wqkv[0], NT) + dot(gqkv[1, rows, :], wqkv[1], NT)
                low[rows, :] = v.astype(BF16)
                (swap_g if j == 0 else own_g).start()

    steps = {
        "n2": norm_two, "t": gradient, "to": gradient_out, "tv": gradient_value, "g": units, "gy": hidden, "n1": norm_one,
        "gc": context, "gx": state, "SUB": red.submit, "ST1": red.cores, "ST2X": red.after_x, "ST2Y": red.after_y,
        "ST3": red.plane, "ST4": red.line, "E": lambda i: early.step(i, vout), "V": lambda i: late.step(i, vlate),
        "SO": lambda: swap_o.start()}
    own_o = pltpu.make_async_copy(outx.at[m], output.at[m], esem.at[0])
    swap_o = remote(outx.at[1 - m], output.at[m], esem.at[1], esem.at[2], p.to_y)
    half = lambda i: low.at[at((S // 2) * i, S // 2), :]
    own_g = pltpu.make_async_copy(half(m), ingrad.at[m], esem.at[3])
    swap_g = remote(half(1 - m), ingrad.at[m], esem.at[4], esem.at[5], p.to_y)
    top = layers - 1
    cload = pltpu.make_async_copy(cotf, low, esem.at[6])
    cload.start()
    begin(top, "n2", "r2", "act")
    weights(0).start()
    begin(top, "dg", "y1r")
    weights(1).start()
    begin(top, "ctx", "qkv", "lse", "xr")
    early.v[0] = jnp.zeros((ROWS, D), F32)
    late.v[0] = jnp.zeros((8, D), F32)
    cload.wait()
    g[...] = low[...].astype(F32)
    own_o.start()
    p.greet()
    plan = list(BACKWARD)
    while plan:
        t = plan.pop(0)
        if t[0] != "a":
            steps[t[0]](*t[1:])
            continue
        inside = [[] for _ in range(6)]
        while (t[0], t[-1]) != ("a", 5):
            if t[0] == "a":
                turn = t[2]
            else:
                inside[turn].append(t)
            t = plan.pop(0)
        attention(t[1], inside)
    red.finish()
    own_o.wait()
    swap_o.wait()
    own_g.wait()
    swap_g.wait()


def backward(w, cotf, outx, glob, lengths, bucket, saved, layers, fold):
    n = 6 * layers
    dma = pltpu.SemaphoreType.DMA
    shape = jax.ShapeDtypeStruct
    vm = pltpu.VMEM
    first, rest = Reduce.scratch(SLOTS, PART)
    return pl.pallas_call(
        functools.partial(backward_kernel, fold, layers),
        out_shape=[shape((2, S // 2, D), BF16), shape((2, S // 2, D), BF16), shape((n, 48, PART), F32),
                   shape((ROWS, D), F32), shape((8, D), F32)],
        in_specs=[ANY, ANY, ANY, VMEM, SMEM, SMEM] + [ANY] * 11,
        out_specs=[ANY, ANY, VMEM, VMEM, VMEM],
        scratch_shapes=[
            vm((2, 2, 4, 2, 2, 48, UNITS), BF16), vm((S, D), F32), vm((S, D), F32), vm((S, D), F32), vm((S, 128), F32),
            vm((S, D), BF16), vm((2, S, UNITS), BF16), vm((2, S, UNITS), BF16), vm((S, D), BF16),
            vm((2, S, HALF), BF16), vm((2, S, 3 * HALF), BF16), vm((12, 1, S), F32), vm((S, D), BF16), vm((2, S, HALF), BF16),
            vm((2, S, 3 * HALF), BF16), vm((2, 2, 1, HALF), F32),
            dma((2,)), dma((11,)), dma((7,)), *first, *rest, *Total.scratch(ROWS), *Total.scratch(8)],
        compiler_params=pltpu.CompilerParams(collective_id=2, has_side_effects=True, vmem_limit_bytes=62 * 2**20),
    )(w, cotf, outx, glob, lengths, bucket, *saved)


def pack(w_qkv, w_out, w_up, w_down):
    parts = []
    for l in range(w_qkv.shape[0]):
        parts.append(jnp.concatenate([w_qkv[l, 0], w_qkv[l, 1], w_qkv[l, 2], w_out[l].T], 1))
        parts.append(w_up[l])
        parts.append(w_down[l].T)
    return jnp.stack(parts)


def per_device(layer_input, cotangent, lengths, bucket, w_qkv, bias_qv, w_out, bias_out, ln_gain, ln_bias, w_up, bias_up, w_down):
    layers = w_qkv.shape[0]
    fold = lax.axis_size("dp") // GROUPS
    members = [[g * fold + i for i in range(fold)] for g in range(GROUPS)]
    packed = pack(w_qkv, w_out, w_up, w_down)
    if fold > 1:
        packed = lax.all_gather(packed, "dp", axis=1, tiled=True, axis_index_groups=members)
    qv = jnp.pad(bias_qv.reshape(layers, 2 * HALF), ((0, 0), (0, UNITS - 2 * HALF)))
    vec = jnp.concatenate([bias_up, qv], 0).astype(F32)
    vec = jnp.pad(vec, ((0, 8 - vec.shape[0]), (0, 0)))
    glob = jnp.concatenate([bias_out, ln_gain, ln_bias], 1).astype(F32).reshape(6 * layers, D)
    glob = jnp.pad(glob, ((0, 16 - 6 * layers), (0, 0)))
    w, cotf, out, *saved = forward(packed, layer_input, cotangent, vec, glob, lengths, bucket, layers, fold)
    output, ingrad, shards, early, late = backward(
        w, cotf.reshape(S, D), out.reshape(2, S // 2, D), glob, lengths, bucket, saved, layers, fold)
    if fold > 1:
        shards = lax.psum_scatter(shards, "dp", scatter_dimension=1, tiled=True, axis_index_groups=members)
        early, late = lax.psum((early, late), "dp", axis_index_groups=members)
    rows = shards.shape[1]
    part = lax.axis_index("mp")
    shards = jnp.flip(shards.reshape(layers, 6, rows, PART), 0)
    down, up, vo, qk = shards[:, 0:2], shards[:, 2:4], shards[:, 4], shards[:, 5]
    grad_qkv = jnp.stack([qk[..., :HALF], qk[..., HALF:], vo[..., :HALF]], 1)
    grad_out = vo[..., HALF:].transpose(0, 2, 1)
    grad_up = up.transpose(0, 2, 1, 3).reshape(layers, rows, UNITS)
    grad_down = down.transpose(0, 1, 3, 2).reshape(layers, UNITS, rows)
    vecs = jnp.flip(early.reshape(layers, 12, D), 0)
    gain, shift, bias = vecs[:, 0:2], vecs[:, 2:4], vecs[:, 4:6]
    grad_bias_up = lax.dynamic_slice_in_dim(vecs[:, 6:10].reshape(layers, 2, UNITS), part, 1, 1)[:, 0]
    qv = jnp.concatenate([late[None, 0:2], vecs[1:, 10:12]], 0)
    qv = lax.dynamic_slice_in_dim(qv, part * HALF, HALF, 2)
    return output, ingrad, grad_qkv, qv, grad_out, bias, gain, shift, grad_up, grad_bias_up, grad_down


def solution(mesh):
    in_specs = (
        P("dp", "mp", None),
        P("dp", "mp", None),
        P("dp", None),
        P("dp"),
        P(None, None, "dp", "mp"),
        P(None, None, "mp"),
        P(None, "mp", "dp"),
        P(),
        P(),
        P(),
        P(None, "dp", "mp"),
        P(None, "mp"),
        P(None, "mp", "dp"),
    )
    out_specs = (
        P("dp", "mp", None),
        P("dp", "mp", None),
        P(None, None, "dp", "mp"),
        P(None, None, "mp"),
        P(None, "mp", "dp"),
        P(),
        P(),
        P(),
        P(None, "dp", "mp"),
        P(None, "mp"),
        P(None, "mp", "dp"),
    )
    return jax.shard_map(
        per_device, mesh=mesh, in_specs=in_specs, out_specs=out_specs, check_vma=False
    )
```

```python
import functools

import jax
import jax.numpy as jnp
from jax import lax
from jax.experimental import pallas as pl
from jax.experimental.pallas import tpu as pltpu
from jax.sharding import PartitionSpec as P

F32 = jnp.float32
BF16 = jnp.bfloat16
S = 512
D = 768
HALF = 384
UNITS = 1536
GROUPS = 16
EPS = 1e-12
MESH = pl.DeviceIdType.MESH
NN = (((1,), (0,)), ((), ()))
NT = (((1,), (1,)), ((), ()))
TN = (((0,), (0,)), ((), ()))
ANY = pl.BlockSpec(memory_space=pl.ANY)
VMEM = pl.BlockSpec(memory_space=pltpu.VMEM)
SMEM = pl.BlockSpec(memory_space=pltpu.SMEM)


def dot(a, b, dims=NN):
    return lax.dot_general(a, b, dims, preferred_element_type=F32)


def at(start, size):
    return pl.ds(pl.multiple_of(start, size), size)


def remote(src, dst, send_sem, recv_sem, device):
    return pltpu.make_async_remote_copy(
        src_ref=src, dst_ref=dst, send_sem=send_sem, recv_sem=recv_sem,
        device_id=device, device_id_type=MESH)


class Place:
    def __init__(self, fold):
        d = lax.axis_index("dp")
        self.fold = fold
        self.member = lax.rem(d, fold) if fold > 1 else 0
        g = d // fold if fold > 1 else d
        self.z = g // 4
        self.xc = lax.rem(g, 4)
        self.x = self.xc // 2
        self.c = lax.rem(self.xc, 2)
        self.y = lax.axis_index("mp")
        self.xo = (1 - self.x) * 2 + self.c
        self.co = self.x * 2 + (1 - self.c)
        self.yo = 1 - self.y
        self.to_z = [None] + [self.device(lax.rem(self.z + j, 4), self.xc, self.y) for j in (1, 2, 3)]
        self.to_x = self.device(self.z, self.xo, self.y)
        self.to_y = self.device(self.z, self.xc, self.yo)
        self.to_c = self.device(self.z, self.co, self.y)

    def device(self, z, xc, y):
        return {"dp": (z * 4 + xc) * self.fold + self.member, "mp": y}

    def greet(self):
        for device in (*self.to_z[1:], self.to_x, self.to_y, self.to_c):
            pl.semaphore_signal(pltpu.get_barrier_semaphore(), inc=1, device_id=device, device_id_type=MESH)

    def greeted(self):
        pl.semaphore_wait(pltpu.get_barrier_semaphore(), 6)


class Gather:
    def __init__(self, place, packed, w, turned, via_x, lsem, zs, zr, xs, xr, ys, yr, fs, fr, cs, cr, qs, qr):
        self.p, self.packed, self.w, self.turned, self.via_x = place, packed, w, turned, via_x
        self.sems = dict(z=(zs, zr), x=(xs, xr), y=(ys, yr), f=(fs, fr), c=(cs, cr), q=(qs, qr))
        self.lsem = lsem
        z = place.z
        low = z < 2
        self.order = [z, jnp.where(low, 1 - z, 5 - z), jnp.where(low, 2, 1), jnp.where(low, 3, 0)]
        self.inner = (z == 1) | (z == 2)
        self.partner = place.device(z + 1 - 2 * lax.rem(z, 2), place.xc, place.y)
        self.across = place.device(3 - z, place.xc, place.y)
        self.sends, self.inner_sends, self.waited = [], [], set()

    def go(self, make):
        make().start()
        self.sends.append(make)

    def go_inner(self, make):
        pl.when(self.inner)(lambda: make().start())
        self.inner_sends.append(make)

    def copy(self, kind, k, i, j, src, dst, device):
        send, recv = self.sems[kind]
        return remote(src, dst, send.at[k, i], recv.at[k, j], device)

    def block(self, k, j=0, other_x=False, other_y=False):
        p = self.p
        return self.w.at[k, p.yo if other_y else p.y, self.order[j], 1 - p.x if other_x else p.x, p.c]

    def source(self, k, j):
        return self.packed.at[k] if j == 0 else self.block(k, j)

    def own(self, k):
        return pltpu.make_async_copy(self.packed.at[k], self.block(k), self.lsem.at[k])

    def load(self, k, j):
        return self.w.at[k, :, self.order[j], :, self.p.c] if k == self.turned else self.block(k, j)

    def line(self, k, i):
        j, slot, device = ((0, 1, self.partner), (0, 2, self.across), (1, 3, self.across), (2, 2, self.partner),
                           (3, 3, self.partner))[i]
        src = dst = self.load(k, j)
        if j == 0 and k != self.turned:
            src = self.packed.at[k]
        return self.copy("z", k, i, slot, src, dst, device)

    def line_start(self, k):
        self.go(lambda: self.line(k, 0))
        self.go_inner(lambda: self.line(k, 1))

    def line_wait(self, k, j):
        self.copy("z", k, 0, j, self.load(k, j), self.load(k, j), self.partner).wait_recv()
        self.go_inner(lambda: self.line(k, j + 1))

    def to_x(self, k, j):
        return self.copy("x", k, j, j, self.source(k, j), self.block(k, j), self.p.to_x)

    def to_y(self, k, j):
        return self.copy("y", k, j, j, self.source(k, j), self.block(k, j), self.p.to_y)

    def diagonal(self, k, j):
        x = self.via_x(k, j)
        block = self.block(k, j, other_x=not x, other_y=x)
        return self.copy("f", k, j, j, block, block, self.p.to_x if x else self.p.to_y)

    def to_core(self, k, i):
        p = self.p
        if k == self.turned:
            block = self.load(k, i)
        else:
            y, x = ((p.y, p.x), (p.y, 1 - p.x), (p.yo, p.x), (p.yo, 1 - p.x))[i]
            block = self.w.at[k, y, :, x, p.c]
        return self.copy("c", k, i, i, block, block, p.to_c)

    def start(self, k):
        self.own(k).start()
        self.line_start(k)
        self.go(lambda: self.to_x(k, 0))
        self.go(lambda: self.to_y(k, 0))

    def spread(self, k, j):
        self.go(lambda: self.to_x(k, j))
        self.go(lambda: self.to_y(k, j))
        if j == 3:
            self.own(k).wait()
            self.go(lambda: self.to_core(k, 0))

    def seen(self, kind, k, j):
        if (kind, k, j) not in self.waited:
            self.waited.add((kind, k, j))
            (self.to_x if kind == "x" else self.to_y)(k, j).wait_recv()

    def forward(self, k, j):
        self.seen("y" if self.via_x(k, j) else "x", k, j)
        self.go(lambda: self.diagonal(k, j))

    def side(self, k, kind):
        for j in range(4):
            self.seen(kind, k, j)
        self.go(lambda: self.to_core(k, 1 if kind == "x" else 2))

    def share(self, k):
        for j in range(4):
            self.diagonal(k, j).wait_recv()
        self.go(lambda: self.to_core(k, 3))

    def arrive(self, k):
        for i in range(4):
            self.to_core(k, i).wait_recv()

    def turned_copy(self, i):
        p, k = self.p, self.turned
        if i < 2:
            return self.copy("q", 0, i, i, self.packed.at[k], self.block(k), (p.to_x, p.to_y)[i])
        half = slice(UNITS // 2 * (i - 2), UNITS // 2 * (i - 1))
        block = self.block(k, other_x=i == 2, other_y=i == 3).at[:, half]
        return self.copy("q", 0, i, i, block, block, (p.to_y, p.to_x)[i - 2])

    def turned_start(self):
        self.own(self.turned).start()
        self.go(lambda: self.turned_copy(0))
        self.go(lambda: self.turned_copy(1))

    def turned_forward(self, i):
        self.turned_copy(i).wait_recv()
        self.go(lambda: self.turned_copy(2 + i))

    def turned_line(self, j):
        k = self.turned
        if j == 0:
            self.own(k).wait()
            self.turned_copy(2).wait_recv()
            self.turned_copy(3).wait_recv()
            self.line_start(k)
        else:
            self.line_wait(k, j)
        self.go(lambda: self.to_core(k, j))

    def finish(self):
        for make in self.sends:
            make().wait_send()
        for make in self.inner_sends:
            pl.when(self.inner)(lambda: make().wait_send())

    @staticmethod
    def scratch(n):
        dma = pltpu.SemaphoreType.DMA
        return [dma((n,)), dma((n, 5)), dma((n, 4))] + [dma((n, 4))] * 8 + [dma((1, 4))] * 2


def columns(w, y, cols):
    v = w[y, :, :, :, :, cols]
    return v.reshape(D, v.shape[-1])


def bounds(lengths, bucket, m):
    l0, l1, one = lengths[m, 0], lengths[m, 1], bucket[m] == 1
    half = S // 2
    return jnp.where(one, l0 + l1, l0), jnp.where(one, 0, half), jnp.where(one, l0 + l1, half + l1)


def key_bias(limits):
    first_end, second_start, second_end = limits
    k = lax.broadcasted_iota(jnp.int32, (S, 128), 0)
    lo = jnp.where(k < first_end, 0.0, -1e9)
    hi = jnp.where((k >= second_start) & (k < second_end), 0.0, -1e9)
    return lo, hi


def with_mask(q2, k2, half, bias):
    lane = lax.broadcasted_iota(jnp.int32, (S, 128), 1)
    low = lax.broadcasted_iota(jnp.int32, (S, 128), 0) < S // 2
    own = (lane // 64) == half
    o = 64 * (1 - half)
    one = lambda pick: jnp.where(pick, 1.0, 0.0)
    qa = jnp.where(lane == o, one(low), jnp.where(lane == o + 1, one(~low), 0.0))
    ka = jnp.where(lane == o, bias[0], jnp.where(lane == o + 1, bias[1], 0.0))
    qm = jnp.where(own, q2.astype(F32) * 0.125, qa).astype(BF16)
    km = jnp.where(own, k2.astype(F32), ka).astype(BF16)
    return qm, km


def head_pair(pair):
    y, r = pair // 3, lax.rem(pair, 3)
    return y, [at(o + 128 * r, 128) for o in (0, HALF, 2 * HALF)]


def attend(qkv, ctx, lse, limits, pair):
    y, (qc, kc, vc) = head_pair(pair)
    q2, k2, v2 = qkv[y, :, qc], qkv[y, :, kc], qkv[y, :, vc]
    bias = key_bias(limits)
    v2t = v2.T
    parts = []
    for half in range(2):
        qm, km = with_mask(q2, k2, half, bias)
        st = dot(km, qm, NT)
        top = jnp.max(st, axis=0, keepdims=True)
        e = jnp.exp(st - top)
        total = jnp.sum(e, axis=0, keepdims=True)
        lse[pair * 2 + half] = top + jnp.log(total)
        ct = dot(v2t[64 * half:64 * half + 64], e.astype(BF16))
        parts.append(ct * (1.0 / total))
    ctx[y, :, qc] = jnp.concatenate(parts, 0).T.astype(BF16)


def normalize(h, rows, gain, shift, n, r):
    v = h[rows, :]
    c = v - jnp.mean(v, axis=-1, keepdims=True)
    inverse = lax.rsqrt(jnp.mean(c * c, axis=-1, keepdims=True) + EPS)
    normed = c * inverse
    n[rows, :] = normed
    r[rows, :] = jnp.broadcast_to(inverse, (inverse.shape[0], 128))
    return normed * gain + shift


def gelu_parts(u):
    cdf = 0.5 * (1.0 + lax.erf(u * 0.7071067811865476))
    return u * cdf, cdf + u * (jnp.exp(-0.5 * u * u) * 0.3989422804014327)


PLAN = (
    ("S", 0), ("TS",), ("S", 1), ("S", 2), ("L", 0, 1), ("L", 1, 1), ("XY", 0, 1), ("L", 0, 2), ("L", 2, 1), ("S", 4),
    ("TF", 0), ("L", 0, 3), ("TF", 1), ("XY", 0, 3), ("L", 1, 2), ("F", 0, 0), ("XY", 0, 2), ("XY", 1, 1), ("F", 0, 1),
    ("L", 1, 3), ("TL", 0), ("F", 0, 3), ("F", 0, 2), ("XY", 1, 3), ("SX",), ("XY", 1, 2), ("S", 5), ("L", 4, 1),
    ("L", 2, 2), ("XY", 2, 1), ("XY", 2, 2), ("F", 4, 0), ("SH", 0), ("CX", 0), ("CY", 0), ("F", 1, 0), ("TL", 1),
    ("L", 2, 3), ("F", 1, 3), ("L", 5, 1), ("F", 1, 1), ("TL", 2), ("AR", 0), ("XY", 2, 3), ("XY", 5, 1), ("F", 1, 2),
    ("CY", 1), ("F", 2, 0), ("CX", 1), ("F", 2, 1), ("TL", 3), ("XY", 4, 1), ("CX", 2), ("AR", 3), ("F", 2, 3),
    ("L", 4, 2), ("SH", 1), ("L", 4, 3), ("F", 2, 2), ("XY", 4, 2), ("L", 5, 2), ("F", 4, 1), ("XY", 5, 2),
    ("XY", 4, 3), ("AR", 1), ("CY", 2), ("SH", 2), ("AR", 2), ("L", 5, 3), ("F", 4, 2), ("XY", 5, 3), ("F", 4, 3),
    ("F", 5, 0), ("CX", 4), ("CY", 4), ("CX", 5), ("F", 5, 2), ("F", 5, 1), ("SH", 4), ("F", 5, 3), ("AR", 4),
    ("CY", 5), ("SC",), ("SH", 5), ("AR", 5),
)
TURNED = 3
VIA_X = ((1, 1, 1, 0), (1, 0, 1, 1), (0, 1, 1, 0), (0, 1, 1, 0), (0, 1, 0, 1), (1, 0, 0, 1))


def forward_kernel(fold, layers, packed, xin, cot, vec, glob, lengths, bucket,
                   w, cotf, out, xr_o, qkv_o, lse_o, ctx_o, n1_o, r1_o, y1r_o, act_o, dg_o, n2_o, r2_o,
                   wv, xh, vecf, x, xr, qkv, lse, ctx, h, n1, r1, y1, y1r, act, dg, n2, r2,
                   wsem, esem, ssem, *gsems):
    p = Place(fold)
    m = p.y
    parts = 3 * layers
    assert parts == len(VIA_X)
    g = Gather(p, packed, w, TURNED, lambda k, j: VIA_X[k][j], *gsems)
    saves = {}
    names = ("xr", "qkv", "lse", "ctx", "n1", "r1", "y1r", "act", "dg", "n2", "r2")

    def load(k):
        return pltpu.make_async_copy(w.at[k], wv.at[k], wsem.at[k])

    def save(i, l, src, dst):
        if i in saves:
            saves.pop(i).wait()
        saves[i] = pltpu.make_async_copy(src, dst.at[l], ssem.at[names.index(i), l])
        saves[i].start()

    def before(*names):
        for i in names:
            if i in saves:
                saves.pop(i).wait()

    own_x = pltpu.make_async_copy(xin.at[m], xh.at[m], esem.at[0])
    swap_x = remote(xin.at[1 - m], xh.at[m], esem.at[1], esem.at[2], p.to_y)
    own_c = pltpu.make_async_copy(cot.at[m], cotf.at[m], esem.at[3])
    swap_c = remote(cot.at[1 - m], cotf.at[m], esem.at[4], esem.at[5], p.to_y)
    own_v = pltpu.make_async_copy(vec, vecf.at[m], esem.at[6])
    swap_v = remote(vec, vecf.at[m], esem.at[7], esem.at[8], p.to_y)
    limits = bounds(lengths, bucket, m)

    def row(i):
        return glob[i:i + 1, :]

    def stage_a(l, y):
        wa = wv.at[3 * l]
        if y == 0:
            before("xr", "qkv", "lse", "ctx", "n1", "r1", "y1r")
            save("xr", l, xr, xr_o)
        for t in range(3):
            cols = slice(HALF * t, HALF * t + HALF)
            v = dot(xr[...], columns(wa, y, cols))
            if t != 1:
                v = v + vecf[y, 2 + l:3 + l, HALF * (t // 2):HALF * (t // 2) + HALF]
            qkv[y, :, cols] = v.astype(BF16)
        if y == 1:
            save("qkv", l, qkv, qkv_o)

    def stage_out(l):
        wa = wv.at[3 * l]
        save("lse", l, lse, lse_o)
        save("ctx", l, ctx, ctx_o)
        wo = [columns(wa, y, slice(3 * HALF, 4 * HALF)) for y in range(2)]
        h[...] = x[...] + row(6 * l) + dot(ctx[0], wo[0], NT) + dot(ctx[1], wo[1], NT)

        @pl.loop(0, 2)
        def _(i):
            rows = at(256 * i, 256)
            o = normalize(h, rows, row(6 * l + 2), row(6 * l + 4), n1, r1)
            y1[rows, :] = o
            y1r[rows, :] = o.astype(BF16)
        save("n1", l, n1, n1_o)
        save("r1", l, r1, r1_o)
        save("y1r", l, y1r, y1r_o)

    def stage_b(l, y, i):
        wb = wv.at[3 * l + 1]
        if y == 0 and i == 0:
            before("act", "dg", "n2", "r2")
        cols = slice(768 * i, 768 * i + 768)
        u = dot(y1r[...], columns(wb, y, cols)) + vecf[y, l:l + 1, cols]
        a, d = gelu_parts(u)
        act[y, :, cols] = a.astype(BF16)
        dg[y, :, cols] = d.astype(BF16)
        if y == 1 and i == 1:
            save("act", l, act, act_o)
            save("dg", l, dg, dg_o)

    def stage_c(l):
        wc = wv.at[3 * l + 2]
        before("xr")
        full = slice(0, UNITS)
        h[...] = (y1[...] + row(6 * l + 1) + dot(act[0], columns(wc, 0, full), NT)
                  + dot(act[1], columns(wc, 1, full), NT))

        @pl.loop(0, 2)
        def _(i):
            rows = at(256 * i, 256)
            o = normalize(h, rows, row(6 * l + 3), row(6 * l + 5), n2, r2)
            x[rows, :] = o
            xr[rows, :] = o.astype(BF16)
        save("n2", l, n2, n2_o)
        save("r2", l, r2, r2_o)

    pending, here, used = [], set(), [0]

    def ready(k):
        l, kind = k // 3, k % 3
        pending.append(lambda: load(k).wait())
        if k == 0:
            pending.append(first)
        if kind == 0:
            pending.append(lambda: stage_a(l, 0))
            pending.append(lambda: stage_a(l, 1))
            pending.append((6, lambda j: attend(qkv, ctx, lse, limits, j)))
            pending.append(lambda: stage_out(l))
        elif kind == 1:
            for y in range(2):
                for i in range(2):
                    pending.append(lambda y=y, i=i: stage_b(l, y, i))
        else:
            pending.append(lambda: stage_c(l))

    def first():
        own_x.wait()
        swap_x.wait()
        own_v.wait()
        swap_v.wait()
        for i in range(2):
            rows = slice(256 * i, 256 * i + 256)
            xr[rows, :] = xh[i]
            x[rows, :] = xh[i].astype(F32)

    def run(steps):
        steps = list(steps)
        while steps or pending:
            piece = pending.pop(0) if pending else None
            if isinstance(piece, tuple):
                inside, steps = steps[:piece[0]], steps[piece[0]:]

                @pl.loop(0, piece[0])
                def _(j):
                    piece[1](j)
                    for i, step in enumerate(inside):
                        pl.when(j == i)(step)
            else:
                if piece is not None:
                    piece()
                if steps:
                    steps.pop(0)()

    def arrived(k):
        g.arrive(k)
        load(k).start()
        here.add(k)
        while used[0] in here:
            ready(used[0])
            used[0] += 1

    steps = {
        "S": g.start, "L": g.line_wait, "XY": g.spread, "F": g.forward, "CX": lambda k: g.side(k, "x"),
        "CY": lambda k: g.side(k, "y"), "SH": g.share, "AR": arrived, "TS": g.turned_start, "TF": g.turned_forward,
        "TL": g.turned_line, "SX": lambda: (swap_v.start(), swap_x.start()), "SC": lambda: swap_c.start()}
    plan = [lambda t=t: steps[t[0]](*t[1:]) for t in PLAN]

    p.greet()
    own_x.start()
    own_v.start()
    own_c.start()
    p.greeted()
    run(plan)
    own_c.wait()
    swap_c.wait()
    last = pltpu.make_async_copy(xr, out, esem.at[9])
    last.start()
    g.finish()
    for copy in saves.values():
        copy.wait()
    last.wait()


def forward(packed, xin, cot, vec, glob, lengths, bucket, layers, fold):
    n = 3 * layers
    dma = pltpu.SemaphoreType.DMA
    saved = [((S, D), BF16), ((2, S, 3 * HALF), BF16), ((12, 1, S), F32), ((2, S, HALF), BF16), ((S, D), F32), ((S, 128), F32),
             ((S, D), BF16), ((2, S, UNITS), BF16), ((2, S, UNITS), BF16), ((S, D), F32), ((S, 128), F32)]
    shape = jax.ShapeDtypeStruct
    vm = pltpu.VMEM
    return pl.pallas_call(
        functools.partial(forward_kernel, fold, layers),
        out_shape=[shape((n, 2, 4, 2, 2, 48, UNITS), BF16), shape((2, S // 2, D), BF16), shape((S, D), BF16)]
        + [shape((layers, *s), d) for s, d in saved],
        in_specs=[ANY, ANY, ANY, ANY, VMEM, SMEM, SMEM],
        out_specs=[ANY] * (3 + len(saved)),
        scratch_shapes=[
            vm((n, 2, 4, 2, 2, 48, UNITS), BF16), vm((2, S // 2, D), BF16), vm((2, 8, UNITS), F32), vm((S, D), F32),
            vm((S, D), BF16), vm((2, S, 3 * HALF), BF16), vm((12, 1, S), F32), vm((2, S, HALF), BF16),
            vm((S, D), F32), vm((S, D), F32), vm((S, 128), F32), vm((S, D), F32), vm((S, D), BF16),
            vm((2, S, UNITS), BF16), vm((2, S, UNITS), BF16), vm((S, D), F32), vm((S, 128), F32),
            dma((n,)), dma((10,)), dma((11, layers)), *Gather.scratch(n)],
        compiler_params=pltpu.CompilerParams(collective_id=1, has_side_effects=True, vmem_limit_bytes=60 * 2**20),
    )(packed, xin, cot, vec, glob, lengths, bucket)


class Reduce:
    def __init__(self, place, total, slots, split, held, out, rc, rx, ry, rx2, ry2, rz, cs, cr, xs, xr, ys, yr, zs, zr, free):
        self.p, self.total, self.slots, self.split = place, total, slots, split
        self.held, self.out, self.buffers = held, out, (rc, rx, ry, rx2, ry2, rz)
        self.sems = (cs, cr, xs, xr, ys, yr, zs, zr)
        self.free = free
        self.sends = {}

    def slot(self, u):
        for args in self.sends.pop(u - self.slots, ()):
            self.copy(u - self.slots, *args).wait_send()
        return self.held.at[u % self.slots]

    def go(self, u, *args):
        self.copy(u, *args).start()
        self.sends.setdefault(u, []).append(args)

    def got(self, u, *args):
        self.copy(u, *args).wait_recv()

    def copy(self, u, kind, j=0):
        p, s, n = self.p, u % self.slots, self.split[u]
        h = self.held.at[s]
        rc, rx, ry, rx2, ry2, rz = self.buffers
        cs, cr, xs, xr, ys, yr, zs, zr = self.sems
        if kind == "c":
            return remote(h.at[:, :, :, 1 - p.c], rc.at[s], cs.at[s], cr.at[s], p.to_c)
        if kind == "x1":
            return remote(h.at[:, 0:n, 1 - p.x, p.c], rx.at[s, :, 0:n], xs.at[s, 0], xr.at[s, 0], p.to_x)
        if kind == "y1":
            return remote(h.at[p.yo, n:4, :, p.c], ry.at[s, 0:4 - n], ys.at[s, 0], yr.at[s, 0], p.to_y)
        if kind == "y2":
            return remote(h.at[p.yo, 0:n, p.x, p.c], ry2.at[s, 0:n], ys.at[s, 1], yr.at[s, 1], p.to_y)
        if kind == "x2":
            return remote(h.at[p.y, n:4, 1 - p.x, p.c], rx2.at[s, 0:4 - n], xs.at[s, 1], xr.at[s, 1], p.to_x)
        to = lax.rem(p.z + j, 4)
        return remote(h.at[p.y, to, p.x, p.c], rz.at[s, j - 1], zs.at[s, j - 1], zr.at[s, j - 1], p.to_z[j])

    def submit(self, u):
        if u >= self.slots:
            for i in range(6):
                pl.semaphore_wait(self.free.at[i], 1)
        self.go(u, "c")

    def cores(self, u):
        p, h, rc = self.p, self.held.at[u % self.slots], self.buffers[0].at[u % self.slots]
        self.got(u, "c")

        @pl.loop(0, 4)
        def _(z):
            for y in range(2):
                for x in range(2):
                    h[y, z, x, p.c] = h[y, z, x, p.c] + rc[y, z, x]
        self.go(u, "x1")
        self.go(u, "y1")

    def after_x(self, u):
        p, h, rx, n = self.p, self.held.at[u % self.slots], self.buffers[1].at[u % self.slots], self.split[u]
        self.got(u, "x1")
        for y in range(2):
            for z in range(n):
                h[y, z, p.x, p.c] = h[y, z, p.x, p.c] + rx[y, z]
        self.go(u, "y2")

    def after_y(self, u):
        p, h, ry, n = self.p, self.held.at[u % self.slots], self.buffers[2].at[u % self.slots], self.split[u]
        self.got(u, "y1")
        for z in range(n, 4):
            for x in range(2):
                h[p.y, z, x, p.c] = h[p.y, z, x, p.c] + ry[z - n, x]
        self.go(u, "x2")

    def plane(self, u):
        p, h, n = self.p, self.held.at[u % self.slots], self.split[u]
        _, _, _, rx2, ry2, _ = (b.at[u % self.slots] for b in self.buffers)
        self.got(u, "x2")
        self.got(u, "y2")
        for z in range(4):
            h[p.y, z, p.x, p.c] = h[p.y, z, p.x, p.c] + (ry2[z] if z < n else rx2[z - n])
        for j in (1, 2, 3):
            self.go(u, "z", j)

    def line(self, u):
        p, h, rz = self.p, self.held.at[u % self.slots], self.buffers[5].at[u % self.slots]
        for j in (1, 2, 3):
            self.got(u, "z", j)
        f = lambda v: v.astype(F32)
        self.out[u] = f(h[p.y, p.z, p.x, p.c]) + f(rz[0]) + f(rz[1]) + f(rz[2])
        if u + self.slots < self.total:
            for i, device in zip((0, 1, 2, 5, 4, 3), (p.to_c, p.to_x, p.to_y, *p.to_z[1:])):
                pl.semaphore_signal(self.free.at[i], inc=1, device_id=device, device_id_type=MESH)

    def finish(self):
        for u, sent in self.sends.items():
            for args in sent:
                self.copy(u, *args).wait_send()

    @staticmethod
    def scratch(n, part):
        dma = pltpu.SemaphoreType.DMA
        v = lambda *s: pltpu.VMEM((n, *s, 48, part), BF16)
        return [v(2, 4, 2, 2)], [v(2, 4, 2), v(2, 3), v(2, 2), v(2), v(3), v(3), dma((n,)), dma((n,))] + [dma((n, 2))] * 4 + [
            dma((n, 3))] * 2 + [pltpu.SemaphoreType.REGULAR((6,))]


class Total:
    def __init__(self, place, v, got, zall, sems):
        self.p, self.v, self.got, self.zall = place, v, got, zall
        self.send, self.recv = sems
        self.last = []

    def copy(self, i):
        p = self.p
        if i < 3:
            return remote(self.v.at[i], self.got.at[i], self.send.at[i], self.recv.at[i], (p.to_c, p.to_x, p.to_y)[i])
        return remote(self.v.at[3], self.zall.at[p.z], self.send.at[i], self.recv.at[i], p.to_z[i - 2])

    def step(self, i, out=None):
        if 1 <= i <= 3:
            self.copy(i - 1).wait_recv()
            self.v[i] = self.v[i - 1] + self.got[i - 1]
        if i < 3:
            self.copy(i).start()
        elif i == 3:
            for j in (3, 4, 5):
                self.copy(j).start()
            self.zall[self.p.z] = self.v[3]
        else:
            for j in (3, 4, 5):
                self.copy(j).wait_recv()
            z = self.zall
            out[...] = (z[0] + z[1]) + (z[2] + z[3])
            for j in range(6):
                self.copy(j).wait_send()

    @staticmethod
    def scratch(rows):
        dma = pltpu.SemaphoreType.DMA
        v = lambda n: pltpu.VMEM((n, rows, D), F32)
        return [v(4), v(3), v(4), dma((6,)), dma((6,))]


def attend_back(qkv, lse, gc, gqkv, sums, limits, pair):
    y, (qc, kc, vc) = head_pair(pair)
    q2, k2, v2, c2 = qkv[y, :, qc], qkv[y, :, kc], qkv[y, :, vc], gc[y, :, qc]
    bias = key_bias(limits)
    lane = lax.broadcasted_iota(jnp.int32, (S, 128), 1)
    k2t = k2.T
    gq, gk, gv = [], [], []
    for half in range(2):
        qm, km = with_mask(q2, k2, half, bias)
        st = dot(km, qm, NT)
        probs = jnp.exp(st - lse[pair * 2 + half])
        vm = jnp.where((lane // 64) == half, v2, jnp.zeros_like(v2))
        gp = dot(vm, c2, NT)
        prod = probs * gp
        total = jnp.sum(prod, axis=0, keepdims=True)
        gs = (prod - probs * total).astype(BF16)
        gv.append(dot(probs.astype(BF16), c2))
        gk.append(dot(gs, q2))
        gq.append(dot(k2t[64 * half:64 * half + 64], gs))
    pick = lambda v: jnp.where(lane < 64, v[0], v[1])
    gqt = jnp.concatenate(gq, 0).T * 0.125
    gkt = pick(gk) * 0.125
    gvt = pick(gv)
    gqkv[y, :, qc] = gqt.astype(BF16)
    gqkv[y, :, kc] = gkt.astype(BF16)
    gqkv[y, :, vc] = gvt.astype(BF16)
    sums[y, 0, :, qc] = jnp.sum(gqt, axis=0, keepdims=True)
    sums[y, 1, :, qc] = jnp.sum(gvt, axis=0, keepdims=True)


def norm_back(g, rows, gain, n, r):
    v = g[rows, :]
    normed, inverse = n[rows, :], r[rows, 0:1]
    e = v * gain
    gh = inverse * (e - jnp.mean(e, axis=-1, keepdims=True) - normed * jnp.mean(e * normed, axis=-1, keepdims=True))
    add = lambda t: jnp.sum(t, axis=0, keepdims=True)
    return gh, add(v * normed), add(v), add(gh)


BACKWARD = (
    ("SO",), ("n2", 0), ("t", 0), ("SUB", 0), ("t", 1), ("SUB", 1), ("ST1", 0), ("g", 0, 0), ("ST1", 1), ("t", 2),
    ("SUB", 2), ("g", 0, 1), ("t", 3), ("ST1", 2), ("gy", 0), ("n1", 0), ("ST2X", 0), ("to", 4), ("gc", 0), ("a", 0, 0),
    ("SUB", 3), ("ST2Y", 0), ("a", 0, 1), ("ST1", 3), ("a", 0, 2), ("ST2Y", 1), ("ST2X", 1), ("ST3", 0), ("a", 0, 3),
    ("a", 0, 4), ("ST2Y", 2), ("ST2X", 2), ("a", 0, 5), ("tv", 4), ("ST3", 1), ("ST2X", 3), ("ST2Y", 3), ("SUB", 4),
    ("ST1", 4), ("ST4", 0), ("t", 5), ("ST3", 2), ("SUB", 5), ("ST1", 5), ("gx", 0), ("n2", 1), ("ST4", 1), ("t", 6),
    ("ST4", 2), ("SUB", 6), ("ST3", 3), ("ST2X", 4), ("ST2Y", 4), ("t", 7), ("ST2Y", 5), ("ST2X", 5), ("ST1", 6),
    ("ST3", 4), ("SUB", 7), ("g", 1, 0), ("ST4", 3), ("t", 8), ("ST1", 7), ("g", 1, 1), ("SUB", 8), ("ST3", 5),
    ("ST4", 4), ("ST2X", 6), ("ST2Y", 6), ("ST1", 8), ("t", 9), ("gy", 1), ("n1", 1), ("SUB", 9), ("ST4", 5),
    ("to", 10), ("ST3", 6), ("ST2X", 7), ("gc", 1), ("E", 0), ("ST2Y", 7), ("a", 1, 0), ("E", 1), ("a", 1, 1),
    ("ST2Y", 8), ("ST2X", 8), ("ST1", 9), ("a", 1, 2), ("ST3", 7), ("a", 1, 3), ("ST3", 8), ("E", 2), ("a", 1, 4),
    ("a", 1, 5), ("ST4", 6), ("ST2Y", 9), ("V", 0), ("ST4", 7), ("ST2X", 9), ("tv", 10), ("V", 1), ("SUB", 10),
    ("E", 3), ("ST1", 10), ("t", 11), ("SUB", 11), ("V", 2), ("ST3", 9), ("ST4", 8), ("ST1", 11), ("ST2Y", 10),
    ("ST2X", 10), ("E", 4), ("V", 3), ("ST2X", 11), ("gx", 1), ("ST3", 10), ("ST2Y", 11), ("ST4", 9), ("ST3", 11),
    ("ST4", 10), ("V", 4), ("ST4", 11),
)
SPLIT = (3, 2, 2, 2, 2, 2, 2, 2, 2, 2, 2, 2)
SLOTS = 5
PART = UNITS // 2
ROWS = 24


def backward_kernel(fold, layers, w, cotf, outx, glob, lengths, bucket,
                    xr_o, qkv_o, lse_o, ctx_o, n1_o, r1_o, y1r_o, act_o, dg_o, n2_o, r2_o,
                    output, ingrad, shards, vout, vlate,
                    wv, g, gh, n, r, low, act, dg, y1r, ctx, qkv, lse, xr, gc, gqkv, sums,
                    wsem, lsem, esem, *rest):
    p = Place(fold)
    p.greet()
    m = p.y
    red = Reduce(p, 6 * layers, SLOTS, SPLIT, rest[0], shards, *rest[1:16])
    early = Total(p, *rest[16:19], rest[19:21])
    late = Total(p, *rest[21:24], rest[24:26])
    limits = bounds(lengths, bucket, m)
    order = [3 * l + t for l in reversed(range(layers)) for t in (2, 1, 0)]
    full = slice(0, UNITS)

    def row(i):
        return glob[i:i + 1, :]

    def weights(i):
        return pltpu.make_async_copy(w.at[order[i]], wv.at[i % 2], wsem.at[i % 2])

    table = {"n2": (n2_o, n), "r2": (r2_o, r), "act": (act_o, act), "dg": (dg_o, dg), "y1r": (y1r_o, y1r),
             "n1": (n1_o, n), "r1": (r1_o, r), "ctx": (ctx_o, ctx), "qkv": (qkv_o, qkv), "lse": (lse_o, lse),
             "xr": (xr_o, xr)}
    loads = {}

    def begin(l, *names):
        for i in names:
            src, dst = table[i]
            loads[i] = pltpu.make_async_copy(src.at[l], dst, lsem.at[list(table).index(i)])
            loads[i].start()

    def need(*names):
        for i in names:
            loads.pop(i).wait()

    def add(line, value):
        early.v[0, line:line + 1, :] = early.v[0, line:line + 1, :] + value

    def norm_stage(l, which):
        base = 12 * (layers - 1 - l)

        @pl.loop(0, 4)
        def _(i):
            rows = at(128 * i, 128)
            v, a, b, c = norm_back(g, rows, row(6 * l + 2 + which), n, r)
            gh[rows, :] = v
            low[rows, :] = v.astype(BF16)
            add(base + which, a)
            add(base + 2 + which, b)
            add(base + 4 + which, c)

    def tiles(u, left, right, start, width, to):
        s = red.slot(u)
        for y in range(2):
            v = dot(left[...], right[y, :, start:start + width], TN).astype(BF16)
            s[y, :, :, :, :, to:to + width] = v.reshape(4, 2, 2, 48, width)

    def norm_two(i):
        l = layers - 1 - i
        need("n2", "r2")
        norm_stage(l, 1)
        begin(l, "n1", "r1")

    def gradient(u):
        l, kind = layers - 1 - u // 6, u % 6
        if kind < 2:
            if kind == 0:
                need("act")
            tiles(u, low, act, PART * kind, PART, 0)
            if kind == 1 and l:
                begin(l - 1, "act")
        elif kind < 4:
            if kind == 2:
                need("y1r")
            tiles(u, y1r, dg, PART * (kind - 2), PART, 0)
        else:
            tiles(u, xr, gqkv, 0, 2 * HALF, 0)

    def gradient_out(u):
        need("ctx")
        tiles(u, low, ctx, 0, HALF, HALF)

    def gradient_value(u):
        need("xr")
        tiles(u, xr, gqkv, 2 * HALF, HALF, 0)

    def units(i, half):
        if half == 0:
            weights(3 * i).wait()
            need("dg")
        wc = wv.at[3 * i % 2]
        for y in range(2):
            cols = slice(PART * half, PART * half + PART)
            gi = dot(low[...], columns(wc, y, cols)) * dg[y, :, cols].astype(F32)
            dg[y, :, cols] = gi.astype(BF16)
            line = 12 * i + 6 + 2 * y + half
            early.v[0, line:line + 1, :] = jnp.sum(gi, axis=0, keepdims=True)
        if half == 1 and 3 * i + 2 < 3 * layers:
            weights(3 * i + 2).start()

    def hidden(i):
        weights(3 * i + 1).wait()
        wb = wv.at[(3 * i + 1) % 2]
        g[...] = gh[...] + dot(dg[0], columns(wb, 0, full), NT) + dot(dg[1], columns(wb, 1, full), NT)
        if 3 * i + 3 < 3 * layers:
            weights(3 * i + 3).start()
        l = layers - 1 - i
        if l:
            begin(l - 1, "dg", "y1r")

    def norm_one(i):
        l = layers - 1 - i
        need("n1", "r1")
        norm_stage(l, 0)
        if l:
            begin(l - 1, "n2", "r2")

    def context(i):
        l = layers - 1 - i
        weights(3 * i + 2).wait()
        wa = wv.at[(3 * i + 2) % 2]
        for y in range(2):
            gc[y] = dot(low[...], columns(wa, y, slice(3 * HALF, 4 * HALF))).astype(BF16)
        if l:
            begin(l - 1, "ctx")
        need("qkv", "lse")

    def attention(i, inside):
        @pl.loop(0, 6)
        def _(j):
            attend_back(qkv, lse, gc, gqkv, sums, limits, j)
            for turn, todo in enumerate(inside):
                if todo:
                    @pl.when(j == turn)
                    def _():
                        for t in todo:
                            steps[t[0]](*t[1:])
        for y in range(2):
            for t in range(2):
                where = slice(HALF * y, HALF * y + HALF)
                if i == layers - 1:
                    late.v[0, t:t + 1, where] = sums[y, t]
                else:
                    early.v[0, 12 * i + 10 + t:12 * i + 11 + t, where] = sums[y, t]

    def state(i):
        l = layers - 1 - i
        wa = wv.at[(3 * i + 2) % 2]
        wqkv = [columns(wa, y, slice(0, 3 * HALF)) for y in range(2)]
        if l:
            g[...] = gh[...] + dot(gqkv[0], wqkv[0], NT) + dot(gqkv[1], wqkv[1], NT)
            begin(l - 1, "qkv", "lse", "xr")
            weights(3 * i + 4).start()
        else:
            for j in range(2):
                rows = at((S // 2) * (1 - m if j == 0 else m), S // 2)
                v = gh[rows, :] + dot(gqkv[0, rows, :], wqkv[0], NT) + dot(gqkv[1, rows, :], wqkv[1], NT)
                low[rows, :] = v.astype(BF16)
                (swap_g if j == 0 else own_g).start()

    steps = {
        "n2": norm_two, "t": gradient, "to": gradient_out, "tv": gradient_value, "g": units, "gy": hidden, "n1": norm_one,
        "gc": context, "gx": state, "SUB": red.submit, "ST1": red.cores, "ST2X": red.after_x, "ST2Y": red.after_y,
        "ST3": red.plane, "ST4": red.line, "E": lambda i: early.step(i, vout), "V": lambda i: late.step(i, vlate),
        "SO": lambda: swap_o.start()}
    own_o = pltpu.make_async_copy(outx.at[m], output.at[m], esem.at[0])
    swap_o = remote(outx.at[1 - m], output.at[m], esem.at[1], esem.at[2], p.to_y)
    half = lambda i: low.at[at((S // 2) * i, S // 2), :]
    own_g = pltpu.make_async_copy(half(m), ingrad.at[m], esem.at[3])
    swap_g = remote(half(1 - m), ingrad.at[m], esem.at[4], esem.at[5], p.to_y)
    top = layers - 1
    cload = pltpu.make_async_copy(cotf, low, esem.at[6])
    cload.start()
    begin(top, "n2", "r2", "act")
    early.v[0] = jnp.zeros((ROWS, D), F32)
    late.v[0] = jnp.zeros((8, D), F32)
    cload.wait()
    g[...] = low[...].astype(F32)
    own_o.start()
    plan = list(BACKWARD)
    met = False
    while plan:
        t = plan.pop(0)
        if t[0] != "a":
            if t[0] in ("SO", "SUB") and not met:
                p.greeted()
                met = True
            steps[t[0]](*t[1:])
            if t == ("SUB", 0):
                begin(top, "dg")
                weights(0).start()
            elif t == ("SUB", 1):
                begin(top, "y1r")
                weights(1).start()
            elif t == ("SUB", 2):
                begin(top, "ctx", "qkv", "lse", "xr")
            continue
        inside = [[] for _ in range(6)]
        while (t[0], t[-1]) != ("a", 5):
            if t[0] == "a":
                turn = t[2]
            else:
                inside[turn].append(t)
            t = plan.pop(0)
        attention(t[1], inside)
    red.finish()
    own_o.wait()
    swap_o.wait()
    own_g.wait()
    swap_g.wait()


def backward(w, cotf, outx, glob, lengths, bucket, saved, layers, fold):
    n = 6 * layers
    dma = pltpu.SemaphoreType.DMA
    shape = jax.ShapeDtypeStruct
    vm = pltpu.VMEM
    first, rest = Reduce.scratch(SLOTS, PART)
    return pl.pallas_call(
        functools.partial(backward_kernel, fold, layers),
        out_shape=[shape((2, S // 2, D), BF16), shape((2, S // 2, D), BF16), shape((n, 48, PART), F32),
                   shape((ROWS, D), F32), shape((8, D), F32)],
        in_specs=[ANY, ANY, ANY, VMEM, SMEM, SMEM] + [ANY] * 11,
        out_specs=[ANY, ANY, VMEM, VMEM, VMEM],
        scratch_shapes=[
            vm((2, 2, 4, 2, 2, 48, UNITS), BF16), vm((S, D), F32), vm((S, D), F32), vm((S, D), F32), vm((S, 128), F32),
            vm((S, D), BF16), vm((2, S, UNITS), BF16), vm((2, S, UNITS), BF16), vm((S, D), BF16),
            vm((2, S, HALF), BF16), vm((2, S, 3 * HALF), BF16), vm((12, 1, S), F32), vm((S, D), BF16), vm((2, S, HALF), BF16),
            vm((2, S, 3 * HALF), BF16), vm((2, 2, 1, HALF), F32),
            dma((2,)), dma((11,)), dma((7,)), *first, *rest, *Total.scratch(ROWS), *Total.scratch(8)],
        compiler_params=pltpu.CompilerParams(collective_id=2, has_side_effects=True, vmem_limit_bytes=62 * 2**20),
    )(w, cotf, outx, glob, lengths, bucket, *saved)


def pack_kernel(w_qkv, w_out, w_up, w_down, bias_qv, bias_up, bias_out, ln_gain, ln_bias, packed, vec, glob):
    vec[...] = jnp.zeros_like(vec)
    glob[...] = jnp.zeros_like(glob)
    for l in range(w_qkv.shape[0]):
        for t in range(3):
            packed[3 * l, :, HALF * t:HALF * t + HALF] = w_qkv[l, t]
        packed[3 * l, :, 3 * HALF:] = w_out[l]
        packed[3 * l + 1] = w_up[l]
        packed[3 * l + 2] = w_down[l]
        qv = bias_qv[l].astype(F32)
        for t in range(2):
            vec[2 + l:3 + l, HALF * t:HALF * t + HALF] = qv[t:t + 1]
        for i, ref in enumerate((bias_out, ln_gain, ln_bias)):
            glob[6 * l + 2 * i:6 * l + 2 * i + 2, :] = ref[l].astype(F32)
    vec[0:2, :] = bias_up[...].astype(F32)


def pack(*args):
    layers = args[0].shape[0]
    shape = jax.ShapeDtypeStruct
    return pl.pallas_call(
        pack_kernel,
        out_shape=[shape((3 * layers, 48, UNITS), BF16), shape((8, UNITS), F32), shape((16, D), F32)],
        in_specs=[VMEM] * len(args), out_specs=[VMEM] * 3,
        compiler_params=pltpu.CompilerParams(vmem_limit_bytes=60 * 2**20))(*args)


def unpack_kernel(layers, shards, early, late, out_in, ingrad_in,
                  out, ingrad, qkv, qv, w_out, bias, gain, shift, up, bias_up, down):
    m = lax.axis_index("mp")
    mine = lambda a, b: jnp.where(m == 0, a, b)
    out[...] = out_in[...]
    ingrad[...] = ingrad_in[...]
    for l in range(layers):
        u = 6 * (layers - 1 - l)
        base = 2 * u
        for half in range(2):
            cols = slice(PART * half, PART * half + PART)
            down[l, :, cols] = shards[u + half]
            up[l, :, cols] = shards[u + 2 + half]
            bias_up[l:l + 1, cols] = mine(early[base + 6 + half:base + 7 + half, :], early[base + 8 + half:base + 9 + half, :])
        qkv[l, 0] = shards[u + 5, :, :HALF]
        qkv[l, 1] = shards[u + 5, :, HALF:]
        qkv[l, 2] = shards[u + 4, :, :HALF]
        w_out[l] = shards[u + 4, :, HALF:]
        gain[l] = early[base:base + 2, :]
        shift[l] = early[base + 2:base + 4, :]
        bias[l] = early[base + 4:base + 6, :]
        for t in range(2):
            line = early[base + 10 + t:base + 11 + t, :] if l else late[t:t + 1, :]
            qv[l, t:t + 1, :] = mine(line[:, :HALF], line[:, HALF:])


def unpack(layers, *args):
    shape = lambda *s: jax.ShapeDtypeStruct(s, F32)
    rows = jax.ShapeDtypeStruct((2, S // 2, D), BF16)
    return pl.pallas_call(
        functools.partial(unpack_kernel, layers),
        out_shape=[rows, rows, shape(layers, 3, 48, HALF), shape(layers, 2, HALF), shape(layers, 48, HALF), shape(layers, 2, D),
                   shape(layers, 2, D), shape(layers, 2, D), shape(layers, 48, UNITS), shape(layers, UNITS),
                   shape(layers, 48, UNITS)],
        in_specs=[VMEM] * len(args), out_specs=[VMEM] * 11,
        compiler_params=pltpu.CompilerParams(vmem_limit_bytes=60 * 2**20))(*args)


def per_device(layer_input, cotangent, lengths, bucket, w_qkv, bias_qv, w_out, bias_out, ln_gain, ln_bias, w_up, bias_up, w_down):
    layers = w_qkv.shape[0]
    fold = lax.axis_size("dp") // GROUPS
    members = [[g * fold + i for i in range(fold)] for g in range(GROUPS)]
    if fold > 1:
        join = lambda v, axis: lax.all_gather(v, "dp", axis=axis, tiled=True, axis_index_groups=members)
        w_qkv, w_out, w_up, w_down = join(w_qkv, 2), join(w_out, 2), join(w_up, 1), join(w_down, 2)
    turn = lambda v: v.transpose(0, 2, 1)
    packed, vec, glob = pack(w_qkv, turn(w_out), w_up, turn(w_down), bias_qv, bias_up, bias_out, ln_gain, ln_bias)
    w, cotf, out, *saved = forward(packed, layer_input, cotangent, vec, glob, lengths, bucket, layers, fold)
    output, ingrad, shards, early, late = backward(
        w, cotf.reshape(S, D), out.reshape(2, S // 2, D), glob, lengths, bucket, saved, layers, fold)
    output, ingrad, qkv, qv, w_out, bias, gain, shift, up, bias_up, down = unpack(layers, shards, early, late, output, ingrad)
    w_out, down = turn(w_out), turn(down)
    if fold > 1:
        part = lambda v, axis: lax.psum_scatter(v, "dp", scatter_dimension=axis, tiled=True, axis_index_groups=members)
        qkv, w_out, up, down = part(qkv, 2), part(w_out, 2), part(up, 1), part(down, 2)
        qv, bias, gain, shift, bias_up = lax.psum((qv, bias, gain, shift, bias_up), "dp", axis_index_groups=members)
    return output, ingrad, qkv, qv, w_out, bias, gain, shift, up, bias_up, down


def solution(mesh):
    in_specs = (
        P("dp", "mp", None),
        P("dp", "mp", None),
        P("dp", None),
        P("dp"),
        P(None, None, "dp", "mp"),
        P(None, None, "mp"),
        P(None, "mp", "dp"),
        P(),
        P(),
        P(),
        P(None, "dp", "mp"),
        P(None, "mp"),
        P(None, "mp", "dp"),
    )
    out_specs = (
        P("dp", "mp", None),
        P("dp", "mp", None),
        P(None, None, "dp", "mp"),
        P(None, None, "mp"),
        P(None, "mp", "dp"),
        P(),
        P(),
        P(),
        P(None, "dp", "mp"),
        P(None, "mp"),
        P(None, "mp", "dp"),
    )
    return jax.shard_map(
        per_device, mesh=mesh, in_specs=in_specs, out_specs=out_specs, check_vma=False
    )
```

```python
import functools

import jax
import jax.numpy as jnp
from jax import lax
from jax.experimental import pallas as pl
from jax.experimental.pallas import tpu as pltpu
from jax.sharding import PartitionSpec as P

F32 = jnp.float32
BF16 = jnp.bfloat16
S = 512
D = 768
HALF = 384
UNITS = 1536
GROUPS = 16
EPS = 1e-12
MESH = pl.DeviceIdType.MESH
NN = (((1,), (0,)), ((), ()))
NT = (((1,), (1,)), ((), ()))
TN = (((0,), (0,)), ((), ()))
ANY = pl.BlockSpec(memory_space=pl.ANY)
VMEM = pl.BlockSpec(memory_space=pltpu.VMEM)
SMEM = pl.BlockSpec(memory_space=pltpu.SMEM)


def dot(a, b, dims=NN):
    return lax.dot_general(a, b, dims, preferred_element_type=F32)


def at(start, size):
    return pl.ds(pl.multiple_of(start, size), size)


def remote(src, dst, send_sem, recv_sem, device):
    return pltpu.make_async_remote_copy(
        src_ref=src, dst_ref=dst, send_sem=send_sem, recv_sem=recv_sem,
        device_id=device, device_id_type=MESH)


class Place:
    def __init__(self, fold):
        d = lax.axis_index("dp")
        self.fold = fold
        self.member = lax.rem(d, fold) if fold > 1 else 0
        g = d // fold if fold > 1 else d
        self.z = g // 4
        self.xc = lax.rem(g, 4)
        self.x = self.xc // 2
        self.c = lax.rem(self.xc, 2)
        self.y = lax.axis_index("mp")
        self.xo = (1 - self.x) * 2 + self.c
        self.co = self.x * 2 + (1 - self.c)
        self.yo = 1 - self.y
        self.to_z = [None] + [self.device(lax.rem(self.z + j, 4), self.xc, self.y) for j in (1, 2, 3)]
        self.to_x = self.device(self.z, self.xo, self.y)
        self.to_y = self.device(self.z, self.xc, self.yo)
        self.to_c = self.device(self.z, self.co, self.y)

    def device(self, z, xc, y):
        return {"dp": (z * 4 + xc) * self.fold + self.member, "mp": y}

    def greet(self):
        for device in (*self.to_z[1:], self.to_x, self.to_y, self.to_c):
            pl.semaphore_signal(pltpu.get_barrier_semaphore(), inc=1, device_id=device, device_id_type=MESH)

    def greeted(self):
        pl.semaphore_wait(pltpu.get_barrier_semaphore(), 6)


class Gather:
    def __init__(self, place, packed, w, turned, via_x, lsem, zs, zr, xs, xr, ys, yr, fs, fr, cs, cr, qs, qr):
        self.p, self.packed, self.w, self.turned, self.via_x = place, packed, w, turned, via_x
        self.sems = dict(z=(zs, zr), x=(xs, xr), y=(ys, yr), f=(fs, fr), c=(cs, cr), q=(qs, qr))
        self.lsem = lsem
        z = place.z
        low = z < 2
        self.order = [z, jnp.where(low, 1 - z, 5 - z), jnp.where(low, 2, 1), jnp.where(low, 3, 0)]
        self.inner = (z == 1) | (z == 2)
        self.partner = place.device(z + 1 - 2 * lax.rem(z, 2), place.xc, place.y)
        self.across = place.device(3 - z, place.xc, place.y)
        self.sends, self.inner_sends, self.waited = [], [], set()

    def go(self, make):
        make().start()
        self.sends.append(make)

    def go_inner(self, make):
        pl.when(self.inner)(lambda: make().start())
        self.inner_sends.append(make)

    def copy(self, kind, k, i, j, src, dst, device):
        send, recv = self.sems[kind]
        return remote(src, dst, send.at[k, i], recv.at[k, j], device)

    def block(self, k, j=0, other_x=False, other_y=False):
        p = self.p
        return self.w.at[k, p.yo if other_y else p.y, self.order[j], 1 - p.x if other_x else p.x, p.c]

    def source(self, k, j):
        return self.packed.at[k] if j == 0 else self.block(k, j)

    def own(self, k):
        return pltpu.make_async_copy(self.packed.at[k], self.block(k), self.lsem.at[k])

    def load(self, k, j):
        return self.w.at[k, :, self.order[j], :, self.p.c] if k == self.turned else self.block(k, j)

    def line(self, k, i):
        j, slot, device = ((0, 1, self.partner), (0, 2, self.across), (1, 3, self.across), (2, 2, self.partner),
                           (3, 3, self.partner))[i]
        src = dst = self.load(k, j)
        if j == 0 and k != self.turned:
            src = self.packed.at[k]
        return self.copy("z", k, i, slot, src, dst, device)

    def line_start(self, k):
        self.go(lambda: self.line(k, 0))
        self.go_inner(lambda: self.line(k, 1))

    def line_wait(self, k, j):
        self.copy("z", k, 0, j, self.load(k, j), self.load(k, j), self.partner).wait_recv()
        self.go_inner(lambda: self.line(k, j + 1))

    def to_x(self, k, j):
        return self.copy("x", k, j, j, self.source(k, j), self.block(k, j), self.p.to_x)

    def to_y(self, k, j):
        return self.copy("y", k, j, j, self.source(k, j), self.block(k, j), self.p.to_y)

    def diagonal(self, k, j):
        x = self.via_x(k, j)
        block = self.block(k, j, other_x=not x, other_y=x)
        return self.copy("f", k, j, j, block, block, self.p.to_x if x else self.p.to_y)

    def to_core(self, k, i):
        p = self.p
        if k == self.turned:
            block = self.load(k, i)
        else:
            y, x = ((p.y, p.x), (p.y, 1 - p.x), (p.yo, p.x), (p.yo, 1 - p.x))[i]
            block = self.w.at[k, y, :, x, p.c]
        return self.copy("c", k, i, i, block, block, p.to_c)

    def start(self, k):
        self.own(k).start()
        self.line_start(k)
        self.go(lambda: self.to_x(k, 0))
        self.go(lambda: self.to_y(k, 0))

    def spread(self, k, j):
        self.go(lambda: self.to_x(k, j))
        self.go(lambda: self.to_y(k, j))
        if j == 3:
            self.own(k).wait()
            self.go(lambda: self.to_core(k, 0))

    def seen(self, kind, k, j):
        if (kind, k, j) not in self.waited:
            self.waited.add((kind, k, j))
            (self.to_x if kind == "x" else self.to_y)(k, j).wait_recv()

    def forward(self, k, j):
        self.seen("y" if self.via_x(k, j) else "x", k, j)
        self.go(lambda: self.diagonal(k, j))

    def side(self, k, kind):
        for j in range(4):
            self.seen(kind, k, j)
        self.go(lambda: self.to_core(k, 1 if kind == "x" else 2))

    def share(self, k):
        for j in range(4):
            self.diagonal(k, j).wait_recv()
        self.go(lambda: self.to_core(k, 3))

    def arrive(self, k):
        for i in range(4):
            self.to_core(k, i).wait_recv()

    def turned_copy(self, i):
        p, k = self.p, self.turned
        if i < 2:
            return self.copy("q", 0, i, i, self.packed.at[k], self.block(k), (p.to_x, p.to_y)[i])
        half = slice(UNITS // 2 * (i - 2), UNITS // 2 * (i - 1))
        block = self.block(k, other_x=i == 2, other_y=i == 3).at[:, half]
        return self.copy("q", 0, i, i, block, block, (p.to_y, p.to_x)[i - 2])

    def turned_start(self):
        self.own(self.turned).start()
        self.go(lambda: self.turned_copy(0))
        self.go(lambda: self.turned_copy(1))

    def turned_forward(self, i):
        self.turned_copy(i).wait_recv()
        self.go(lambda: self.turned_copy(2 + i))

    def turned_line(self, j):
        k = self.turned
        if j == 0:
            self.own(k).wait()
            self.turned_copy(2).wait_recv()
            self.turned_copy(3).wait_recv()
            self.line_start(k)
        else:
            self.line_wait(k, j)
        self.go(lambda: self.to_core(k, j))

    def finish(self):
        for make in self.sends:
            make().wait_send()
        for make in self.inner_sends:
            pl.when(self.inner)(lambda: make().wait_send())

    @staticmethod
    def scratch(n):
        dma = pltpu.SemaphoreType.DMA
        return [dma((n,)), dma((n, 5)), dma((n, 4))] + [dma((n, 4))] * 8 + [dma((1, 4))] * 2


def columns(w, y, cols):
    v = w[y, :, :, :, :, cols]
    return v.reshape(D, v.shape[-1])


def bounds(lengths, bucket, m):
    l0, l1, one = lengths[m, 0], lengths[m, 1], bucket[m] == 1
    half = S // 2
    return jnp.where(one, l0 + l1, l0), jnp.where(one, 0, half), jnp.where(one, l0 + l1, half + l1)


def key_bias(limits):
    first_end, second_start, second_end = limits
    k = lax.broadcasted_iota(jnp.int32, (S, 128), 0)
    lo = jnp.where(k < first_end, 0.0, -1e9)
    hi = jnp.where((k >= second_start) & (k < second_end), 0.0, -1e9)
    return lo, hi


def with_mask(q2, k2, half, bias):
    lane = lax.broadcasted_iota(jnp.int32, (S, 128), 1)
    low = lax.broadcasted_iota(jnp.int32, (S, 128), 0) < S // 2
    own = (lane // 64) == half
    o = 64 * (1 - half)
    one = lambda pick: jnp.where(pick, 1.0, 0.0)
    qa = jnp.where(lane == o, one(low), jnp.where(lane == o + 1, one(~low), 0.0))
    ka = jnp.where(lane == o, bias[0], jnp.where(lane == o + 1, bias[1], 0.0))
    qm = jnp.where(own, q2.astype(F32) * 0.125, qa).astype(BF16)
    km = jnp.where(own, k2.astype(F32), ka).astype(BF16)
    return qm, km


def head_pair(pair):
    y, r = pair // 3, lax.rem(pair, 3)
    return y, [at(o + 128 * r, 128) for o in (0, HALF, 2 * HALF)]


def attend(qkv, ctx, lse, limits, pair):
    y, (qc, kc, vc) = head_pair(pair)
    q2, k2, v2 = qkv[y, :, qc], qkv[y, :, kc], qkv[y, :, vc]
    bias = key_bias(limits)
    v2t = v2.T
    parts = []
    for half in range(2):
        qm, km = with_mask(q2, k2, half, bias)
        st = dot(km, qm, NT)
        top = jnp.max(st, axis=0, keepdims=True)
        e = jnp.exp(st - top)
        total = jnp.sum(e, axis=0, keepdims=True)
        lse[pair * 2 + half] = top + jnp.log(total)
        ct = dot(v2t[64 * half:64 * half + 64], e.astype(BF16))
        parts.append(ct * (1.0 / total))
    ctx[y, :, qc] = jnp.concatenate(parts, 0).T.astype(BF16)


def normalize(h, rows, gain, shift, n, r):
    v = h[rows, :]
    c = v - jnp.mean(v, axis=-1, keepdims=True)
    inverse = lax.rsqrt(jnp.mean(c * c, axis=-1, keepdims=True) + EPS)
    normed = c * inverse
    n[rows, :] = normed
    r[rows, :] = jnp.broadcast_to(inverse, (inverse.shape[0], 128))
    return normed * gain + shift


def gelu_parts(u):
    cdf = 0.5 * (1.0 + lax.erf(u * 0.7071067811865476))
    return u * cdf, cdf + u * (jnp.exp(-0.5 * u * u) * 0.3989422804014327)


PLAN = (
    ("S", 0), ("TS",), ("S", 1), ("S", 2), ("L", 0, 1), ("L", 1, 1), ("XY", 0, 1), ("L", 0, 2), ("L", 2, 1), ("S", 4),
    ("TF", 0), ("L", 0, 3), ("TF", 1), ("XY", 0, 3), ("L", 1, 2), ("F", 0, 0), ("XY", 0, 2), ("XY", 1, 1), ("F", 0, 1),
    ("L", 1, 3), ("TL", 0), ("F", 0, 3), ("F", 0, 2), ("XY", 1, 3), ("SX",), ("XY", 1, 2), ("S", 5), ("L", 4, 1),
    ("L", 2, 2), ("XY", 2, 1), ("XY", 2, 2), ("F", 4, 0), ("SH", 0), ("CX", 0), ("CY", 0), ("F", 1, 0), ("TL", 1),
    ("L", 2, 3), ("F", 1, 3), ("L", 5, 1), ("F", 1, 1), ("TL", 2), ("AR", 0), ("XY", 2, 3), ("XY", 5, 1), ("F", 1, 2),
    ("CY", 1), ("F", 2, 0), ("CX", 1), ("F", 2, 1), ("TL", 3), ("XY", 4, 1), ("CX", 2), ("AR", 3), ("F", 2, 3),
    ("L", 4, 2), ("SH", 1), ("L", 4, 3), ("F", 2, 2), ("XY", 4, 2), ("L", 5, 2), ("F", 4, 1), ("XY", 5, 2),
    ("XY", 4, 3), ("AR", 1), ("CY", 2), ("SH", 2), ("AR", 2), ("L", 5, 3), ("F", 4, 2), ("XY", 5, 3), ("F", 4, 3),
    ("F", 5, 0), ("CX", 4), ("CY", 4), ("CX", 5), ("F", 5, 2), ("F", 5, 1), ("SH", 4), ("F", 5, 3), ("AR", 4),
    ("CY", 5), ("SC",), ("SH", 5), ("AR", 5),
)
TURNED = 3
VIA_X = ((1, 1, 1, 0), (1, 0, 1, 1), (0, 1, 1, 0), (0, 1, 1, 0), (0, 1, 0, 1), (1, 0, 0, 1))


def forward_kernel(fold, layers, packed, xin, cot, vec, glob, lengths, bucket,
                   w, cotf, out, xr_o, qkv_o, lse_o, ctx_o, n1_o, r1_o, y1r_o, act_o, dg_o, n2_o, r2_o,
                   wv, xh, vecf, x, xr, qkv, lse, ctx, h, n1, r1, y1, y1r, act, dg, n2, r2,
                   wsem, esem, ssem, *gsems):
    p = Place(fold)
    m = p.y
    parts = 3 * layers
    assert parts == len(VIA_X)
    g = Gather(p, packed, w, TURNED, lambda k, j: VIA_X[k][j], *gsems)
    saves = {}
    names = ("xr", "qkv", "lse", "ctx", "n1", "r1", "y1r", "act", "dg", "n2", "r2")

    def load(k):
        return pltpu.make_async_copy(w.at[k], wv.at[k], wsem.at[k])

    def save(i, l, src, dst):
        if i in saves:
            saves.pop(i).wait()
        saves[i] = pltpu.make_async_copy(src, dst.at[l], ssem.at[names.index(i), l])
        saves[i].start()

    def before(*names):
        for i in names:
            if i in saves:
                saves.pop(i).wait()

    own_x = pltpu.make_async_copy(xin.at[m], xh.at[m], esem.at[0])
    swap_x = remote(xin.at[1 - m], xh.at[m], esem.at[1], esem.at[2], p.to_y)
    own_c = pltpu.make_async_copy(cot.at[m], cotf.at[m], esem.at[3])
    swap_c = remote(cot.at[1 - m], cotf.at[m], esem.at[4], esem.at[5], p.to_y)
    own_v = pltpu.make_async_copy(vec, vecf.at[m], esem.at[6])
    swap_v = remote(vec, vecf.at[m], esem.at[7], esem.at[8], p.to_y)
    limits = bounds(lengths, bucket, m)

    def row(i):
        return glob[i:i + 1, :]

    def stage_a(l, y):
        wa = wv.at[3 * l]
        if y == 0:
            before("xr", "qkv", "lse", "ctx", "n1", "r1", "y1r")
            save("xr", l, xr, xr_o)
        for t in range(3):
            cols = slice(HALF * t, HALF * t + HALF)
            v = dot(xr[...], columns(wa, y, cols))
            if t != 1:
                v = v + vecf[y, 2 + l:3 + l, HALF * (t // 2):HALF * (t // 2) + HALF]
            qkv[y, :, cols] = v.astype(BF16)
        if y == 1:
            save("qkv", l, qkv, qkv_o)

    def stage_out(l):
        wa = wv.at[3 * l]
        save("lse", l, lse, lse_o)
        save("ctx", l, ctx, ctx_o)
        wo = [columns(wa, y, slice(3 * HALF, 4 * HALF)) for y in range(2)]
        h[...] = x[...] + row(6 * l) + dot(ctx[0], wo[0], NT) + dot(ctx[1], wo[1], NT)

        @pl.loop(0, 2)
        def _(i):
            rows = at(256 * i, 256)
            o = normalize(h, rows, row(6 * l + 2), row(6 * l + 4), n1, r1)
            y1[rows, :] = o
            y1r[rows, :] = o.astype(BF16)
        save("n1", l, n1, n1_o)
        save("r1", l, r1, r1_o)
        save("y1r", l, y1r, y1r_o)

    def stage_b(l, y, i):
        wb = wv.at[3 * l + 1]
        if y == 0 and i == 0:
            before("act", "dg", "n2", "r2")
        cols = slice(768 * i, 768 * i + 768)
        u = dot(y1r[...], columns(wb, y, cols)) + vecf[y, l:l + 1, cols]
        a, d = gelu_parts(u)
        act[y, :, cols] = a.astype(BF16)
        dg[y, :, cols] = d.astype(BF16)
        if y == 1 and i == 1:
            save("act", l, act, act_o)
            save("dg", l, dg, dg_o)

    def stage_c(l):
        wc = wv.at[3 * l + 2]
        before("xr")
        full = slice(0, UNITS)
        h[...] = (y1[...] + row(6 * l + 1) + dot(act[0], columns(wc, 0, full), NT)
                  + dot(act[1], columns(wc, 1, full), NT))

        @pl.loop(0, 2)
        def _(i):
            rows = at(256 * i, 256)
            o = normalize(h, rows, row(6 * l + 3), row(6 * l + 5), n2, r2)
            x[rows, :] = o
            xr[rows, :] = o.astype(BF16)
        save("n2", l, n2, n2_o)
        save("r2", l, r2, r2_o)

    pending, here, used = [], set(), [0]

    def ready(k):
        l, kind = k // 3, k % 3
        pending.append(lambda: load(k).wait())
        if k == 0:
            pending.append(first)
        if kind == 0:
            pending.append(lambda: stage_a(l, 0))
            pending.append(lambda: stage_a(l, 1))
            pending.append((6, lambda j: attend(qkv, ctx, lse, limits, j)))
            pending.append(lambda: stage_out(l))
        elif kind == 1:
            for y in range(2):
                for i in range(2):
                    pending.append(lambda y=y, i=i: stage_b(l, y, i))
        else:
            pending.append(lambda: stage_c(l))

    def first():
        own_x.wait()
        swap_x.wait()
        own_v.wait()
        swap_v.wait()
        for i in range(2):
            rows = slice(256 * i, 256 * i + 256)
            xr[rows, :] = xh[i]
            x[rows, :] = xh[i].astype(F32)

    def run(steps):
        steps = list(steps)
        while steps or pending:
            piece = pending.pop(0) if pending else None
            if isinstance(piece, tuple):
                inside, steps = steps[:piece[0]], steps[piece[0]:]

                @pl.loop(0, piece[0])
                def _(j):
                    piece[1](j)
                    for i, step in enumerate(inside):
                        pl.when(j == i)(step)
            else:
                if piece is not None:
                    piece()
                if steps:
                    steps.pop(0)()

    def arrived(k):
        g.arrive(k)
        load(k).start()
        here.add(k)
        while used[0] in here:
            ready(used[0])
            used[0] += 1

    steps = {
        "S": g.start, "L": g.line_wait, "XY": g.spread, "F": g.forward, "CX": lambda k: g.side(k, "x"),
        "CY": lambda k: g.side(k, "y"), "SH": g.share, "AR": arrived, "TS": g.turned_start, "TF": g.turned_forward,
        "TL": g.turned_line, "SX": lambda: (swap_v.start(), swap_x.start()), "SC": lambda: swap_c.start()}
    plan = [lambda t=t: steps[t[0]](*t[1:]) for t in PLAN]

    p.greet()
    own_x.start()
    own_v.start()
    own_c.start()
    p.greeted()
    run(plan)
    own_c.wait()
    swap_c.wait()
    last = pltpu.make_async_copy(xr, out, esem.at[9])
    last.start()
    g.finish()
    for copy in saves.values():
        copy.wait()
    last.wait()


def forward(packed, xin, cot, vec, glob, lengths, bucket, layers, fold):
    n = 3 * layers
    dma = pltpu.SemaphoreType.DMA
    saved = [((S, D), BF16), ((2, S, 3 * HALF), BF16), ((12, 1, S), F32), ((2, S, HALF), BF16), ((S, D), F32), ((S, 128), F32),
             ((S, D), BF16), ((2, S, UNITS), BF16), ((2, S, UNITS), BF16), ((S, D), F32), ((S, 128), F32)]
    shape = jax.ShapeDtypeStruct
    vm = pltpu.VMEM
    return pl.pallas_call(
        functools.partial(forward_kernel, fold, layers),
        out_shape=[shape((n, 2, 4, 2, 2, 48, UNITS), BF16), shape((2, S // 2, D), BF16), shape((S, D), BF16)]
        + [shape((layers, *s), d) for s, d in saved],
        in_specs=[ANY, ANY, ANY, ANY, VMEM, SMEM, SMEM],
        out_specs=[ANY] * (3 + len(saved)),
        scratch_shapes=[
            vm((n, 2, 4, 2, 2, 48, UNITS), BF16), vm((2, S // 2, D), BF16), vm((2, 8, UNITS), F32), vm((S, D), F32),
            vm((S, D), BF16), vm((2, S, 3 * HALF), BF16), vm((12, 1, S), F32), vm((2, S, HALF), BF16),
            vm((S, D), F32), vm((S, D), F32), vm((S, 128), F32), vm((S, D), F32), vm((S, D), BF16),
            vm((2, S, UNITS), BF16), vm((2, S, UNITS), BF16), vm((S, D), F32), vm((S, 128), F32),
            dma((n,)), dma((10,)), dma((11, layers)), *Gather.scratch(n)],
        compiler_params=pltpu.CompilerParams(collective_id=1, has_side_effects=True, vmem_limit_bytes=60 * 2**20),
    )(packed, xin, cot, vec, glob, lengths, bucket)


class Reduce:
    def __init__(self, place, total, slots, split, held, out, rc, rx, ry, rx2, ry2, rz, cs, cr, xs, xr, ys, yr, zs, zr, free):
        self.p, self.total, self.slots, self.split = place, total, slots, split
        self.held, self.out, self.buffers = held, out, (rc, rx, ry, rx2, ry2, rz)
        self.sems = (cs, cr, xs, xr, ys, yr, zs, zr)
        self.free = free
        self.sends = {}

    def slot(self, u):
        for args in self.sends.pop(u - self.slots, ()):
            self.copy(u - self.slots, *args).wait_send()
        return self.held.at[u % self.slots]

    def go(self, u, *args):
        self.copy(u, *args).start()
        self.sends.setdefault(u, []).append(args)

    def got(self, u, *args):
        self.copy(u, *args).wait_recv()

    def copy(self, u, kind, j=0):
        p, s, n = self.p, u % self.slots, self.split[u]
        h = self.held.at[s]
        rc, rx, ry, rx2, ry2, rz = self.buffers
        cs, cr, xs, xr, ys, yr, zs, zr = self.sems
        if kind == "c":
            return remote(h.at[:, :, :, 1 - p.c], rc.at[s], cs.at[s], cr.at[s], p.to_c)
        if kind == "x1":
            return remote(h.at[:, 0:n, 1 - p.x, p.c], rx.at[s, :, 0:n], xs.at[s, 0], xr.at[s, 0], p.to_x)
        if kind == "y1":
            return remote(h.at[p.yo, n:4, :, p.c], ry.at[s, 0:4 - n], ys.at[s, 0], yr.at[s, 0], p.to_y)
        if kind == "y2":
            return remote(h.at[p.yo, 0:n, p.x, p.c], ry2.at[s, 0:n], ys.at[s, 1], yr.at[s, 1], p.to_y)
        if kind == "x2":
            return remote(h.at[p.y, n:4, 1 - p.x, p.c], rx2.at[s, 0:4 - n], xs.at[s, 1], xr.at[s, 1], p.to_x)
        to = lax.rem(p.z + j, 4)
        return remote(h.at[p.y, to, p.x, p.c], rz.at[s, j - 1], zs.at[s, j - 1], zr.at[s, j - 1], p.to_z[j])

    def submit(self, u):
        if u >= self.slots:
            for i in range(6):
                pl.semaphore_wait(self.free.at[i], 1)
        self.go(u, "c")

    def cores(self, u):
        p, h, rc = self.p, self.held.at[u % self.slots], self.buffers[0].at[u % self.slots]
        self.got(u, "c")

        @pl.loop(0, 4)
        def _(z):
            for y in range(2):
                for x in range(2):
                    h[y, z, x, p.c] = h[y, z, x, p.c] + rc[y, z, x]
        self.go(u, "x1")
        self.go(u, "y1")

    def after_x(self, u):
        p, h, rx, n = self.p, self.held.at[u % self.slots], self.buffers[1].at[u % self.slots], self.split[u]
        self.got(u, "x1")
        for y in range(2):
            for z in range(n):
                h[y, z, p.x, p.c] = h[y, z, p.x, p.c] + rx[y, z]
        self.go(u, "y2")

    def after_y(self, u):
        p, h, ry, n = self.p, self.held.at[u % self.slots], self.buffers[2].at[u % self.slots], self.split[u]
        self.got(u, "y1")
        for z in range(n, 4):
            for x in range(2):
                h[p.y, z, x, p.c] = h[p.y, z, x, p.c] + ry[z - n, x]
        self.go(u, "x2")

    def plane(self, u):
        p, h, n = self.p, self.held.at[u % self.slots], self.split[u]
        _, _, _, rx2, ry2, _ = (b.at[u % self.slots] for b in self.buffers)
        self.got(u, "x2")
        self.got(u, "y2")
        for z in range(4):
            h[p.y, z, p.x, p.c] = h[p.y, z, p.x, p.c] + (ry2[z] if z < n else rx2[z - n])
        for j in (1, 2, 3):
            self.go(u, "z", j)

    def line(self, u):
        p, h, rz = self.p, self.held.at[u % self.slots], self.buffers[5].at[u % self.slots]
        for j in (1, 2, 3):
            self.got(u, "z", j)
        f = lambda v: v.astype(F32)
        self.out[u] = f(h[p.y, p.z, p.x, p.c]) + f(rz[0]) + f(rz[1]) + f(rz[2])
        if u + self.slots < self.total:
            for i, device in zip((0, 1, 2, 5, 4, 3), (p.to_c, p.to_x, p.to_y, *p.to_z[1:])):
                pl.semaphore_signal(self.free.at[i], inc=1, device_id=device, device_id_type=MESH)

    def finish(self):
        for u, sent in self.sends.items():
            for args in sent:
                self.copy(u, *args).wait_send()

    @staticmethod
    def scratch(n, part):
        dma = pltpu.SemaphoreType.DMA
        v = lambda *s: pltpu.VMEM((n, *s, 48, part), BF16)
        return [v(2, 4, 2, 2)], [v(2, 4, 2), v(2, 3), v(2, 2), v(2), v(3), v(3), dma((n,)), dma((n,))] + [dma((n, 2))] * 4 + [
            dma((n, 3))] * 2 + [pltpu.SemaphoreType.REGULAR((6,))]


class Total:
    def __init__(self, place, v, got, zall, sems):
        self.p, self.v, self.got, self.zall = place, v, got, zall
        self.send, self.recv = sems
        self.last = []

    def copy(self, i):
        p = self.p
        if i < 3:
            return remote(self.v.at[i], self.got.at[i], self.send.at[i], self.recv.at[i], (p.to_c, p.to_x, p.to_y)[i])
        return remote(self.v.at[3], self.zall.at[p.z], self.send.at[i], self.recv.at[i], p.to_z[i - 2])

    def step(self, i, out=None):
        if 1 <= i <= 3:
            self.copy(i - 1).wait_recv()
            self.v[i] = self.v[i - 1] + self.got[i - 1]
        if i < 3:
            self.copy(i).start()
        elif i == 3:
            for j in (3, 4, 5):
                self.copy(j).start()
            self.zall[self.p.z] = self.v[3]
        else:
            for j in (3, 4, 5):
                self.copy(j).wait_recv()
            z = self.zall
            out[...] = (z[0] + z[1]) + (z[2] + z[3])
            for j in range(6):
                self.copy(j).wait_send()

    @staticmethod
    def scratch(rows):
        dma = pltpu.SemaphoreType.DMA
        v = lambda n: pltpu.VMEM((n, rows, D), F32)
        return [v(4), v(3), v(4), dma((6,)), dma((6,))]


def attend_back(qkv, lse, gc, gqkv, sums, limits, pair):
    y, (qc, kc, vc) = head_pair(pair)
    q2, k2, v2, c2 = qkv[y, :, qc], qkv[y, :, kc], qkv[y, :, vc], gc[y, :, qc]
    bias = key_bias(limits)
    lane = lax.broadcasted_iota(jnp.int32, (S, 128), 1)
    k2t = k2.T
    gq, gk, gv = [], [], []
    for half in range(2):
        qm, km = with_mask(q2, k2, half, bias)
        st = dot(km, qm, NT)
        probs = jnp.exp(st - lse[pair * 2 + half])
        vm = jnp.where((lane // 64) == half, v2, jnp.zeros_like(v2))
        gp = dot(vm, c2, NT)
        prod = probs * gp
        total = jnp.sum(prod, axis=0, keepdims=True)
        gs = (prod - probs * total).astype(BF16)
        gv.append(dot(probs.astype(BF16), c2))
        gk.append(dot(gs, q2))
        gq.append(dot(k2t[64 * half:64 * half + 64], gs))
    pick = lambda v: jnp.where(lane < 64, v[0], v[1])
    gqt = jnp.concatenate(gq, 0).T * 0.125
    gkt = pick(gk) * 0.125
    gvt = pick(gv)
    gqkv[y, :, qc] = gqt.astype(BF16)
    gqkv[y, :, kc] = gkt.astype(BF16)
    gqkv[y, :, vc] = gvt.astype(BF16)
    sums[y, 0, :, qc] = jnp.sum(gqt, axis=0, keepdims=True)
    sums[y, 1, :, qc] = jnp.sum(gvt, axis=0, keepdims=True)


def norm_back(g, rows, gain, n, r):
    v = g[rows, :]
    normed, inverse = n[rows, :], r[rows, 0:1]
    e = v * gain
    gh = inverse * (e - jnp.mean(e, axis=-1, keepdims=True) - normed * jnp.mean(e * normed, axis=-1, keepdims=True))
    add = lambda t: jnp.sum(t, axis=0, keepdims=True)
    return gh, add(v * normed), add(v), add(gh)


BACKWARD = (
    ("SO",), ("n2", 0), ("t", 0), ("SUB", 0), ("t", 1), ("ST1", 0), ("g", 0, 0), ("SUB", 1), ("t", 2), ("g", 0, 1),
    ("ST1", 1), ("t", 3), ("SUB", 3), ("SUB", 2), ("gy", 0), ("ST2Y", 0), ("ST2X", 0), ("n1", 0), ("ST1", 2), ("to", 4),
    ("gc", 0), ("ST2Y", 1), ("a", 0, 0), ("ST3", 0), ("a", 0, 1), ("ST2X", 1), ("a", 0, 2), ("ST1", 3), ("ST2X", 2),
    ("a", 0, 3), ("a", 0, 4), ("a", 0, 5), ("ST2Y", 2), ("tv", 4), ("ST4", 0), ("ST3", 1), ("ST2X", 3), ("SUB", 4),
    ("ST2Y", 3), ("t", 5), ("ST3", 2), ("SUB", 5), ("ST1", 4), ("gx", 0), ("ST4", 1), ("ST3", 3), ("ST1", 5), ("n2", 1),
    ("ST2Y", 4), ("t", 6), ("ST2X", 4), ("ST4", 2), ("t", 7), ("SUB", 7), ("g", 1, 0), ("ST2X", 5), ("SUB", 6),
    ("ST4", 3), ("ST2Y", 5), ("ST3", 4), ("ST1", 6), ("ST1", 7), ("t", 8), ("g", 1, 1), ("ST3", 5), ("ST4", 4),
    ("t", 9), ("gy", 1), ("ST2Y", 6), ("ST2X", 6), ("n1", 1), ("ST4", 5), ("E", 0), ("SUB", 9), ("to", 10), ("ST2X", 7),
    ("E", 1), ("gc", 1), ("SUB", 8), ("ST2Y", 7), ("a", 1, 0), ("E", 2), ("ST1", 8), ("ST3", 6), ("a", 1, 1),
    ("ST1", 9), ("ST3", 7), ("a", 1, 2), ("a", 1, 3), ("a", 1, 4), ("E", 3), ("a", 1, 5), ("ST2Y", 8), ("ST2X", 8),
    ("ST4", 6), ("tv", 10), ("SUB", 10), ("ST2Y", 9), ("ST2X", 9), ("V", 0), ("t", 11), ("ST3", 8), ("V", 1),
    ("ST1", 10), ("V", 2), ("SUB", 11), ("ST3", 9), ("ST4", 7), ("E", 4), ("ST1", 11), ("ST2X", 10), ("ST2Y", 10),
    ("ST4", 8), ("V", 3), ("ST2X", 11), ("ST2Y", 11), ("ST3", 10), ("gx", 1), ("ST3", 11), ("ST4", 9), ("ST4", 10),
    ("V", 4), ("ST4", 11),
)
SPLIT = (3, 2, 2, 2, 2, 2, 2, 2, 2, 2, 2, 2)
SLOTS = 5
PART = UNITS // 2
ROWS = 24


def backward_kernel(fold, layers, w, cotf, outx, glob, lengths, bucket,
                    xr_o, qkv_o, lse_o, ctx_o, n1_o, r1_o, y1r_o, act_o, dg_o, n2_o, r2_o,
                    output, ingrad, shards, vout, vlate,
                    wv, g, gh, n, r, low, act, dg, y1r, ctx, qkv, lse, xr, gc, gqkv, sums,
                    wsem, lsem, esem, *rest):
    p = Place(fold)
    p.greet()
    m = p.y
    red = Reduce(p, 6 * layers, SLOTS, SPLIT, rest[0], shards, *rest[1:16])
    early = Total(p, *rest[16:19], rest[19:21])
    late = Total(p, *rest[21:24], rest[24:26])
    limits = bounds(lengths, bucket, m)
    order = [3 * l + t for l in reversed(range(layers)) for t in (2, 1, 0)]
    full = slice(0, UNITS)

    def row(i):
        return glob[i:i + 1, :]

    def weights(i):
        return pltpu.make_async_copy(w.at[order[i]], wv.at[i % 2], wsem.at[i % 2])

    table = {"n2": (n2_o, n), "r2": (r2_o, r), "act": (act_o, act), "dg": (dg_o, dg), "y1r": (y1r_o, y1r),
             "n1": (n1_o, n), "r1": (r1_o, r), "ctx": (ctx_o, ctx), "qkv": (qkv_o, qkv), "lse": (lse_o, lse),
             "xr": (xr_o, xr)}
    loads = {}

    def begin(l, *names):
        for i in names:
            src, dst = table[i]
            loads[i] = pltpu.make_async_copy(src.at[l], dst, lsem.at[list(table).index(i)])
            loads[i].start()

    def need(*names):
        for i in names:
            loads.pop(i).wait()

    def add(line, value):
        early.v[0, line:line + 1, :] = early.v[0, line:line + 1, :] + value

    def norm_stage(l, which):
        base = 12 * (layers - 1 - l)

        @pl.loop(0, 4)
        def _(i):
            rows = at(128 * i, 128)
            v, a, b, c = norm_back(g, rows, row(6 * l + 2 + which), n, r)
            gh[rows, :] = v
            low[rows, :] = v.astype(BF16)
            add(base + which, a)
            add(base + 2 + which, b)
            add(base + 4 + which, c)

    def tiles(u, left, right, start, width, to):
        s = red.slot(u)
        for y in range(2):
            v = dot(left[...], right[y, :, start:start + width], TN).astype(BF16)
            s[y, :, :, :, :, to:to + width] = v.reshape(4, 2, 2, 48, width)

    def norm_two(i):
        l = layers - 1 - i
        need("n2", "r2")
        norm_stage(l, 1)
        begin(l, "n1", "r1")

    def gradient(u):
        l, kind = layers - 1 - u // 6, u % 6
        if kind < 2:
            if kind == 0:
                need("act")
            tiles(u, low, act, PART * kind, PART, 0)
            if kind == 1 and l:
                begin(l - 1, "act")
        elif kind < 4:
            if kind == 2:
                need("y1r")
            tiles(u, y1r, dg, PART * (kind - 2), PART, 0)
        else:
            tiles(u, xr, gqkv, 0, 2 * HALF, 0)

    def gradient_out(u):
        need("ctx")
        tiles(u, low, ctx, 0, HALF, HALF)

    def gradient_value(u):
        need("xr")
        tiles(u, xr, gqkv, 2 * HALF, HALF, 0)

    def units(i, half):
        if half == 0:
            weights(3 * i).wait()
            need("dg")
        wc = wv.at[3 * i % 2]
        for y in range(2):
            cols = slice(PART * half, PART * half + PART)
            gi = dot(low[...], columns(wc, y, cols)) * dg[y, :, cols].astype(F32)
            dg[y, :, cols] = gi.astype(BF16)
            line = 12 * i + 6 + 2 * y + half
            early.v[0, line:line + 1, :] = jnp.sum(gi, axis=0, keepdims=True)
        if half == 1 and 3 * i + 2 < 3 * layers:
            weights(3 * i + 2).start()

    def hidden(i):
        weights(3 * i + 1).wait()
        wb = wv.at[(3 * i + 1) % 2]
        g[...] = gh[...] + dot(dg[0], columns(wb, 0, full), NT) + dot(dg[1], columns(wb, 1, full), NT)
        if 3 * i + 3 < 3 * layers:
            weights(3 * i + 3).start()
        l = layers - 1 - i
        if l:
            begin(l - 1, "dg", "y1r")

    def norm_one(i):
        l = layers - 1 - i
        need("n1", "r1")
        norm_stage(l, 0)
        if l:
            begin(l - 1, "n2", "r2")

    def context(i):
        l = layers - 1 - i
        weights(3 * i + 2).wait()
        wa = wv.at[(3 * i + 2) % 2]
        for y in range(2):
            gc[y] = dot(low[...], columns(wa, y, slice(3 * HALF, 4 * HALF))).astype(BF16)
        if l:
            begin(l - 1, "ctx")
        need("qkv", "lse")

    def attention(i, inside):
        @pl.loop(0, 6)
        def _(j):
            attend_back(qkv, lse, gc, gqkv, sums, limits, j)
            for turn, todo in enumerate(inside):
                if todo:
                    @pl.when(j == turn)
                    def _():
                        for t in todo:
                            steps[t[0]](*t[1:])
        for y in range(2):
            for t in range(2):
                where = slice(HALF * y, HALF * y + HALF)
                if i == layers - 1:
                    late.v[0, t:t + 1, where] = sums[y, t]
                else:
                    early.v[0, 12 * i + 10 + t:12 * i + 11 + t, where] = sums[y, t]

    def state(i):
        l = layers - 1 - i
        wa = wv.at[(3 * i + 2) % 2]
        wqkv = [columns(wa, y, slice(0, 3 * HALF)) for y in range(2)]
        if l:
            g[...] = gh[...] + dot(gqkv[0], wqkv[0], NT) + dot(gqkv[1], wqkv[1], NT)
            begin(l - 1, "qkv", "lse", "xr")
            weights(3 * i + 4).start()
        else:
            for j in range(2):
                rows = at((S // 2) * (1 - m if j == 0 else m), S // 2)
                v = gh[rows, :] + dot(gqkv[0, rows, :], wqkv[0], NT) + dot(gqkv[1, rows, :], wqkv[1], NT)
                low[rows, :] = v.astype(BF16)
                (swap_g if j == 0 else own_g).start()

    steps = {
        "n2": norm_two, "t": gradient, "to": gradient_out, "tv": gradient_value, "g": units, "gy": hidden, "n1": norm_one,
        "gc": context, "gx": state, "SUB": red.submit, "ST1": red.cores, "ST2X": red.after_x, "ST2Y": red.after_y,
        "ST3": red.plane, "ST4": red.line, "E": lambda i: early.step(i, vout), "V": lambda i: late.step(i, vlate),
        "SO": lambda: swap_o.start()}
    own_o = pltpu.make_async_copy(outx.at[m], output.at[m], esem.at[0])
    swap_o = remote(outx.at[1 - m], output.at[m], esem.at[1], esem.at[2], p.to_y)
    half = lambda i: low.at[at((S // 2) * i, S // 2), :]
    own_g = pltpu.make_async_copy(half(m), ingrad.at[m], esem.at[3])
    swap_g = remote(half(1 - m), ingrad.at[m], esem.at[4], esem.at[5], p.to_y)
    top = layers - 1
    cload = pltpu.make_async_copy(cotf, low, esem.at[6])
    cload.start()
    begin(top, "n2", "r2", "act")
    early.v[0] = jnp.zeros((ROWS, D), F32)
    late.v[0] = jnp.zeros((8, D), F32)
    cload.wait()
    g[...] = low[...].astype(F32)
    own_o.start()
    plan = list(BACKWARD)
    met = False
    while plan:
        t = plan.pop(0)
        if t[0] != "a":
            if t[0] in ("SO", "SUB") and not met:
                p.greeted()
                met = True
            steps[t[0]](*t[1:])
            if t == ("SUB", 0):
                begin(top, "dg")
                weights(0).start()
            elif t == ("SUB", 1):
                begin(top, "y1r")
                weights(1).start()
            elif t == ("SUB", 2):
                begin(top, "ctx", "qkv", "lse", "xr")
            continue
        inside = [[] for _ in range(6)]
        while (t[0], t[-1]) != ("a", 5):
            if t[0] == "a":
                turn = t[2]
            else:
                inside[turn].append(t)
            t = plan.pop(0)
        attention(t[1], inside)
    red.finish()
    own_o.wait()
    swap_o.wait()
    own_g.wait()
    swap_g.wait()


def backward(w, cotf, outx, glob, lengths, bucket, saved, layers, fold):
    n = 6 * layers
    dma = pltpu.SemaphoreType.DMA
    shape = jax.ShapeDtypeStruct
    vm = pltpu.VMEM
    first, rest = Reduce.scratch(SLOTS, PART)
    return pl.pallas_call(
        functools.partial(backward_kernel, fold, layers),
        out_shape=[shape((2, S // 2, D), BF16), shape((2, S // 2, D), BF16), shape((n, 48, PART), F32),
                   shape((ROWS, D), F32), shape((8, D), F32)],
        in_specs=[ANY, ANY, ANY, VMEM, SMEM, SMEM] + [ANY] * 11,
        out_specs=[ANY, ANY, VMEM, VMEM, VMEM],
        scratch_shapes=[
            vm((2, 2, 4, 2, 2, 48, UNITS), BF16), vm((S, D), F32), vm((S, D), F32), vm((S, D), F32), vm((S, 128), F32),
            vm((S, D), BF16), vm((2, S, UNITS), BF16), vm((2, S, UNITS), BF16), vm((S, D), BF16),
            vm((2, S, HALF), BF16), vm((2, S, 3 * HALF), BF16), vm((12, 1, S), F32), vm((S, D), BF16), vm((2, S, HALF), BF16),
            vm((2, S, 3 * HALF), BF16), vm((2, 2, 1, HALF), F32),
            dma((2,)), dma((11,)), dma((7,)), *first, *rest, *Total.scratch(ROWS), *Total.scratch(8)],
        compiler_params=pltpu.CompilerParams(collective_id=2, has_side_effects=True, vmem_limit_bytes=62 * 2**20),
    )(w, cotf, outx, glob, lengths, bucket, *saved)


def pack_kernel(w_qkv, w_out, w_up, w_down, bias_qv, bias_up, bias_out, ln_gain, ln_bias, packed, vec, glob):
    vec[...] = jnp.zeros_like(vec)
    glob[...] = jnp.zeros_like(glob)
    for l in range(w_qkv.shape[0]):
        for t in range(3):
            packed[3 * l, :, HALF * t:HALF * t + HALF] = w_qkv[l, t]
        packed[3 * l, :, 3 * HALF:] = w_out[l]
        packed[3 * l + 1] = w_up[l]
        packed[3 * l + 2] = w_down[l]
        qv = bias_qv[l].astype(F32)
        for t in range(2):
            vec[2 + l:3 + l, HALF * t:HALF * t + HALF] = qv[t:t + 1]
        for i, ref in enumerate((bias_out, ln_gain, ln_bias)):
            glob[6 * l + 2 * i:6 * l + 2 * i + 2, :] = ref[l].astype(F32)
    vec[0:2, :] = bias_up[...].astype(F32)


def pack(*args):
    layers = args[0].shape[0]
    shape = jax.ShapeDtypeStruct
    return pl.pallas_call(
        pack_kernel,
        out_shape=[shape((3 * layers, 48, UNITS), BF16), shape((8, UNITS), F32), shape((16, D), F32)],
        in_specs=[VMEM] * len(args), out_specs=[VMEM] * 3,
        compiler_params=pltpu.CompilerParams(vmem_limit_bytes=60 * 2**20))(*args)


def unpack_kernel(layers, shards, early, late, out_in, ingrad_in,
                  out, ingrad, qkv, qv, w_out, bias, gain, shift, up, bias_up, down):
    m = lax.axis_index("mp")
    mine = lambda a, b: jnp.where(m == 0, a, b)
    out[...] = out_in[...]
    ingrad[...] = ingrad_in[...]
    for l in range(layers):
        u = 6 * (layers - 1 - l)
        base = 2 * u
        for half in range(2):
            cols = slice(PART * half, PART * half + PART)
            down[l, :, cols] = shards[u + half]
            up[l, :, cols] = shards[u + 2 + half]
            bias_up[l:l + 1, cols] = mine(early[base + 6 + half:base + 7 + half, :], early[base + 8 + half:base + 9 + half, :])
        qkv[l, 0] = shards[u + 5, :, :HALF]
        qkv[l, 1] = shards[u + 5, :, HALF:]
        qkv[l, 2] = shards[u + 4, :, :HALF]
        w_out[l] = shards[u + 4, :, HALF:]
        gain[l] = early[base:base + 2, :]
        shift[l] = early[base + 2:base + 4, :]
        bias[l] = early[base + 4:base + 6, :]
        for t in range(2):
            line = early[base + 10 + t:base + 11 + t, :] if l else late[t:t + 1, :]
            qv[l, t:t + 1, :] = mine(line[:, :HALF], line[:, HALF:])


def unpack(layers, *args):
    shape = lambda *s: jax.ShapeDtypeStruct(s, F32)
    rows = jax.ShapeDtypeStruct((2, S // 2, D), BF16)
    return pl.pallas_call(
        functools.partial(unpack_kernel, layers),
        out_shape=[rows, rows, shape(layers, 3, 48, HALF), shape(layers, 2, HALF), shape(layers, 48, HALF), shape(layers, 2, D),
                   shape(layers, 2, D), shape(layers, 2, D), shape(layers, 48, UNITS), shape(layers, UNITS),
                   shape(layers, 48, UNITS)],
        in_specs=[VMEM] * len(args), out_specs=[VMEM] * 11,
        compiler_params=pltpu.CompilerParams(vmem_limit_bytes=60 * 2**20))(*args)


def per_device(layer_input, cotangent, lengths, bucket, w_qkv, bias_qv, w_out, bias_out, ln_gain, ln_bias, w_up, bias_up, w_down):
    layers = w_qkv.shape[0]
    fold = lax.axis_size("dp") // GROUPS
    members = [[g * fold + i for i in range(fold)] for g in range(GROUPS)]
    if fold > 1:
        join = lambda v, axis: lax.all_gather(v, "dp", axis=axis, tiled=True, axis_index_groups=members)
        w_qkv, w_out, w_up, w_down = join(w_qkv, 2), join(w_out, 2), join(w_up, 1), join(w_down, 2)
    turn = lambda v: v.transpose(0, 2, 1)
    packed, vec, glob = pack(w_qkv, turn(w_out), w_up, turn(w_down), bias_qv, bias_up, bias_out, ln_gain, ln_bias)
    w, cotf, out, *saved = forward(packed, layer_input, cotangent, vec, glob, lengths, bucket, layers, fold)
    output, ingrad, shards, early, late = backward(
        w, cotf.reshape(S, D), out.reshape(2, S // 2, D), glob, lengths, bucket, saved, layers, fold)
    output, ingrad, qkv, qv, w_out, bias, gain, shift, up, bias_up, down = unpack(layers, shards, early, late, output, ingrad)
    w_out, down = turn(w_out), turn(down)
    if fold > 1:
        part = lambda v, axis: lax.psum_scatter(v, "dp", scatter_dimension=axis, tiled=True, axis_index_groups=members)
        qkv, w_out, up, down = part(qkv, 2), part(w_out, 2), part(up, 1), part(down, 2)
        qv, bias, gain, shift, bias_up = lax.psum((qv, bias, gain, shift, bias_up), "dp", axis_index_groups=members)
    return output, ingrad, qkv, qv, w_out, bias, gain, shift, up, bias_up, down


def solution(mesh):
    in_specs = (
        P("dp", "mp", None),
        P("dp", "mp", None),
        P("dp", None),
        P("dp"),
        P(None, None, "dp", "mp"),
        P(None, None, "mp"),
        P(None, "mp", "dp"),
        P(),
        P(),
        P(),
        P(None, "dp", "mp"),
        P(None, "mp"),
        P(None, "mp", "dp"),
    )
    out_specs = (
        P("dp", "mp", None),
        P("dp", "mp", None),
        P(None, None, "dp", "mp"),
        P(None, None, "mp"),
        P(None, "mp", "dp"),
        P(),
        P(),
        P(),
        P(None, "dp", "mp"),
        P(None, "mp"),
        P(None, "mp", "dp"),
    )
    return jax.shard_map(
        per_device, mesh=mesh, in_specs=in_specs, out_specs=out_specs, check_vma=False
    )
```

```python
import functools

import jax
import jax.numpy as jnp
from jax import lax
from jax.experimental import pallas as pl
from jax.experimental.pallas import tpu as pltpu
from jax.sharding import PartitionSpec as P

F32 = jnp.float32
BF16 = jnp.bfloat16
S = 512
D = 768
HALF = 384
UNITS = 1536
GROUPS = 16
EPS = 1e-12
MESH = pl.DeviceIdType.MESH
NN = (((1,), (0,)), ((), ()))
NT = (((1,), (1,)), ((), ()))
TN = (((0,), (0,)), ((), ()))
ANY = pl.BlockSpec(memory_space=pl.ANY)
VMEM = pl.BlockSpec(memory_space=pltpu.VMEM)
SMEM = pl.BlockSpec(memory_space=pltpu.SMEM)


def dot(a, b, dims=NN):
    return lax.dot_general(a, b, dims, preferred_element_type=F32)


def at(start, size):
    return pl.ds(pl.multiple_of(start, size), size)


def remote(src, dst, send_sem, recv_sem, device):
    return pltpu.make_async_remote_copy(
        src_ref=src, dst_ref=dst, send_sem=send_sem, recv_sem=recv_sem,
        device_id=device, device_id_type=MESH)


class Place:
    def __init__(self, fold):
        d = lax.axis_index("dp")
        self.fold = fold
        self.member = lax.rem(d, fold) if fold > 1 else 0
        g = d // fold if fold > 1 else d
        self.z = g // 4
        self.xc = lax.rem(g, 4)
        self.x = self.xc // 2
        self.c = lax.rem(self.xc, 2)
        self.y = lax.axis_index("mp")
        self.xo = (1 - self.x) * 2 + self.c
        self.co = self.x * 2 + (1 - self.c)
        self.yo = 1 - self.y
        self.to_z = [None] + [self.device(lax.rem(self.z + j, 4), self.xc, self.y) for j in (1, 2, 3)]
        self.to_x = self.device(self.z, self.xo, self.y)
        self.to_y = self.device(self.z, self.xc, self.yo)
        self.to_c = self.device(self.z, self.co, self.y)

    def device(self, z, xc, y):
        return {"dp": (z * 4 + xc) * self.fold + self.member, "mp": y}

    def greet(self):
        for device in (*self.to_z[1:], self.to_x, self.to_y, self.to_c):
            pl.semaphore_signal(pltpu.get_barrier_semaphore(), inc=1, device_id=device, device_id_type=MESH)

    def greeted(self):
        pl.semaphore_wait(pltpu.get_barrier_semaphore(), 6)


class Gather:
    def __init__(self, place, packed, w, turned, via_x, lsem, zs, zr, xs, xr, ys, yr, fs, fr, cs, cr, qs, qr):
        self.p, self.packed, self.w, self.turned, self.via_x = place, packed, w, turned, via_x
        self.sems = dict(z=(zs, zr), x=(xs, xr), y=(ys, yr), f=(fs, fr), c=(cs, cr), q=(qs, qr))
        self.lsem = lsem
        z = place.z
        low = z < 2
        self.order = [z, jnp.where(low, 1 - z, 5 - z), jnp.where(low, 2, 1), jnp.where(low, 3, 0)]
        self.inner = (z == 1) | (z == 2)
        self.partner = place.device(z + 1 - 2 * lax.rem(z, 2), place.xc, place.y)
        self.across = place.device(3 - z, place.xc, place.y)
        self.sends, self.inner_sends, self.waited = [], [], set()

    def go(self, make):
        make().start()
        self.sends.append(make)

    def go_inner(self, make):
        pl.when(self.inner)(lambda: make().start())
        self.inner_sends.append(make)

    def copy(self, kind, k, i, j, src, dst, device):
        send, recv = self.sems[kind]
        return remote(src, dst, send.at[k, i], recv.at[k, j], device)

    def block(self, k, j=0, other_x=False, other_y=False):
        p = self.p
        return self.w.at[k, p.yo if other_y else p.y, self.order[j], 1 - p.x if other_x else p.x, p.c]

    def source(self, k, j):
        return self.packed.at[k] if j == 0 else self.block(k, j)

    def own(self, k):
        return pltpu.make_async_copy(self.packed.at[k], self.block(k), self.lsem.at[k])

    def load(self, k, j):
        return self.w.at[k, :, self.order[j], :, self.p.c] if k == self.turned else self.block(k, j)

    def line(self, k, i):
        j, slot, device = ((0, 1, self.partner), (0, 2, self.across), (1, 3, self.across), (2, 2, self.partner),
                           (3, 3, self.partner))[i]
        src = dst = self.load(k, j)
        if j == 0 and k != self.turned:
            src = self.packed.at[k]
        return self.copy("z", k, i, slot, src, dst, device)

    def line_start(self, k):
        self.go(lambda: self.line(k, 0))
        self.go_inner(lambda: self.line(k, 1))

    def line_wait(self, k, j):
        self.copy("z", k, 0, j, self.load(k, j), self.load(k, j), self.partner).wait_recv()
        self.go_inner(lambda: self.line(k, j + 1))

    def to_x(self, k, j):
        return self.copy("x", k, j, j, self.source(k, j), self.block(k, j), self.p.to_x)

    def to_y(self, k, j):
        return self.copy("y", k, j, j, self.source(k, j), self.block(k, j), self.p.to_y)

    def diagonal(self, k, j):
        x = self.via_x(k, j)
        block = self.block(k, j, other_x=not x, other_y=x)
        return self.copy("f", k, j, j, block, block, self.p.to_x if x else self.p.to_y)

    def to_core(self, k, i):
        p = self.p
        if k == self.turned:
            block = self.load(k, i)
        else:
            y, x = ((p.y, p.x), (p.y, 1 - p.x), (p.yo, p.x), (p.yo, 1 - p.x))[i]
            block = self.w.at[k, y, :, x, p.c]
        return self.copy("c", k, i, i, block, block, p.to_c)

    def start(self, k):
        self.own(k).start()
        self.line_start(k)
        self.go(lambda: self.to_x(k, 0))
        self.go(lambda: self.to_y(k, 0))

    def spread(self, k, j):
        self.go(lambda: self.to_x(k, j))
        self.go(lambda: self.to_y(k, j))
        if j == 3:
            self.own(k).wait()
            self.go(lambda: self.to_core(k, 0))

    def seen(self, kind, k, j):
        if (kind, k, j) not in self.waited:
            self.waited.add((kind, k, j))
            (self.to_x if kind == "x" else self.to_y)(k, j).wait_recv()

    def forward(self, k, j):
        self.seen("y" if self.via_x(k, j) else "x", k, j)
        self.go(lambda: self.diagonal(k, j))

    def side(self, k, kind):
        for j in range(4):
            self.seen(kind, k, j)
        self.go(lambda: self.to_core(k, 1 if kind == "x" else 2))

    def share(self, k):
        for j in range(4):
            self.diagonal(k, j).wait_recv()
        self.go(lambda: self.to_core(k, 3))

    def arrive(self, k):
        for i in range(4):
            self.to_core(k, i).wait_recv()

    def turned_copy(self, i):
        p, k = self.p, self.turned
        if i < 2:
            return self.copy("q", 0, i, i, self.packed.at[k], self.block(k), (p.to_x, p.to_y)[i])
        half = slice(UNITS // 2 * (i - 2), UNITS // 2 * (i - 1))
        block = self.block(k, other_x=i == 2, other_y=i == 3).at[:, half]
        return self.copy("q", 0, i, i, block, block, (p.to_y, p.to_x)[i - 2])

    def turned_start(self):
        self.own(self.turned).start()
        self.go(lambda: self.turned_copy(0))
        self.go(lambda: self.turned_copy(1))

    def turned_forward(self, i):
        self.turned_copy(i).wait_recv()
        self.go(lambda: self.turned_copy(2 + i))

    def turned_line(self, j):
        k = self.turned
        if j == 0:
            self.own(k).wait()
            self.turned_copy(2).wait_recv()
            self.turned_copy(3).wait_recv()
            self.line_start(k)
        else:
            self.line_wait(k, j)
        self.go(lambda: self.to_core(k, j))

    def finish(self):
        for make in self.sends:
            make().wait_send()
        for make in self.inner_sends:
            pl.when(self.inner)(lambda: make().wait_send())

    @staticmethod
    def scratch(n):
        dma = pltpu.SemaphoreType.DMA
        return [dma((n,)), dma((n, 5)), dma((n, 4))] + [dma((n, 4))] * 8 + [dma((1, 4))] * 2


def columns(w, y, cols):
    v = w[y, :, :, :, :, cols]
    return v.reshape(D, v.shape[-1])


def bounds(lengths, bucket, m):
    l0, l1, one = lengths[m, 0], lengths[m, 1], bucket[m] == 1
    half = S // 2
    return jnp.where(one, l0 + l1, l0), jnp.where(one, 0, half), jnp.where(one, l0 + l1, half + l1)


def key_bias(limits):
    first_end, second_start, second_end = limits
    k = lax.broadcasted_iota(jnp.int32, (S, 128), 0)
    lo = jnp.where(k < first_end, 0.0, -1e9)
    hi = jnp.where((k >= second_start) & (k < second_end), 0.0, -1e9)
    return lo, hi


def with_mask(q2, k2, half, bias):
    lane = lax.broadcasted_iota(jnp.int32, (S, 128), 1)
    low = lax.broadcasted_iota(jnp.int32, (S, 128), 0) < S // 2
    own = (lane // 64) == half
    o = 64 * (1 - half)
    one = lambda pick: jnp.where(pick, 1.0, 0.0)
    qa = jnp.where(lane == o, one(low), jnp.where(lane == o + 1, one(~low), 0.0))
    ka = jnp.where(lane == o, bias[0], jnp.where(lane == o + 1, bias[1], 0.0))
    qm = jnp.where(own, q2.astype(F32) * 0.125, qa).astype(BF16)
    km = jnp.where(own, k2.astype(F32), ka).astype(BF16)
    return qm, km


def head_pair(pair):
    y, r = pair // 3, lax.rem(pair, 3)
    return y, [at(o + 128 * r, 128) for o in (0, HALF, 2 * HALF)]


def attend(qkv, ctx, lse, limits, pair):
    y, (qc, kc, vc) = head_pair(pair)
    q2, k2, v2 = qkv[y, :, qc], qkv[y, :, kc], qkv[y, :, vc]
    bias = key_bias(limits)
    v2t = v2.T
    parts = []
    for half in range(2):
        qm, km = with_mask(q2, k2, half, bias)
        st = dot(km, qm, NT)
        top = jnp.max(st, axis=0, keepdims=True)
        e = jnp.exp(st - top)
        total = jnp.sum(e, axis=0, keepdims=True)
        lse[pair * 2 + half] = top + jnp.log(total)
        ct = dot(v2t[64 * half:64 * half + 64], e.astype(BF16))
        parts.append(ct * (1.0 / total))
    ctx[y, :, qc] = jnp.concatenate(parts, 0).T.astype(BF16)


def normalize(h, rows, gain, shift, n, r):
    v = h[rows, :]
    c = v - jnp.mean(v, axis=-1, keepdims=True)
    inverse = lax.rsqrt(jnp.mean(c * c, axis=-1, keepdims=True) + EPS)
    normed = c * inverse
    n[rows, :] = normed
    r[rows, :] = jnp.broadcast_to(inverse, (inverse.shape[0], 128))
    return normed * gain + shift


def gelu_parts(u):
    cdf = 0.5 * (1.0 + lax.erf(u * 0.7071067811865476))
    return u * cdf, cdf + u * (jnp.exp(-0.5 * u * u) * 0.3989422804014327)


PLAN = (
    ("S", 0), ("TS",), ("S", 1), ("S", 2), ("L", 0, 1), ("L", 1, 1), ("XY", 0, 1), ("L", 0, 2), ("L", 2, 1), ("S", 4),
    ("TF", 0), ("L", 0, 3), ("TF", 1), ("XY", 0, 3), ("L", 1, 2), ("F", 0, 0), ("XY", 0, 2), ("XY", 1, 1), ("F", 0, 1),
    ("L", 1, 3), ("TL", 0), ("F", 0, 3), ("F", 0, 2), ("XY", 1, 3), ("SX",), ("XY", 1, 2), ("S", 5), ("L", 4, 1),
    ("L", 2, 2), ("XY", 2, 1), ("XY", 2, 2), ("F", 4, 0), ("SH", 0), ("CX", 0), ("CY", 0), ("F", 1, 0), ("TL", 1),
    ("L", 2, 3), ("F", 1, 3), ("L", 5, 1), ("F", 1, 1), ("TL", 2), ("AR", 0), ("XY", 2, 3), ("XY", 5, 1), ("F", 1, 2),
    ("CY", 1), ("F", 2, 0), ("CX", 1), ("F", 2, 1), ("TL", 3), ("XY", 4, 1), ("CX", 2), ("AR", 3), ("F", 2, 3),
    ("L", 4, 2), ("SH", 1), ("L", 4, 3), ("F", 2, 2), ("XY", 4, 2), ("L", 5, 2), ("F", 4, 1), ("XY", 5, 2),
    ("XY", 4, 3), ("AR", 1), ("CY", 2), ("SH", 2), ("AR", 2), ("L", 5, 3), ("F", 4, 2), ("XY", 5, 3), ("F", 4, 3),
    ("F", 5, 0), ("CX", 4), ("CY", 4), ("CX", 5), ("F", 5, 2), ("F", 5, 1), ("SH", 4), ("F", 5, 3), ("AR", 4),
    ("CY", 5), ("SC",), ("SH", 5), ("AR", 5),
)
TURNED = 3
VIA_X = ((1, 1, 1, 0), (1, 0, 1, 1), (0, 1, 1, 0), (0, 1, 1, 0), (0, 1, 0, 1), (1, 0, 0, 1))


def forward_kernel(fold, layers, packed, xin, cot, vec, glob, lengths, bucket,
                   w, cotf, out, xr_o, qkv_o, lse_o, ctx_o, n1_o, r1_o, y1r_o, act_o, dg_o, n2_o, r2_o,
                   wv, xh, vecf, x, xr, qkv, lse, ctx, h, n1, r1, y1, y1r, act, dg, n2, r2,
                   wsem, esem, ssem, *gsems):
    p = Place(fold)
    m = p.y
    parts = 3 * layers
    assert parts == len(VIA_X)
    g = Gather(p, packed, w, TURNED, lambda k, j: VIA_X[k][j], *gsems)
    saves = {}
    names = ("xr", "qkv", "lse", "ctx", "n1", "r1", "y1r", "act", "dg", "n2", "r2")

    def load(k):
        return pltpu.make_async_copy(w.at[k], wv.at[k], wsem.at[k])

    def save(i, l, src, dst):
        if i in saves:
            saves.pop(i).wait()
        saves[i] = pltpu.make_async_copy(src, dst.at[l], ssem.at[names.index(i), l])
        saves[i].start()

    def before(*names):
        for i in names:
            if i in saves:
                saves.pop(i).wait()

    own_x = pltpu.make_async_copy(xin.at[m], xh.at[m], esem.at[0])
    swap_x = remote(xin.at[1 - m], xh.at[m], esem.at[1], esem.at[2], p.to_y)
    own_c = pltpu.make_async_copy(cot.at[m], cotf.at[m], esem.at[3])
    swap_c = remote(cot.at[1 - m], cotf.at[m], esem.at[4], esem.at[5], p.to_y)
    own_v = pltpu.make_async_copy(vec, vecf.at[m], esem.at[6])
    swap_v = remote(vec, vecf.at[m], esem.at[7], esem.at[8], p.to_y)
    limits = bounds(lengths, bucket, m)

    def row(i):
        return glob[i:i + 1, :]

    def stage_a(l, y):
        wa = wv.at[3 * l]
        if y == 0:
            before("xr", "qkv", "lse", "ctx", "n1", "r1", "y1r")
            save("xr", l, xr, xr_o)
        for t in range(3):
            cols = slice(HALF * t, HALF * t + HALF)
            v = dot(xr[...], columns(wa, y, cols))
            if t != 1:
                v = v + vecf[y, 2 + l:3 + l, HALF * (t // 2):HALF * (t // 2) + HALF]
            qkv[y, :, cols] = v.astype(BF16)
        if y == 1:
            save("qkv", l, qkv, qkv_o)

    def stage_out(l):
        wa = wv.at[3 * l]
        save("lse", l, lse, lse_o)
        save("ctx", l, ctx, ctx_o)
        wo = [columns(wa, y, slice(3 * HALF, 4 * HALF)) for y in range(2)]
        h[...] = x[...] + row(6 * l) + dot(ctx[0], wo[0], NT) + dot(ctx[1], wo[1], NT)

        @pl.loop(0, 2)
        def _(i):
            rows = at(256 * i, 256)
            o = normalize(h, rows, row(6 * l + 2), row(6 * l + 4), n1, r1)
            y1[rows, :] = o
            y1r[rows, :] = o.astype(BF16)
        save("n1", l, n1, n1_o)
        save("r1", l, r1, r1_o)
        save("y1r", l, y1r, y1r_o)

    def stage_b(l, y, i):
        wb = wv.at[3 * l + 1]
        if y == 0 and i == 0:
            before("act", "dg", "n2", "r2")
        cols = slice(768 * i, 768 * i + 768)
        u = dot(y1r[...], columns(wb, y, cols)) + vecf[y, l:l + 1, cols]
        a, d = gelu_parts(u)
        act[y, :, cols] = a.astype(BF16)
        dg[y, :, cols] = d.astype(BF16)
        if y == 1 and i == 1:
            save("act", l, act, act_o)
            save("dg", l, dg, dg_o)

    def stage_c(l):
        wc = wv.at[3 * l + 2]
        before("xr")
        full = slice(0, UNITS)
        h[...] = (y1[...] + row(6 * l + 1) + dot(act[0], columns(wc, 0, full), NT)
                  + dot(act[1], columns(wc, 1, full), NT))

        @pl.loop(0, 2)
        def _(i):
            rows = at(256 * i, 256)
            o = normalize(h, rows, row(6 * l + 3), row(6 * l + 5), n2, r2)
            x[rows, :] = o
            xr[rows, :] = o.astype(BF16)
        save("n2", l, n2, n2_o)
        save("r2", l, r2, r2_o)

    pending, here, used = [], set(), [0]

    def ready(k):
        l, kind = k // 3, k % 3
        pending.append(lambda: load(k).wait())
        if k == 0:
            pending.append(first)
        if kind == 0:
            pending.append(lambda: stage_a(l, 0))
            pending.append(lambda: stage_a(l, 1))
            pending.append((6, lambda j: attend(qkv, ctx, lse, limits, j)))
            pending.append(lambda: stage_out(l))
        elif kind == 1:
            for y in range(2):
                for i in range(2):
                    pending.append(lambda y=y, i=i: stage_b(l, y, i))
        else:
            pending.append(lambda: stage_c(l))

    def first():
        own_x.wait()
        swap_x.wait()
        own_v.wait()
        swap_v.wait()
        for i in range(2):
            rows = slice(256 * i, 256 * i + 256)
            xr[rows, :] = xh[i]
            x[rows, :] = xh[i].astype(F32)

    def run(steps):
        steps = list(steps)
        while steps or pending:
            piece = pending.pop(0) if pending else None
            if isinstance(piece, tuple):
                inside, steps = steps[:piece[0]], steps[piece[0]:]

                @pl.loop(0, piece[0])
                def _(j):
                    piece[1](j)
                    for i, step in enumerate(inside):
                        pl.when(j == i)(step)
            else:
                if piece is not None:
                    piece()
                if steps:
                    steps.pop(0)()

    def arrived(k):
        g.arrive(k)
        load(k).start()
        here.add(k)
        while used[0] in here:
            ready(used[0])
            used[0] += 1

    steps = {
        "S": g.start, "L": g.line_wait, "XY": g.spread, "F": g.forward, "CX": lambda k: g.side(k, "x"),
        "CY": lambda k: g.side(k, "y"), "SH": g.share, "AR": arrived, "TS": g.turned_start, "TF": g.turned_forward,
        "TL": g.turned_line, "SX": lambda: (swap_v.start(), swap_x.start()), "SC": lambda: swap_c.start()}
    plan = [lambda t=t: steps[t[0]](*t[1:]) for t in PLAN]

    p.greet()
    own_x.start()
    own_v.start()
    own_c.start()
    p.greeted()
    run(plan)
    own_c.wait()
    swap_c.wait()
    last = pltpu.make_async_copy(xr, out, esem.at[9])
    last.start()
    g.finish()
    for copy in saves.values():
        copy.wait()
    last.wait()


def forward(packed, xin, cot, vec, glob, lengths, bucket, layers, fold):
    n = 3 * layers
    dma = pltpu.SemaphoreType.DMA
    saved = [((S, D), BF16), ((2, S, 3 * HALF), BF16), ((12, 1, S), F32), ((2, S, HALF), BF16), ((S, D), F32), ((S, 128), F32),
             ((S, D), BF16), ((2, S, UNITS), BF16), ((2, S, UNITS), BF16), ((S, D), F32), ((S, 128), F32)]
    shape = jax.ShapeDtypeStruct
    vm = pltpu.VMEM
    return pl.pallas_call(
        functools.partial(forward_kernel, fold, layers),
        out_shape=[shape((n, 2, 4, 2, 2, 48, UNITS), BF16), shape((2, S // 2, D), BF16), shape((S, D), BF16)]
        + [shape((layers, *s), d) for s, d in saved],
        in_specs=[ANY, ANY, ANY, ANY, VMEM, SMEM, SMEM],
        out_specs=[ANY] * (3 + len(saved)),
        scratch_shapes=[
            vm((n, 2, 4, 2, 2, 48, UNITS), BF16), vm((2, S // 2, D), BF16), vm((2, 8, UNITS), F32), vm((S, D), F32),
            vm((S, D), BF16), vm((2, S, 3 * HALF), BF16), vm((12, 1, S), F32), vm((2, S, HALF), BF16),
            vm((S, D), F32), vm((S, D), F32), vm((S, 128), F32), vm((S, D), F32), vm((S, D), BF16),
            vm((2, S, UNITS), BF16), vm((2, S, UNITS), BF16), vm((S, D), F32), vm((S, 128), F32),
            dma((n,)), dma((10,)), dma((11, layers)), *Gather.scratch(n)],
        compiler_params=pltpu.CompilerParams(collective_id=1, has_side_effects=True, vmem_limit_bytes=60 * 2**20),
    )(packed, xin, cot, vec, glob, lengths, bucket)


class Reduce:
    def __init__(self, place, total, slots, split, held, out, rc, rx, ry, rx2, ry2, rz, cs, cr, xs, xr, ys, yr, zs, zr, free):
        self.p, self.total, self.slots, self.split = place, total, slots, split
        self.held, self.out, self.buffers = held, out, (rc, rx, ry, rx2, ry2, rz)
        self.sems = (cs, cr, xs, xr, ys, yr, zs, zr)
        self.free = free
        self.sends = {}

    def slot(self, u):
        for args in self.sends.pop(u - self.slots, ()):
            self.copy(u - self.slots, *args).wait_send()
        return self.held.at[u % self.slots]

    def go(self, u, *args):
        self.copy(u, *args).start()
        self.sends.setdefault(u, []).append(args)

    def got(self, u, *args):
        self.copy(u, *args).wait_recv()

    def copy(self, u, kind, j=0):
        p, s, n = self.p, u % self.slots, self.split[u]
        h = self.held.at[s]
        rc, rx, ry, rx2, ry2, rz = self.buffers
        cs, cr, xs, xr, ys, yr, zs, zr = self.sems
        if kind == "c":
            return remote(h.at[:, :, :, 1 - p.c], rc.at[s], cs.at[s], cr.at[s], p.to_c)
        if kind == "x1":
            return remote(h.at[:, 0:n, 1 - p.x, p.c], rx.at[s, :, 0:n], xs.at[s, 0], xr.at[s, 0], p.to_x)
        if kind == "y1":
            return remote(h.at[p.yo, n:4, :, p.c], ry.at[s, 0:4 - n], ys.at[s, 0], yr.at[s, 0], p.to_y)
        if kind == "y2":
            return remote(h.at[p.yo, 0:n, p.x, p.c], ry2.at[s, 0:n], ys.at[s, 1], yr.at[s, 1], p.to_y)
        if kind == "x2":
            return remote(h.at[p.y, n:4, 1 - p.x, p.c], rx2.at[s, 0:4 - n], xs.at[s, 1], xr.at[s, 1], p.to_x)
        to = lax.rem(p.z + j, 4)
        return remote(h.at[p.y, to, p.x, p.c], rz.at[s, j - 1], zs.at[s, j - 1], zr.at[s, j - 1], p.to_z[j])

    def submit(self, u):
        if u >= self.slots:
            for i in range(6):
                pl.semaphore_wait(self.free.at[i], 1)
        self.go(u, "c")

    def cores(self, u):
        p, h, rc = self.p, self.held.at[u % self.slots], self.buffers[0].at[u % self.slots]
        self.got(u, "c")

        @pl.loop(0, 4)
        def _(z):
            for y in range(2):
                for x in range(2):
                    h[y, z, x, p.c] = h[y, z, x, p.c] + rc[y, z, x]
        self.go(u, "x1")
        self.go(u, "y1")

    def after_x(self, u):
        p, h, rx, n = self.p, self.held.at[u % self.slots], self.buffers[1].at[u % self.slots], self.split[u]
        self.got(u, "x1")
        for y in range(2):
            for z in range(n):
                h[y, z, p.x, p.c] = h[y, z, p.x, p.c] + rx[y, z]
        self.go(u, "y2")

    def after_y(self, u):
        p, h, ry, n = self.p, self.held.at[u % self.slots], self.buffers[2].at[u % self.slots], self.split[u]
        self.got(u, "y1")
        for z in range(n, 4):
            for x in range(2):
                h[p.y, z, x, p.c] = h[p.y, z, x, p.c] + ry[z - n, x]
        self.go(u, "x2")

    def plane(self, u):
        p, h, n = self.p, self.held.at[u % self.slots], self.split[u]
        _, _, _, rx2, ry2, _ = (b.at[u % self.slots] for b in self.buffers)
        self.got(u, "x2")
        self.got(u, "y2")
        for z in range(4):
            h[p.y, z, p.x, p.c] = h[p.y, z, p.x, p.c] + (ry2[z] if z < n else rx2[z - n])
        for j in (1, 2, 3):
            self.go(u, "z", j)

    def line(self, u):
        p, h, rz = self.p, self.held.at[u % self.slots], self.buffers[5].at[u % self.slots]
        for j in (1, 2, 3):
            self.got(u, "z", j)
        f = lambda v: v.astype(F32)
        self.out[u] = f(h[p.y, p.z, p.x, p.c]) + f(rz[0]) + f(rz[1]) + f(rz[2])
        if u + self.slots < self.total:
            for i, device in zip((0, 1, 2, 5, 4, 3), (p.to_c, p.to_x, p.to_y, *p.to_z[1:])):
                pl.semaphore_signal(self.free.at[i], inc=1, device_id=device, device_id_type=MESH)

    def finish(self):
        for u, sent in self.sends.items():
            for args in sent:
                self.copy(u, *args).wait_send()

    @staticmethod
    def scratch(n, part):
        dma = pltpu.SemaphoreType.DMA
        v = lambda *s: pltpu.VMEM((n, *s, 48, part), BF16)
        return [v(2, 4, 2, 2)], [v(2, 4, 2), v(2, 3), v(2, 2), v(2), v(3), v(3), dma((n,)), dma((n,))] + [dma((n, 2))] * 4 + [
            dma((n, 3))] * 2 + [pltpu.SemaphoreType.REGULAR((6,))]


class Total:
    def __init__(self, place, v, got, zall, sems):
        self.p, self.v, self.got, self.zall = place, v, got, zall
        self.send, self.recv = sems
        self.last = []

    def copy(self, i):
        p = self.p
        if i < 3:
            return remote(self.v.at[i], self.got.at[i], self.send.at[i], self.recv.at[i], (p.to_c, p.to_x, p.to_y)[i])
        return remote(self.v.at[3], self.zall.at[p.z], self.send.at[i], self.recv.at[i], p.to_z[i - 2])

    def step(self, i, out=None):
        if 1 <= i <= 3:
            self.copy(i - 1).wait_recv()
            self.v[i] = self.v[i - 1] + self.got[i - 1]
        if i < 3:
            self.copy(i).start()
        elif i == 3:
            for j in (3, 4, 5):
                self.copy(j).start()
            self.zall[self.p.z] = self.v[3]
        else:
            for j in (3, 4, 5):
                self.copy(j).wait_recv()
            z = self.zall
            out[...] = (z[0] + z[1]) + (z[2] + z[3])
            for j in range(6):
                self.copy(j).wait_send()

    @staticmethod
    def scratch(rows):
        dma = pltpu.SemaphoreType.DMA
        v = lambda n: pltpu.VMEM((n, rows, D), F32)
        return [v(4), v(3), v(4), dma((6,)), dma((6,))]


def attend_back(qkv, lse, gc, gqkv, sums, limits, pair):
    y, (qc, kc, vc) = head_pair(pair)
    q2, k2, v2, c2 = qkv[y, :, qc], qkv[y, :, kc], qkv[y, :, vc], gc[y, :, qc]
    bias = key_bias(limits)
    lane = lax.broadcasted_iota(jnp.int32, (S, 128), 1)
    k2t = k2.T
    both = range(2)
    masked = [with_mask(q2, k2, h, bias) for h in both]
    st = [dot(km, qm, NT) for qm, km in masked]
    gp = [dot(jnp.where((lane // 64) == h, v2, jnp.zeros_like(v2)), c2, NT) for h in both]
    probs = [jnp.exp(st[h] - lse[pair * 2 + h]) for h in both]
    gv = [dot(probs[h].astype(BF16), c2) for h in both]
    prod = [probs[h] * gp[h] for h in both]
    total = [jnp.sum(prod[h], axis=0, keepdims=True) for h in both]
    gs = [(prod[h] - probs[h] * total[h]).astype(BF16) for h in both]
    gk = [dot(gs[h], q2) for h in both]
    gq = [dot(k2t[64 * h:64 * h + 64], gs[h]) for h in both]
    pick = lambda v: jnp.where(lane < 64, v[0], v[1])
    gqt = jnp.concatenate(gq, 0).T * 0.125
    gkt = pick(gk) * 0.125
    gvt = pick(gv)
    gqkv[y, :, qc] = gqt.astype(BF16)
    gqkv[y, :, kc] = gkt.astype(BF16)
    gqkv[y, :, vc] = gvt.astype(BF16)
    sums[y, 0, :, qc] = jnp.sum(gqt, axis=0, keepdims=True)
    sums[y, 1, :, qc] = jnp.sum(gvt, axis=0, keepdims=True)


def norm_back(g, rows, gain, n, r):
    v = g[rows, :]
    normed, inverse = n[rows, :], r[rows, 0:1]
    e = v * gain
    gh = inverse * (e - jnp.mean(e, axis=-1, keepdims=True) - normed * jnp.mean(e * normed, axis=-1, keepdims=True))
    add = lambda t: jnp.sum(t, axis=0, keepdims=True)
    return gh, add(v * normed), add(v), add(gh)


BACKWARD = (
    ("SO",), ("n2", 0), ("t", 0), ("SUB", 0), ("t", 1), ("ST1", 0), ("g", 0, 0), ("SUB", 1), ("t", 2), ("g", 0, 1),
    ("ST1", 1), ("t", 3), ("SUB", 3), ("SUB", 2), ("gy", 0), ("ST2Y", 0), ("ST2X", 0), ("n1", 0), ("ST1", 2), ("to", 4),
    ("gc", 0), ("ST2Y", 1), ("a", 0, 0), ("ST3", 0), ("a", 0, 1), ("ST2X", 1), ("a", 0, 2), ("ST1", 3), ("ST2X", 2),
    ("a", 0, 3), ("a", 0, 4), ("a", 0, 5), ("ST2Y", 2), ("tv", 4), ("ST4", 0), ("ST3", 1), ("ST2X", 3), ("SUB", 4),
    ("ST2Y", 3), ("t", 5), ("ST3", 2), ("SUB", 5), ("ST1", 4), ("gx", 0), ("ST4", 1), ("ST3", 3), ("ST1", 5), ("n2", 1),
    ("ST2Y", 4), ("t", 6), ("ST2X", 4), ("ST4", 2), ("t", 7), ("SUB", 7), ("g", 1, 0), ("ST2X", 5), ("SUB", 6),
    ("ST4", 3), ("ST2Y", 5), ("ST3", 4), ("ST1", 6), ("ST1", 7), ("t", 8), ("g", 1, 1), ("ST3", 5), ("ST4", 4),
    ("t", 9), ("gy", 1), ("ST2Y", 6), ("ST2X", 6), ("n1", 1), ("ST4", 5), ("E", 0), ("SUB", 9), ("to", 10), ("ST2X", 7),
    ("E", 1), ("gc", 1), ("SUB", 8), ("ST2Y", 7), ("a", 1, 0), ("E", 2), ("ST1", 8), ("ST3", 6), ("a", 1, 1),
    ("ST1", 9), ("ST3", 7), ("a", 1, 2), ("a", 1, 3), ("a", 1, 4), ("E", 3), ("a", 1, 5), ("ST2Y", 8), ("ST2X", 8),
    ("ST4", 6), ("tv", 10), ("SUB", 10), ("ST2Y", 9), ("ST2X", 9), ("V", 0), ("t", 11), ("ST3", 8), ("V", 1),
    ("ST1", 10), ("V", 2), ("SUB", 11), ("ST3", 9), ("ST4", 7), ("E", 4), ("ST1", 11), ("ST2X", 10), ("ST2Y", 10),
    ("ST4", 8), ("V", 3), ("ST2X", 11), ("ST2Y", 11), ("ST3", 10), ("gx", 1), ("ST3", 11), ("ST4", 9), ("ST4", 10),
    ("V", 4), ("ST4", 11),
)
SPLIT = (3, 2, 2, 2, 2, 2, 2, 2, 2, 2, 2, 2)
SLOTS = 5
PART = UNITS // 2
ROWS = 24


def backward_kernel(fold, layers, w, cotf, outx, glob, lengths, bucket,
                    xr_o, qkv_o, lse_o, ctx_o, n1_o, r1_o, y1r_o, act_o, dg_o, n2_o, r2_o,
                    output, ingrad, shards, vout, vlate,
                    wv, g, gh, n, r, low, act, dg, y1r, ctx, qkv, lse, xr, gc, sums,
                    wsem, lsem, esem, *rest):
    p = Place(fold)
    p.greet()
    m = p.y
    red = Reduce(p, 6 * layers, SLOTS, SPLIT, rest[0], shards, *rest[1:16])
    early = Total(p, *rest[16:19], rest[19:21])
    late = Total(p, *rest[21:24], rest[24:26])
    limits = bounds(lengths, bucket, m)
    gqkv = qkv
    order = [3 * l + t for l in reversed(range(layers)) for t in (2, 1, 0)]
    full = slice(0, UNITS)

    def row(i):
        return glob[i:i + 1, :]

    def weights(i):
        return pltpu.make_async_copy(w.at[order[i]], wv.at[i % 2], wsem.at[i % 2])

    table = {"n2": (n2_o, n), "r2": (r2_o, r), "act": (act_o, act), "dg": (dg_o, dg), "y1r": (y1r_o, y1r),
             "n1": (n1_o, n), "r1": (r1_o, r), "ctx": (ctx_o, ctx), "qkv": (qkv_o, qkv), "lse": (lse_o, lse),
             "xr": (xr_o, xr)}
    loads = {}

    def begin(l, *names):
        for i in names:
            src, dst = table[i]
            loads[i] = pltpu.make_async_copy(src.at[l], dst, lsem.at[list(table).index(i)])
            loads[i].start()

    def need(*names):
        for i in names:
            loads.pop(i).wait()

    def add(line, value):
        early.v[0, line:line + 1, :] = early.v[0, line:line + 1, :] + value

    def norm_stage(l, which):
        base = 12 * (layers - 1 - l)

        @pl.loop(0, 4)
        def _(i):
            rows = at(128 * i, 128)
            v, a, b, c = norm_back(g, rows, row(6 * l + 2 + which), n, r)
            gh[rows, :] = v
            low[rows, :] = v.astype(BF16)
            add(base + which, a)
            add(base + 2 + which, b)
            add(base + 4 + which, c)

    def tiles(u, left, right, start, width, to):
        s = red.slot(u)
        for y in range(2):
            v = dot(left[...], right[y, :, start:start + width], TN).astype(BF16)
            s[y, :, :, :, :, to:to + width] = v.reshape(4, 2, 2, 48, width)

    def norm_two(i):
        l = layers - 1 - i
        need("n2", "r2")
        norm_stage(l, 1)
        begin(l, "n1", "r1")

    def gradient(u):
        l, kind = layers - 1 - u // 6, u % 6
        if kind < 2:
            if kind == 0:
                need("act")
            tiles(u, low, act, PART * kind, PART, 0)
            if kind == 1 and l:
                begin(l - 1, "act")
        elif kind < 4:
            if kind == 2:
                need("y1r")
            tiles(u, y1r, dg, PART * (kind - 2), PART, 0)
        else:
            tiles(u, xr, gqkv, 0, 2 * HALF, 0)

    def gradient_out(u):
        need("ctx")
        tiles(u, low, ctx, 0, HALF, HALF)

    def gradient_value(u):
        need("xr")
        tiles(u, xr, gqkv, 2 * HALF, HALF, 0)

    def units(i, half):
        if half == 0:
            weights(3 * i).wait()
            need("dg")
        wc = wv.at[3 * i % 2]
        for y in range(2):
            cols = slice(PART * half, PART * half + PART)
            gi = dot(low[...], columns(wc, y, cols)) * dg[y, :, cols].astype(F32)
            dg[y, :, cols] = gi.astype(BF16)
            line = 12 * i + 6 + 2 * y + half
            early.v[0, line:line + 1, :] = jnp.sum(gi, axis=0, keepdims=True)
        if half == 1 and 3 * i + 2 < 3 * layers:
            weights(3 * i + 2).start()

    def hidden(i):
        weights(3 * i + 1).wait()
        wb = wv.at[(3 * i + 1) % 2]
        g[...] = gh[...] + dot(dg[0], columns(wb, 0, full), NT) + dot(dg[1], columns(wb, 1, full), NT)
        if 3 * i + 3 < 3 * layers:
            weights(3 * i + 3).start()
        l = layers - 1 - i
        if l:
            begin(l - 1, "dg", "y1r")

    def norm_one(i):
        l = layers - 1 - i
        need("n1", "r1")
        norm_stage(l, 0)
        if l:
            begin(l - 1, "n2", "r2")

    def context(i):
        l = layers - 1 - i
        weights(3 * i + 2).wait()
        wa = wv.at[(3 * i + 2) % 2]
        for y in range(2):
            gc[y] = dot(low[...], columns(wa, y, slice(3 * HALF, 4 * HALF))).astype(BF16)
        if l:
            begin(l - 1, "ctx")
        need("qkv", "lse")

    def attention(i, inside):
        @pl.loop(0, 6)
        def _(j):
            attend_back(qkv, lse, gc, gqkv, sums, limits, j)
            for turn, todo in enumerate(inside):
                if todo:
                    @pl.when(j == turn)
                    def _():
                        for t in todo:
                            steps[t[0]](*t[1:])
        for y in range(2):
            for t in range(2):
                where = slice(HALF * y, HALF * y + HALF)
                if i == layers - 1:
                    late.v[0, t:t + 1, where] = sums[y, t]
                else:
                    early.v[0, 12 * i + 10 + t:12 * i + 11 + t, where] = sums[y, t]

    def state(i):
        l = layers - 1 - i
        wa = wv.at[(3 * i + 2) % 2]
        wqkv = [columns(wa, y, slice(0, 3 * HALF)) for y in range(2)]
        if l:
            g[...] = gh[...] + dot(gqkv[0], wqkv[0], NT) + dot(gqkv[1], wqkv[1], NT)
            begin(l - 1, "qkv", "lse", "xr")
            weights(3 * i + 4).start()
        else:
            for j in range(2):
                rows = at((S // 2) * (1 - m if j == 0 else m), S // 2)
                v = gh[rows, :] + dot(gqkv[0, rows, :], wqkv[0], NT) + dot(gqkv[1, rows, :], wqkv[1], NT)
                low[rows, :] = v.astype(BF16)
                (swap_g if j == 0 else own_g).start()

    steps = {
        "n2": norm_two, "t": gradient, "to": gradient_out, "tv": gradient_value, "g": units, "gy": hidden, "n1": norm_one,
        "gc": context, "gx": state, "SUB": red.submit, "ST1": red.cores, "ST2X": red.after_x, "ST2Y": red.after_y,
        "ST3": red.plane, "ST4": red.line, "E": lambda i: early.step(i, vout), "V": lambda i: late.step(i, vlate),
        "SO": lambda: swap_o.start()}
    own_o = pltpu.make_async_copy(outx.at[m], output.at[m], esem.at[0])
    swap_o = remote(outx.at[1 - m], output.at[m], esem.at[1], esem.at[2], p.to_y)
    half = lambda i: low.at[at((S // 2) * i, S // 2), :]
    own_g = pltpu.make_async_copy(half(m), ingrad.at[m], esem.at[3])
    swap_g = remote(half(1 - m), ingrad.at[m], esem.at[4], esem.at[5], p.to_y)
    top = layers - 1
    cload = pltpu.make_async_copy(cotf, low, esem.at[6])
    cload.start()
    begin(top, "n2", "r2", "act")
    early.v[0] = jnp.zeros((ROWS, D), F32)
    late.v[0] = jnp.zeros((8, D), F32)
    cload.wait()
    g[...] = low[...].astype(F32)
    own_o.start()
    plan = list(BACKWARD)
    met = False
    while plan:
        t = plan.pop(0)
        if t[0] != "a":
            if t[0] in ("SO", "SUB") and not met:
                p.greeted()
                met = True
            steps[t[0]](*t[1:])
            if t == ("SUB", 0):
                begin(top, "dg")
                weights(0).start()
            elif t == ("SUB", 1):
                begin(top, "y1r")
                weights(1).start()
            elif t == ("SUB", 2):
                begin(top, "ctx", "qkv", "lse", "xr")
            continue
        inside = [[] for _ in range(6)]
        while (t[0], t[-1]) != ("a", 5):
            if t[0] == "a":
                turn = t[2]
            else:
                inside[turn].append(t)
            t = plan.pop(0)
        attention(t[1], inside)
    red.finish()
    own_o.wait()
    swap_o.wait()
    own_g.wait()
    swap_g.wait()


def backward(w, cotf, outx, glob, lengths, bucket, saved, layers, fold):
    n = 6 * layers
    dma = pltpu.SemaphoreType.DMA
    shape = jax.ShapeDtypeStruct
    vm = pltpu.VMEM
    first, rest = Reduce.scratch(SLOTS, PART)
    return pl.pallas_call(
        functools.partial(backward_kernel, fold, layers),
        out_shape=[shape((2, S // 2, D), BF16), shape((2, S // 2, D), BF16), shape((n, 48, PART), F32),
                   shape((ROWS, D), F32), shape((8, D), F32)],
        in_specs=[ANY, ANY, ANY, VMEM, SMEM, SMEM] + [ANY] * 11,
        out_specs=[ANY, ANY, VMEM, VMEM, VMEM],
        scratch_shapes=[
            vm((2, 2, 4, 2, 2, 48, UNITS), BF16), vm((S, D), F32), vm((S, D), F32), vm((S, D), F32), vm((S, 128), F32),
            vm((S, D), BF16), vm((2, S, UNITS), BF16), vm((2, S, UNITS), BF16), vm((S, D), BF16),
            vm((2, S, HALF), BF16), vm((2, S, 3 * HALF), BF16), vm((12, 1, S), F32), vm((S, D), BF16), vm((2, S, HALF), BF16),
            vm((2, 2, 1, HALF), F32),
            dma((2,)), dma((11,)), dma((7,)), *first, *rest, *Total.scratch(ROWS), *Total.scratch(8)],
        compiler_params=pltpu.CompilerParams(collective_id=2, has_side_effects=True, vmem_limit_bytes=62 * 2**20),
    )(w, cotf, outx, glob, lengths, bucket, *saved)


def pack_kernel(w_qkv, w_out, w_up, w_down, bias_qv, bias_up, bias_out, ln_gain, ln_bias, packed, vec, glob):
    vec[...] = jnp.zeros_like(vec)
    glob[...] = jnp.zeros_like(glob)
    for l in range(w_qkv.shape[0]):
        for t in range(3):
            packed[3 * l, :, HALF * t:HALF * t + HALF] = w_qkv[l, t]
        packed[3 * l, :, 3 * HALF:] = w_out[l]
        packed[3 * l + 1] = w_up[l]
        packed[3 * l + 2] = w_down[l]
        qv = bias_qv[l].astype(F32)
        for t in range(2):
            vec[2 + l:3 + l, HALF * t:HALF * t + HALF] = qv[t:t + 1]
        for i, ref in enumerate((bias_out, ln_gain, ln_bias)):
            glob[6 * l + 2 * i:6 * l + 2 * i + 2, :] = ref[l].astype(F32)
    vec[0:2, :] = bias_up[...].astype(F32)


def pack(*args):
    layers = args[0].shape[0]
    shape = jax.ShapeDtypeStruct
    return pl.pallas_call(
        pack_kernel,
        out_shape=[shape((3 * layers, 48, UNITS), BF16), shape((8, UNITS), F32), shape((16, D), F32)],
        in_specs=[VMEM] * len(args), out_specs=[VMEM] * 3,
        compiler_params=pltpu.CompilerParams(vmem_limit_bytes=60 * 2**20))(*args)


def unpack_kernel(layers, shards, early, late, out_in, ingrad_in,
                  out, ingrad, qkv, qv, w_out, bias, gain, shift, up, bias_up, down):
    m = lax.axis_index("mp")
    mine = lambda a, b: jnp.where(m == 0, a, b)
    out[...] = out_in[...]
    ingrad[...] = ingrad_in[...]
    for l in range(layers):
        u = 6 * (layers - 1 - l)
        base = 2 * u
        for half in range(2):
            cols = slice(PART * half, PART * half + PART)
            down[l, :, cols] = shards[u + half]
            up[l, :, cols] = shards[u + 2 + half]
            bias_up[l:l + 1, cols] = mine(early[base + 6 + half:base + 7 + half, :], early[base + 8 + half:base + 9 + half, :])
        qkv[l, 0] = shards[u + 5, :, :HALF]
        qkv[l, 1] = shards[u + 5, :, HALF:]
        qkv[l, 2] = shards[u + 4, :, :HALF]
        w_out[l] = shards[u + 4, :, HALF:]
        gain[l] = early[base:base + 2, :]
        shift[l] = early[base + 2:base + 4, :]
        bias[l] = early[base + 4:base + 6, :]
        for t in range(2):
            line = early[base + 10 + t:base + 11 + t, :] if l else late[t:t + 1, :]
            qv[l, t:t + 1, :] = mine(line[:, :HALF], line[:, HALF:])


def unpack(layers, *args):
    shape = lambda *s: jax.ShapeDtypeStruct(s, F32)
    rows = jax.ShapeDtypeStruct((2, S // 2, D), BF16)
    return pl.pallas_call(
        functools.partial(unpack_kernel, layers),
        out_shape=[rows, rows, shape(layers, 3, 48, HALF), shape(layers, 2, HALF), shape(layers, 48, HALF), shape(layers, 2, D),
                   shape(layers, 2, D), shape(layers, 2, D), shape(layers, 48, UNITS), shape(layers, UNITS),
                   shape(layers, 48, UNITS)],
        in_specs=[VMEM] * len(args), out_specs=[VMEM] * 11,
        compiler_params=pltpu.CompilerParams(vmem_limit_bytes=60 * 2**20))(*args)


def per_device(layer_input, cotangent, lengths, bucket, w_qkv, bias_qv, w_out, bias_out, ln_gain, ln_bias, w_up, bias_up, w_down):
    layers = w_qkv.shape[0]
    fold = lax.axis_size("dp") // GROUPS
    members = [[g * fold + i for i in range(fold)] for g in range(GROUPS)]
    if fold > 1:
        join = lambda v, axis: lax.all_gather(v, "dp", axis=axis, tiled=True, axis_index_groups=members)
        w_qkv, w_out, w_up, w_down = join(w_qkv, 2), join(w_out, 2), join(w_up, 1), join(w_down, 2)
    turn = lambda v: v.transpose(0, 2, 1)
    packed, vec, glob = pack(w_qkv, turn(w_out), w_up, turn(w_down), bias_qv, bias_up, bias_out, ln_gain, ln_bias)
    w, cotf, out, *saved = forward(packed, layer_input, cotangent, vec, glob, lengths, bucket, layers, fold)
    output, ingrad, shards, early, late = backward(
        w, cotf.reshape(S, D), out.reshape(2, S // 2, D), glob, lengths, bucket, saved, layers, fold)
    output, ingrad, qkv, qv, w_out, bias, gain, shift, up, bias_up, down = unpack(layers, shards, early, late, output, ingrad)
    w_out, down = turn(w_out), turn(down)
    if fold > 1:
        part = lambda v, axis: lax.psum_scatter(v, "dp", scatter_dimension=axis, tiled=True, axis_index_groups=members)
        qkv, w_out, up, down = part(qkv, 2), part(w_out, 2), part(up, 1), part(down, 2)
        qv, bias, gain, shift, bias_up = lax.psum((qv, bias, gain, shift, bias_up), "dp", axis_index_groups=members)
    return output, ingrad, qkv, qv, w_out, bias, gain, shift, up, bias_up, down


def solution(mesh):
    in_specs = (
        P("dp", "mp", None),
        P("dp", "mp", None),
        P("dp", None),
        P("dp"),
        P(None, None, "dp", "mp"),
        P(None, None, "mp"),
        P(None, "mp", "dp"),
        P(),
        P(),
        P(),
        P(None, "dp", "mp"),
        P(None, "mp"),
        P(None, "mp", "dp"),
    )
    out_specs = (
        P("dp", "mp", None),
        P("dp", "mp", None),
        P(None, None, "dp", "mp"),
        P(None, None, "mp"),
        P(None, "mp", "dp"),
        P(),
        P(),
        P(),
        P(None, "dp", "mp"),
        P(None, "mp"),
        P(None, "mp", "dp"),
    )
    return jax.shard_map(
        per_device, mesh=mesh, in_specs=in_specs, out_specs=out_specs, check_vma=False
    )
```
